128 devices in a mesh: domain: 32 (over y, x, z_lo), inner: 4 (over z_hi, core).
Axes of the slice: x: 4, y: 4, z: 4 (z_hi: 2, z_lo: 2; z = z_hi * 2 + z_lo), core: 2. Of those that a mesh axis runs over, the one named last changes fastest.
Arguments:
- atom_cells: int32 [32, 4, 3, 512], P('domain', 'inner'), may hold values from 0 to 141, as said below
- atom_frac: float32 [32, 4, 3, 512], P('domain', 'inner'), may hold values from 0 to 1
- species: int32 [32, 4, 512], P('domain', 'inner'), may hold values from 0 to 7
- nbr_index: int32 [32, 4, 512, 32], P('domain', 'inner'), may hold values from 504 to 4103, as said below
- nbr_count: int32 [32, 4, 512], P('domain', 'inner'), may hold values from 4 to 32
- embed: bfloat16 [8, 128], replicated, may hold values from -6 to 6
- radial_in: bfloat16 [1, 8, 64], replicated, may hold values from -2 to 2
- radial_out: bfloat16 [1, 64, 384], replicated, may hold values from -0.75 to 0.75
- mix_weight: bfloat16 [1, 3, 128, 128], replicated, may hold values from -0.5 to 0.5
- product_weight: bfloat16 [1, 384, 128], replicated, may hold values from -0.3125 to 0.3125
- read_weight: bfloat16 [1, 128], replicated, may hold values from -0.5 to 0.5
- charge_weight: bfloat16 [128], replicated, may hold values from -0.5 to 0.5
Outputs:
- atom_energy: float32 [32, 4, 512], P('domain', 'inner')
- atom_potential: float32 [32, 4, 512], P('domain', 'inner')
The draws below stay inside these ranges and needn't reach their ends.
Inputs may be any that keep to these rules, and one draw needn't show every extreme that they name: Within a block, atoms sit on a lattice of 4 x 16 x 8 sites 4 cells apart; component 0 of atom_cells is at most 13, component 1 at most 61, component 2 lies in 112 to 141. Two different atoms are at least 2 cells apart. `nbr_index`: each slot names an atom other than the atom itself, on a lattice site at most 2 sites away; live slots come first.
All inputs are finite; a program needn't handle non-finite values.
Results may differ from the reference program's by a relative error of at most 0.0059.
The reference program's roundings to bfloat16 on the way count: a program that leaves them out, or rounds other values in their place, can miss the bound.
Values may be sent and summed in bfloat16 or wider, within the bound.
A program may use at most 192 MiB of HBM per device.

```python
import math
import jax
import jax.numpy as jnp
import numpy as np
from jax import lax

C = 128
NB = 8
RH = 64
S = 8
K = 32
LAYERS = 1
LX = 4
LY = 16
LZ = 8
MZ = 256
ATOM_DEV = 512
N_DOMAIN = 32
N_INNER = 4


def offset_table():
    moves_list = [(step_x, step_y, step_z) for step_x in (-1, 0, 1) for step_y in (-1, 0, 1) for step_z in (-1, 0, 1) if (step_x, step_y, step_z) != (0, 0, 0)]
    moves_list = moves_list + [(2, 0, 0), (-2, 0, 0), (0, 2, 0), (0, -2, 0), (0, 0, 2), (0, 0, -2)]
    return jnp.array(np.array(moves_list, dtype=np.int32))


def lattice_sites():
    serial = jnp.arange(LX * LY * LZ, dtype=jnp.int32)
    return (serial // (LY * LZ), serial // LZ % LY, serial % LZ)


def draw_nbr_index(key, part):
    key = jax.random.fold_in(key, 11)
    site_x, site_y, site_z = lattice_sites()
    table_moves = offset_table()
    target_z = site_z[:, None] + table_moves[None, :, 2]
    inside = (target_z >= 0) & (target_z < LZ)
    target_z = jnp.where(inside, target_z, site_z[:, None] - table_moves[None, :, 2])
    target_x = site_x[:, None] + table_moves[None, :, 0]
    target_y = site_y[:, None] + table_moves[None, :, 1]
    block_x = jnp.floor_divide(target_x, LX) + 1
    block_y = jnp.floor_divide(target_y, LY) + 1
    local_x = target_x - (block_x - 1) * LX
    local_y = target_y - (block_y - 1) * LY
    naming = (block_x * 3 + block_y) * (LX * LY * LZ) + (local_x * LY + local_y) * LZ + target_z
    array_shape = (N_DOMAIN, N_INNER, LX * LY * LZ, K)
    scores = jax.random.randint(key, array_shape, 0, 1 << 19) * K + jnp.arange(K, dtype=jnp.int32) + jnp.where(inside, 0, 1 << 26)
    ordering = jnp.argsort(scores, axis=-1)
    return jnp.take_along_axis(jnp.broadcast_to(naming, array_shape), ordering, axis=-1)


def draw_nbr_count(key, part):
    key = jax.random.fold_in(key, 12)
    key_low, key_rest = jax.random.split(key)
    site_x, site_y, site_z = lattice_sites()
    table_moves = offset_table()
    target_z = site_z[:, None] + table_moves[None, :, 2]
    usable = jnp.sum(((target_z >= 0) & (target_z < LZ)).astype(jnp.int32), axis=1)
    atom_total = LX * LY * LZ
    lowest = jax.random.randint(key_low, (N_DOMAIN, N_INNER, 1), 4, 17)
    random_part = jax.random.randint(key_rest, (N_DOMAIN, N_INNER, atom_total), 0, 1 << 20)
    drawn = lowest + random_part % (K + 1 - lowest)
    serial = jnp.arange(atom_total, dtype=jnp.int32)
    drawn = jnp.where(serial == LZ // 2, K, jnp.where(serial == 1, 4, drawn))
    return jnp.minimum(drawn, usable)


def draw_atom_cells(key, part):
    key = jax.random.fold_in(key, 13)
    site_x, site_y, site_z = lattice_sites()
    atom_total = LX * LY * LZ
    base_cells = jnp.stack([4 * site_x, 4 * site_y, MZ // 2 - 2 * LZ + 4 * site_z])
    jitter = jax.random.randint(key, (N_DOMAIN, N_INNER, 3, atom_total), 0, 2)
    serial = jnp.arange(atom_total, dtype=jnp.int32)
    jitter = jnp.where(serial == 0, 0, jnp.where(serial == atom_total - 1, 1, jitter))
    return base_cells + jitter


def touch_ends(entries, rng, smallest, top_value):
    spot = [jax.random.randint(jax.random.fold_in(rng, axis), (), 0, length) for axis, length in enumerate(entries.shape)]
    main_axis = entries.shape.index(max(entries.shape))
    next_to = spot[:main_axis] + [(spot[main_axis] + 1) % entries.shape[main_axis]] + spot[main_axis + 1:]
    return entries.at[tuple(spot)].set(smallest).at[tuple(next_to)].set(top_value)


def steps_of(key, extent, pieces, smallest, top_value):
    gain = 1.0
    for position, blocks in pieces:
        steps = jax.random.uniform(jax.random.fold_in(jax.random.fold_in(key, 6), position), (blocks,), jnp.float32, smallest / len(pieces), top_value / len(pieces))
        gain = gain * jnp.repeat(jnp.exp(steps), extent[position] // blocks).reshape((-1,) + (1,) * (len(extent) - 1 - position))
    return gain


def gaussian(key, extent, width, most, held_as=jnp.bfloat16):
    values = jax.random.normal(key, extent, jnp.float32) * width
    return jnp.minimum(jnp.maximum(values, -most), most).astype(held_as)


def setup_inputs(seed: int = 0) -> dict:
    keys = jax.random.split(jax.random.key(seed), 13)
    atom_cells = draw_atom_cells(jax.random.fold_in(keys[12], 71), 0)
    atom_frac = jnp.clip(1.0 * jax.random.uniform(keys[1], (N_DOMAIN, N_INNER, 3, ATOM_DEV), jnp.float32) ** steps_of(keys[1], (N_DOMAIN, N_INNER, 3, ATOM_DEV), ((0, 32), (1, 4)), -0.2, 0.2), 0.0, 1.0)
    species = touch_ends(jax.random.randint(keys[2], (N_DOMAIN, N_INNER, ATOM_DEV), 0, S), jax.random.fold_in(keys[2], 1), 0, S - 1).astype(jnp.int32)
    nbr_index = draw_nbr_index(jax.random.fold_in(keys[12], 71), 0)
    nbr_count = draw_nbr_count(jax.random.fold_in(keys[12], 71), 0)
    embed = gaussian(keys[5], (S, C), 1.0, 6.0)
    radial_in = gaussian(keys[6], (LAYERS, NB, RH), NB ** -0.5, 2.0)
    radial_out = gaussian(keys[7], (LAYERS, RH, 3 * C), RH ** -0.5, 0.75)
    mix_weight = gaussian(keys[8], (LAYERS, 3, C, C), C ** -0.5, 0.5)
    product_weight = gaussian(keys[9], (LAYERS, 3 * C, C), (3 * C) ** -0.5, 0.3125)
    read_weight = gaussian(keys[10], (LAYERS, C), C ** -0.5, 0.5)
    charge_weight = gaussian(keys[11], (C,), C ** -0.5, 0.5)
    return dict(atom_cells=atom_cells, atom_frac=atom_frac, species=species, nbr_index=nbr_index, nbr_count=nbr_count, embed=embed, radial_in=radial_in, radial_out=radial_out, mix_weight=mix_weight, product_weight=product_weight, read_weight=read_weight, charge_weight=charge_weight)


spacing = 0.55
cutoff = 5.0
smearing = 0.2
coulomb = 14.399645
neighbour_scale = 0.25

def surround(values):
    blocks = []
    for shift_x in range(3):
        row_blocks = []
        for shift_y in range(3):
            row_blocks.append(jnp.roll(values, (1 - shift_x, 1 - shift_y), axis=(0, 1)))
        blocks.append(jnp.stack(row_blocks, axis=2))
    return jnp.stack(blocks, axis=2)

def place_blocks(geo_ext, planes_x, planes_y):
    atom_count = geo_ext.shape[-1]
    steps_off = jnp.arange(3, dtype=jnp.float32) - 1.0
    off_x = jnp.broadcast_to(steps_off[:, None] * planes_x, (3, 3))
    off_y = jnp.broadcast_to(steps_off[None, :] * planes_y, (3, 3))
    offsets = jnp.stack([off_x, off_y, jnp.zeros((3, 3), jnp.float32)], axis=2)[..., None]
    placed = geo_ext + offsets
    return jnp.transpose(placed, (2, 0, 1, 3)).reshape(3, 9 * atom_count)

def edge_basis(placed, own_place, neighbours, live_count):
    atom_count, slot_count = neighbours.shape
    displacement = (placed[:, neighbours] - own_place[:, :, None]) * spacing
    distance = jnp.sqrt(lax.optimization_barrier(jnp.sum(displacement * displacement, axis=0)))
    direction = displacement / distance[None]
    scaled = distance / cutoff
    scaled_sq = scaled * scaled
    scaled_six = scaled_sq * scaled_sq * scaled_sq
    envelope = 1.0 - 28.0 * scaled_six + 48.0 * scaled_six * scaled - 21.0 * scaled_six * scaled_sq
    active = (jnp.arange(slot_count, dtype=jnp.int32)[None, :] < live_count[:, None]) & (scaled < 1.0)
    envelope = jnp.where(active, envelope, 0.0)
    bessel_order = jnp.arange(1, NB + 1, dtype=jnp.float32)
    radial_basis = math.sqrt(2.0 / cutoff) * jnp.sin(bessel_order * (math.pi / cutoff) * distance[:, :, None]) / distance[:, :, None]
    along_x = direction[0]
    along_y = direction[1]
    along_z = direction[2]
    root_three = math.sqrt(3.0)
    root_fifteen = math.sqrt(15.0)
    root_five = math.sqrt(5.0)
    harmonic = jnp.stack([jnp.ones_like(along_x), root_three * along_x, root_three * along_y, root_three * along_z, root_fifteen * along_x * along_y, root_fifteen * along_y * along_z, 0.5 * root_five * (3.0 * along_z * along_z - 1.0), root_fifteen * along_x * along_z, 0.5 * root_fifteen * (along_x * along_x - along_y * along_y)], axis=-1)
    return (radial_basis.astype(jnp.bfloat16), envelope, harmonic)

def message_layer(extended_state, node_state, radial_basis, envelope, harmonic, neighbours, weight_in, weight_out, weight_mix, weight_product, weight_read):
    atom_count, slot_count = neighbours.shape
    channels = node_state.shape[-1]
    hidden = jax.nn.silu(jnp.dot(radial_basis.reshape(atom_count * slot_count, -1), weight_in, preferred_element_type=jnp.float32)).astype(jnp.bfloat16)
    radial = jnp.dot(hidden, weight_out, preferred_element_type=jnp.float32).reshape(atom_count, slot_count, 3, channels) * envelope[:, :, None, None]
    neighbour_state = extended_state[neighbours]
    weighted = radial * neighbour_state[:, :, None, :].astype(jnp.float32)
    highest = lax.Precision.HIGHEST
    degree_zero = jnp.einsum('akc,ak->ac', weighted[:, :, 0], harmonic[:, :, 0], precision=highest)
    degree_one = jnp.einsum('akc,akm->amc', weighted[:, :, 1], harmonic[:, :, 1:4], precision=highest)
    degree_two = jnp.einsum('akc,akm->amc', weighted[:, :, 2], harmonic[:, :, 4:9], precision=highest)
    gathered = (jnp.concatenate([degree_zero[:, None], degree_one, degree_two], axis=1) * neighbour_scale).astype(jnp.bfloat16)
    mixed_zero = jnp.dot(gathered[:, 0], weight_mix[0], preferred_element_type=jnp.float32)
    mixed_one = jnp.dot(gathered[:, 1:4].reshape(-1, channels), weight_mix[1], preferred_element_type=jnp.float32).reshape(atom_count, 3, channels)
    mixed_two = jnp.dot(gathered[:, 4:9].reshape(-1, channels), weight_mix[2], preferred_element_type=jnp.float32).reshape(atom_count, 5, channels)
    invariants = jnp.concatenate([mixed_zero, lax.optimization_barrier(jnp.sum(mixed_one * mixed_one, axis=1)), lax.optimization_barrier(jnp.sum(mixed_two * mixed_two, axis=1))], axis=-1).astype(jnp.bfloat16)
    update = jax.nn.silu(jnp.dot(invariants, weight_product, preferred_element_type=jnp.float32))
    new_state = (node_state.astype(jnp.float32) + update).astype(jnp.bfloat16)
    energy_term = jnp.dot(new_state, weight_read, preferred_element_type=jnp.float32)
    return (new_state, energy_term)

def spline_weights(fraction):
    rest = 1.0 - fraction
    cube = fraction * fraction * fraction
    square = fraction * fraction
    return jnp.stack([rest * rest * rest / 6.0, (3.0 * cube - 6.0 * square + 4.0) / 6.0, (-3.0 * cube + 3.0 * square + 3.0 * fraction + 1.0) / 6.0, cube / 6.0])

def influence(freq_z, freq_x, freq_y, size_x, size_y, size_z):

    def signed_freq(wavenumber, length):
        return jnp.where(wavenumber < length // 2, wavenumber, wavenumber - length).astype(jnp.float32) / (length * spacing)

    def modulus(wavenumber, length):
        cosine = jnp.cos(2.0 * math.pi / length * wavenumber.astype(jnp.float32))
        return (2.0 + cosine) * (2.0 + cosine) / 9.0
    along_z = signed_freq(freq_z, size_z)[:, None, None]
    along_x = signed_freq(freq_x, size_x)[None, :, None]
    along_y = signed_freq(freq_y, size_y)[None, None, :]
    squared = along_z * along_z + along_x * along_x + along_y * along_y
    safe_sq = jnp.where(squared > 0.0, squared, 1.0)
    moduli = modulus(freq_z, size_z)[:, None, None] * modulus(freq_x, size_x)[None, :, None] * modulus(freq_y, size_y)[None, None, :]
    volume = size_x * size_y * size_z * spacing * spacing * spacing
    values = coulomb * jnp.exp(-2.0 * math.pi * math.pi * smearing * smearing * squared) / (math.pi * volume * safe_sq * moduli)
    return jnp.where(squared > 0.0, values, 0.0)

def reference(atom_cells, atom_frac, species, nbr_index, nbr_count, embed, radial_in, radial_out, mix_weight, product_weight, read_weight, charge_weight):
    domain_count = N_DOMAIN
    inner_count = N_INNER
    atom_count = ATOM_DEV
    channels = C
    planes_x = 4 * LX
    planes_y = 4 * LY
    full_x = planes_x * domain_count
    full_y = planes_y * inner_count
    blocks_all = domain_count * inner_count
    geometry = atom_cells.astype(jnp.float32) + atom_frac
    geo_ext = surround(geometry).reshape(blocks_all, 3, 3, 3, atom_count)
    own_all = geometry.reshape(blocks_all, 3, atom_count)
    nbr_all = nbr_index.reshape(blocks_all, atom_count, K)
    count_all = nbr_count.reshape(blocks_all, atom_count)
    node_state = embed[species]
    energy = jnp.zeros((blocks_all, atom_count), jnp.float32)
    for layer_index in range(LAYERS):
        extended = surround(node_state).reshape(blocks_all, 9 * atom_count, channels)

        def one_block(block_items):
            geo_block, own_block, nbr_block, count_block, ext_block, state_block = block_items
            placed = place_blocks(geo_block, planes_x, planes_y)
            radial_basis, envelope, harmonic = edge_basis(placed, own_block, nbr_block, count_block)
            return message_layer(ext_block, state_block, radial_basis, envelope, harmonic, nbr_block, radial_in[layer_index], radial_out[layer_index], mix_weight[layer_index], product_weight[layer_index], read_weight[layer_index])
        new_state, energy_term = lax.map(one_block, (geo_ext, own_all, nbr_all, count_all, extended, node_state.reshape(blocks_all, atom_count, channels)))
        node_state = new_state.reshape(domain_count, inner_count, atom_count, channels)
        energy = energy + energy_term
    latent = jnp.dot(node_state.reshape(-1, channels), charge_weight, preferred_element_type=jnp.float32).reshape(domain_count, inner_count, atom_count)
    charge = latent - jnp.sum(latent) / (blocks_all * atom_count)
    weights = spline_weights(atom_frac)
    offsets = jnp.arange(4, dtype=jnp.int32) - 1
    anchor_x = (jnp.arange(domain_count, dtype=jnp.int32) * planes_x)[:, None, None]
    anchor_y = (jnp.arange(inner_count, dtype=jnp.int32) * planes_y)[None, :, None]
    index_x = (atom_cells[:, :, 0][None] + anchor_x[None] + offsets[:, None, None, None]) % full_x
    index_y = (atom_cells[:, :, 1][None] + anchor_y[None] + offsets[:, None, None, None]) % full_y
    index_z = atom_cells[:, :, 2][None] + offsets[:, None, None, None]
    flat_index = (index_x[:, None, None] * full_y + index_y[None, :, None]) * MZ + index_z[None, None, :]
    spread_weight = weights[:, :, :, 0][:, None, None] * weights[:, :, :, 1][None, :, None] * weights[:, :, :, 2][None, None, :]
    charge_mesh = jnp.zeros((full_x * full_y * MZ,), jnp.float32).at[flat_index.reshape(-1)].add((spread_weight * charge[None, None, None]).reshape(-1))
    spectrum = jnp.fft.fftn(charge_mesh.reshape(full_x, full_y, MZ))
    influence_mesh = jnp.transpose(influence(jnp.arange(MZ, dtype=jnp.int32), jnp.arange(full_x, dtype=jnp.int32), jnp.arange(full_y, dtype=jnp.int32), full_x, full_y, MZ), (1, 2, 0))
    potential = jnp.real(jnp.fft.ifftn(spectrum * influence_mesh)) * (full_x * full_y * MZ)
    potential = potential.astype(jnp.float32).reshape(-1)
    potential_at = lax.optimization_barrier(jnp.sum(potential[flat_index] * spread_weight, axis=(0, 1, 2)))
    atom_energy = energy.reshape(domain_count, inner_count, atom_count) + 0.5 * charge * potential_at
    return (atom_energy, potential_at)
```

```python
import functools
import math

import jax
import jax.numpy as jnp
import ml_dtypes
import numpy as np
from jax import lax
from jax.experimental import pallas as pl
from jax.experimental.pallas import tpu as pltpu
from jax.sharding import PartitionSpec as P

MESH = pl.DeviceIdType.MESH
VMEM = pltpu.VMEM
F32 = jnp.float32
BF16 = jnp.bfloat16

spacing = 0.55
cutoff = 5.0
smearing = 0.2
coulomb = 14.399645
neighbour_scale = 0.25

Z_LOW = 111
Z_SPAN = 33
PLANES = 2 * Z_SPAN
ROW_LOW = 504 // 128
ROW_HIGH = 4103 // 128

DEGREE = (0, 1, 1, 1, 2, 2, 2, 2, 2)


def dot(a, b):
    return lax.dot_general(a, b, (((1,), (0,)), ((), ())), preferred_element_type=F32)


def dot_nt(a, b):
    return lax.dot_general(a, b, (((1,), (1,)), ((), ())), preferred_element_type=F32)


def split(x):
    high = x.astype(BF16)
    return high, (x - high.astype(F32)).astype(BF16)


def dot_split(a, b, form):
    return form(a[0], b[0]) + (form(a[0], b[1]) + form(a[1], b[0]))


def basis_rows(length, positions):
    half = length // 2
    k = np.arange(half)
    angle = 2.0 * np.pi * ((k[:, None] * positions[None, :]) % length) / length
    cosine = np.cos(angle)
    sine = np.sin(angle)
    sine[0] = np.cos(np.pi * positions)
    return np.concatenate([cosine, sine], axis=0)


def host_split(x):
    x = x.astype(np.float32)
    high = x.astype(ml_dtypes.bfloat16)
    low = (x - high.astype(np.float32)).astype(ml_dtypes.bfloat16)
    return high, low


@functools.lru_cache(maxsize=None)
def host_tables(domain_count, inner_count, planes_x, planes_y, depth):
    full_x = planes_x * domain_count
    full_y = planes_y * inner_count
    table_x = basis_rows(full_x, np.arange(full_x))
    table_y = np.zeros((inner_count, 128, 3, full_y))
    for i in range(inner_count):
        all_y = basis_rows(full_y, (planes_y * i - 1 + np.arange(planes_y + 1)) % full_y).T
        table_y[i, : planes_y + 1, 0] = all_y
        table_y[i, 65:98, 1] = all_y[:33]
        table_y[i, 65:97, 2] = all_y[33:]
    table_y = table_y.reshape(inner_count * 128, 3 * full_y)

    def squared_freq(length, count):
        return (np.arange(count) / (length * spacing)) ** 2

    def modulus(length, count):
        return (2.0 + np.cos(2.0 * np.pi * np.arange(count) / length)) ** 2 / 9.0

    def twice(length, count):
        k = np.arange(count)
        return np.where((k == 0) | (k == length // 2), 1.0, 2.0)

    cx, cy, cz = full_x // 2 + 1, full_y // 2 + 1, depth // 2 + 1
    squared = (
        squared_freq(full_x, cx)[:, None, None]
        + squared_freq(full_y, cy)[None, :, None]
        + squared_freq(depth, cz)[None, None, :]
    )
    safe = np.where(squared > 0.0, squared, 1.0)
    moduli = (
        modulus(full_x, cx)[:, None, None]
        * modulus(full_y, cy)[None, :, None]
        * modulus(depth, cz)[None, None, :]
    )
    volume = full_x * full_y * depth * spacing**3
    kernel = (
        coulomb
        * np.exp(-2.0 * np.pi**2 * smearing**2 * squared)
        / (np.pi * volume * safe * moduli)
    )
    kernel = np.where(squared > 0.0, kernel, 0.0)
    kernel = kernel * twice(full_x, cx)[:, None, None] * twice(full_y, cy)[None, :, None]
    step = np.arange(Z_SPAN)
    along = np.cos(2.0 * np.pi * np.arange(cz)[:, None] * step[None, :] / depth)
    along = along * twice(depth, cz)[:, None]
    wave = np.cos(np.pi * (2 * np.arange(Z_SPAN)[None, :] + 1) * step[:, None] / (2 * Z_SPAN))
    wave = wave * np.where(step == 0, 1.0, 2.0)[:, None] / Z_SPAN
    gain = np.moveaxis(kernel @ (along @ wave), 2, 0)
    order_y = np.concatenate([np.arange(full_y // 2), [full_y // 2], np.arange(1, full_y // 2)])
    gain = gain[:, :, order_y]
    half = full_x // 2
    padded = np.zeros((Z_SPAN, half + 8, full_y), np.float32)
    padded[:, :half] = gain[:, :half]
    padded[:, half] = gain[:, half]
    plane = np.arange(PLANES)
    angle = (
        np.pi * (2 * (plane // 2)[:, None] + 1) * np.arange(40)[None, :] / (2 * Z_SPAN)
    )
    zeta = np.where(plane[:, None] % 2 == 0, np.cos(angle), np.sin(angle))
    zeta[:, Z_SPAN:] = 0.0
    zeta_full = np.zeros((72, 40), np.float32)
    zeta_full[:PLANES] = zeta
    return dict(
        x=host_split(table_x),
        xt=host_split(table_x.T),
        y=host_split(table_y),
        gain=padded,
        zeta=zeta_full,
    )


def exchange_kernel(counts, cells_ref, frac_ref, species_ref, ext_ref, mine, send_sem, recv_sem):
    at = (lax.axis_index("domain"), lax.axis_index("inner"))
    barrier = pltpu.get_barrier_semaphore()
    moves = [(dx, dy) for dx in (-1, 0, 1) for dy in (-1, 0, 1) if (dx, dy) != (0, 0)]

    def target(move):
        return tuple(lax.rem(at[n] + counts[n] + move[n], counts[n]) for n in range(2))

    for move in moves:
        pl.semaphore_signal(barrier, inc=1, device_id=target(move), device_id_type=MESH)
    mine[...] = jnp.zeros_like(mine)
    mine[0:3, :] = cells_ref[...].astype(F32) + frac_ref[...]
    mine[3:4, :] = species_ref[...].astype(F32)
    pl.semaphore_wait(barrier, len(moves))
    copies = []
    for n, (dx, dy) in enumerate(moves):
        copy = pltpu.make_async_remote_copy(
            src_ref=mine,
            dst_ref=ext_ref.at[(1 - dx) * 3 + (1 - dy)],
            send_sem=send_sem.at[n],
            recv_sem=recv_sem.at[n],
            device_id=target((dx, dy)),
            device_id_type=MESH,
        )
        copy.start()
        copies.append(copy)
    ext_ref[4] = mine[...]
    for copy in copies:
        copy.wait()


def exchange(cells, frac, species, counts):
    atoms = cells.shape[-1]
    return pl.pallas_call(
        functools.partial(exchange_kernel, counts),
        out_shape=jax.ShapeDtypeStruct((9, 8, atoms), F32),
        in_specs=[pl.BlockSpec(memory_space=VMEM)] * 3,
        out_specs=pl.BlockSpec(memory_space=VMEM),
        scratch_shapes=[
            VMEM((8, atoms), F32),
            pltpu.SemaphoreType.DMA((8,)),
            pltpu.SemaphoreType.DMA((8,)),
        ],
        compiler_params=pltpu.CompilerParams(collective_id=0, has_side_effects=True),
        name="exchange",
    )(cells, frac, species)


def half_tanh_silu(x):
    half = 0.5 * x
    return half + half * jnp.tanh(half)


def message_kernel(
    planes,
    ext_ref,
    nbr_ref,
    count_ref,
    embed_ref,
    win_ref,
    wout_ref,
    mix_ref,
    prod_ref,
    read_ref,
    charge_ref,
    out_ref,
    placed,
    found,
    weight,
    basis,
    onehot,
    radial,
    state,
    total,
):
    atoms = ext_ref.shape[-1]
    slots = nbr_ref.shape[0]
    tiles = atoms // 128
    channels = embed_ref.shape[1]
    for b in range(9):
        row = lax.broadcasted_iota(jnp.int32, (8, atoms), 0)
        shift = jnp.where(
            row == 0, planes[0] * (b // 3 - 1.0), jnp.where(row == 1, planes[1] * (b % 3 - 1.0), 0.0)
        )
        placed[b] = ext_ref[b] + shift

    def gather(t, carry):
        rows = pl.ds(pl.multiple_of((t // tiles) * 8, 8), 8)
        lanes = pl.ds(pl.multiple_of((t % tiles) * 128, 128), 128)
        index = nbr_ref[rows, lanes]
        low = index & 127
        high = index >> 7
        values = [jnp.zeros((8, 128), F32) for _ in range(4)]
        for r in range(ROW_LOW, ROW_HIGH + 1):
            here = high == r
            piece = slice((r % tiles) * 128, (r % tiles) * 128 + 128)
            for c in range(4):
                line = jnp.broadcast_to(placed[r // tiles, c : c + 1, piece], (8, 128))
                picked = jnp.take_along_axis(line, low, axis=1)
                values[c] = jnp.where(here, picked, values[c])
        for c in range(4):
            found[c, rows, lanes] = values[c]
        return carry

    lax.fori_loop(0, (slots // 8) * tiles, gather, 0)

    own = ext_ref[4]
    dx = (found[0] - own[0:1]) * spacing
    dy = (found[1] - own[1:2]) * spacing
    dz = (found[2] - own[2:3]) * spacing
    distance = jnp.sqrt(dx * dx + dy * dy + dz * dz)
    inverse = 1.0 / distance
    ux, uy, uz = dx * inverse, dy * inverse, dz * inverse
    scaled = distance * (1.0 / cutoff)
    scaled_sq = scaled * scaled
    six = scaled_sq * scaled_sq * scaled_sq
    envelope = 1.0 - 28.0 * six + 48.0 * six * scaled - 21.0 * six * scaled_sq
    slot = lax.broadcasted_iota(jnp.int32, (slots, atoms), 0)
    active = (slot < count_ref[...]) & (scaled < 1.0)
    envelope = jnp.where(active, envelope * neighbour_scale, 0.0)
    r3, r5, r15 = math.sqrt(3.0), math.sqrt(5.0), math.sqrt(15.0)
    factors = (
        None,
        r3 * ux,
        r3 * uy,
        r3 * uz,
        r15 * ux * uy,
        r15 * uy * uz,
        0.5 * r5 * (3.0 * uz * uz - 1.0),
        r15 * ux * uz,
        0.5 * r15 * (ux * ux - uy * uy),
    )
    for m, factor in enumerate(factors):
        full = envelope if factor is None else envelope * factor
        for q in range(slots // 8):
            weight[m, q] = full[8 * q : 8 * q + 8]
    theta = (math.pi / cutoff) * distance
    sine = jnp.sin(theta)
    cosine = 2.0 * jnp.cos(theta)
    scale = math.sqrt(2.0 / cutoff) * inverse
    before = jnp.zeros_like(sine)
    species = found[3]
    for n in range(8):
        value = scale * sine
        marks = (species == float(n)).astype(F32)
        for q in range(slots // 8):
            basis[q, 8 * n : 8 * n + 8, :] = value[8 * q : 8 * q + 8]
            onehot[q, 8 * n : 8 * n + 8, :] = marks[8 * q : 8 * q + 8]
        sine, before = cosine * sine - before, sine

    spread_in = (
        lax.broadcasted_iota(jnp.int32, (8, 64), 1) // 8
        == lax.broadcasted_iota(jnp.int32, (8, 64), 0)
    ).astype(BF16)

    def by_slot(matrix_t):
        outputs = matrix_t.shape[0]
        wide = dot(matrix_t.astype(BF16), spread_in)
        full = jnp.concatenate([wide] * 8, axis=0)
        row = lax.broadcasted_iota(jnp.int32, full.shape, 0) // outputs
        column = lax.broadcasted_iota(jnp.int32, full.shape, 1) % 8
        return jnp.where(row == column, full, 0.0).astype(BF16)

    win_wide = by_slot(win_ref[...].astype(F32).T)
    embed_t = embed_ref[...].astype(F32).T
    embed_wide = by_slot(embed_t)
    wout_t = wout_ref[...].astype(F32).T.astype(BF16)
    hidden_size = win_ref.shape[1]
    total[...] = jnp.zeros_like(total)

    def octet(q, carry):
        hidden = dot(win_wide, basis[q].astype(BF16))
        hidden = half_tanh_silu(hidden).astype(BF16)
        state[...] = dot(embed_wide, onehot[q].astype(BF16))
        for k in range(8):
            radial[k] = dot(wout_t, hidden[k * hidden_size : (k + 1) * hidden_size])

        def tile(t, carry):
            lanes = pl.ds(pl.multiple_of((t % tiles) * 128, 128), 128)
            first = pl.multiple_of((t // tiles) * 16, 16)
            sums = [total[m, pl.ds(first, 16), lanes] for m in range(9)]
            for k in range(8):
                near = state[pl.ds(k * channels + first, 16), lanes]
                weighted = [
                    radial[k, pl.ds(l * channels + first, 16), lanes] * near for l in range(3)
                ]
                for m in range(9):
                    line = weight[m, q, k : k + 1, lanes]
                    sums[m] = sums[m] + weighted[DEGREE[m]] * line
            for m in range(9):
                total[m, pl.ds(first, 16), lanes] = sums[m]
            return carry

        lax.fori_loop(0, tiles * (channels // 16), tile, 0)
        return carry

    lax.fori_loop(0, slots // 8, octet, 0)

    invariants = [None, None, None]
    for m in range(9):
        degree = DEGREE[m]
        mix_t = mix_ref[degree].astype(F32).T.astype(BF16)
        mixed = dot(mix_t, total[m].astype(BF16))
        if degree == 0:
            invariants[0] = mixed
        elif invariants[degree] is None:
            invariants[degree] = mixed * mixed
        else:
            invariants[degree] = invariants[degree] + mixed * mixed
    stacked = jnp.concatenate(invariants, axis=0).astype(BF16)
    prod_t = prod_ref[...].astype(F32).T.astype(BF16)
    update = dot(prod_t, stacked)
    update = update / (1.0 + jnp.exp(-update))
    kinds = lax.broadcasted_iota(jnp.int32, (8, atoms), 0).astype(F32)
    own_state = dot(embed_t.astype(BF16), (kinds == own[3:4]).astype(BF16))
    new_state = (own_state + update).astype(BF16)
    rows = jnp.concatenate(
        [read_ref[...], charge_ref[...], jnp.zeros((14, channels), BF16)], axis=0
    )
    out_ref[...] = dot(rows, new_state)[0:8]


def message(ext, nbr_t, count, embed, win, wout, mix, prod, read, charge, planes):
    atoms = ext.shape[-1]
    slots = nbr_t.shape[0]
    channels = embed.shape[1]
    octets = slots // 8
    return pl.pallas_call(
        functools.partial(message_kernel, planes),
        out_shape=jax.ShapeDtypeStruct((8, atoms), F32),
        in_specs=[pl.BlockSpec(memory_space=VMEM)] * 10,
        out_specs=pl.BlockSpec(memory_space=VMEM),
        scratch_shapes=[
            VMEM((9, 8, atoms), F32),
            VMEM((4, slots, atoms), F32),
            VMEM((9, octets, 8, atoms), F32),
            VMEM((octets, 64, atoms), F32),
            VMEM((octets, 64, atoms), F32),
            VMEM((8, 3 * channels, atoms), F32),
            VMEM((8 * channels, atoms), F32),
            VMEM((9, channels, atoms), F32),
        ],
        compiler_params=pltpu.CompilerParams(vmem_limit_bytes=40 << 20),
        name="message",
    )(ext, nbr_t, count, embed, win, wout, mix, prod, read, charge)


def spline_rows(fraction):
    rest = 1.0 - fraction
    square = fraction * fraction
    cube = square * fraction
    return (
        rest * rest * rest * (1.0 / 6.0),
        (3.0 * cube - 6.0 * square + 4.0) * (1.0 / 6.0),
        (-3.0 * cube + 3.0 * square + 3.0 * fraction + 1.0) * (1.0 / 6.0),
        cube * (1.0 / 6.0),
    )


def stencil_rows(rows, first, weights):
    at = lax.broadcasted_iota(jnp.int32, (rows, first.shape[1]), 0) - first
    out = jnp.where(at == 0, weights[0], 0.0)
    for j in range(1, 4):
        out = jnp.where(at == j, weights[j], out)
    return out


def mesh_kernel(
    counts,
    cells_ref,
    frac_ref,
    local_ref,
    zeta_ref,
    x_hi,
    x_lo,
    xt_hi,
    xt_lo,
    y_hi,
    y_lo,
    gain_ref,
    energy_ref,
    potential_ref,
    sums,
    patch32,
    patch,
    received,
    spectrum,
    answer,
    back,
    back32,
    gain,
    product,
    sum_send,
    sum_recv,
    patch_send,
    patch_recv,
    back_send,
    back_recv,
    gain_sem,
):
    domain_count, inner_count = counts
    devices = domain_count * inner_count
    d, i = lax.axis_index("domain"), lax.axis_index("inner")
    me = d * inner_count + i
    atoms = cells_ref.shape[-1]
    per_core = devices // 2

    def device(t):
        return (t // inner_count, lax.rem(t, inner_count))

    def owner(r):
        rest = lax.rem(r, per_core)
        return (rest // 2, lax.rem(rest, 2) * 2 + r // per_core)

    my_plane = d * 2 + i // 2 + per_core * lax.rem(i, 2)
    owns = my_plane < PLANES

    barrier = pltpu.get_barrier_semaphore()

    def greet(k, carry):
        pl.semaphore_signal(
            barrier, inc=1, device_id=device(lax.rem(me + k, devices)), device_id_type=MESH
        )
        return carry

    lax.fori_loop(1, devices, greet, 0)
    gain_copy = pltpu.make_async_copy(
        gain_ref.at[jnp.minimum(my_plane, PLANES - 1) // 2], gain, gain_sem
    )
    gain_copy.start()

    latent = local_ref[1:2, :]
    part = latent[:, 0:128]
    for t in range(1, atoms // 128):
        part = part + latent[:, t * 128 : (t + 1) * 128]
    sums[me] = part

    weights_x = spline_rows(frac_ref[0:1, :])
    weights_y = spline_rows(frac_ref[1:2, :])
    weights_z = spline_rows(frac_ref[2:3, :])
    cell_x, cell_y, cell_z = cells_ref[0:1, :], cells_ref[1:2, :], cells_ref[2:3, :]
    sten_x = stencil_rows(16, cell_x - 1, weights_x)
    rim_x = jnp.where(cell_x == 0, weights_x[0], 0.0)
    sten_z = stencil_rows(40, cell_z - 1 - Z_LOW, weights_z)
    lane = lax.broadcasted_iota(jnp.int32, (128, atoms), 0)
    y_main = split(stencil_rows(128, cell_y, weights_y))
    y_low = split(jnp.where(lane <= 97, stencil_rows(128, cell_y + 65, weights_y), 0.0))
    y_high = split(jnp.where(lane >= 65, stencil_rows(128, cell_y + 32, weights_y), 0.0))
    waves = jnp.dot(zeta_ref[...], sten_z, precision=lax.Precision.HIGHEST)

    pl.semaphore_wait(barrier, devices - 1)

    def sum_copy(k):
        return pltpu.make_async_remote_copy(
            src_ref=sums.at[me],
            dst_ref=sums.at[me],
            send_sem=sum_send.at[k],
            recv_sem=sum_recv.at[k],
            device_id=device(lax.rem(me + k, devices)),
            device_id_type=MESH,
        )

    def sum_start(k, carry):
        sum_copy(k).start()
        return carry

    def sum_wait(k, carry):
        sum_copy(k).wait()
        return carry

    lax.fori_loop(1, devices, sum_start, 0)
    lax.fori_loop(1, devices, sum_wait, 0)
    mean = jnp.sum(jnp.sum(sums[...], axis=0), axis=1, keepdims=True) / (
        atoms * devices
    )
    charge = latent - mean

    charged = waves * charge
    for r in range(PLANES):
        product[16 * r : 16 * r + 16, :] = sten_x * charged[r : r + 1]
    patch32[...] = dot_split(split(product[...]), y_main, dot_nt)
    rim = split(charged * rim_x)
    low = dot_split(rim, y_low, dot_nt)
    high = dot_split(rim, y_high, dot_nt)
    patch32[pl.ds(0, PLANES, 16), :] = patch32[pl.ds(0, PLANES, 16), :] + low[:PLANES]
    patch32[pl.ds(1, PLANES, 16), :] = patch32[pl.ds(1, PLANES, 16), :] + high[:PLANES]
    patch[...] = patch32[...].astype(BF16)

    my_rows = pl.ds(pl.multiple_of(d * 16, 16), 16)
    my_lanes = pl.ds(pl.multiple_of(i * 128, 128), 128)

    def patch_copy(r):
        return pltpu.make_async_remote_copy(
            src_ref=patch.at[pl.ds(pl.multiple_of(r * 16, 16), 16), :],
            dst_ref=received.at[my_rows, my_lanes],
            send_sem=patch_send.at[r],
            recv_sem=patch_recv.at[me],
            device_id=owner(r),
            device_id_type=MESH,
        )

    def patch_start(k, carry):
        r = lax.rem(my_plane + k, PLANES)

        @pl.when(r != my_plane)
        def _():
            patch_copy(r).start()

        return carry

    lax.fori_loop(0, PLANES, patch_start, 0)

    def back_copy(t):
        return pltpu.make_async_remote_copy(
            src_ref=answer.at[
                pl.ds(pl.multiple_of((t // inner_count) * 16, 16), 16),
                pl.ds(pl.multiple_of(lax.rem(t, inner_count) * 128, 128), 128),
            ],
            dst_ref=back.at[pl.ds(pl.multiple_of(my_plane * 16, 16), 16), :],
            send_sem=back_send.at[t],
            recv_sem=back_recv.at[my_plane],
            device_id=device(t),
            device_id_type=MESH,
        )

    gain_copy.wait()

    @pl.when(owns)
    def _():
        mine = pl.ds(pl.multiple_of(my_plane * 16, 16), 16)
        received[my_rows, my_lanes] = patch[mine, :]

        def arrive(k, carry):
            t = lax.rem(me + k, devices)
            pltpu.make_async_remote_copy(
                src_ref=patch.at[pl.ds(0, 16), :],
                dst_ref=received.at[
                    pl.ds(pl.multiple_of((t // inner_count) * 16, 16), 16),
                    pl.ds(pl.multiple_of(lax.rem(t, inner_count) * 128, 128), 128),
                ],
                send_sem=patch_send.at[0],
                recv_sem=patch_recv.at[t],
                device_id=device(t),
                device_id_type=MESH,
            ).wait_recv()
            return carry

        lax.fori_loop(1, devices, arrive, 0)
        grid = received[...]
        along_y = dot(grid, y_hi[...]) + dot(grid, y_lo[...])
        full_y = along_y.shape[1] // 3
        row = lax.rem(lax.broadcasted_iota(jnp.int32, (grid.shape[0], full_y), 0), 16)
        low_rim = jnp.where(row == 0, along_y[:, full_y : 2 * full_y], 0.0)
        high_rim = jnp.where(row == 1, along_y[:, 2 * full_y :], 0.0)
        count_x = grid.shape[0]
        lines = (
            along_y[:, :full_y]
            + pltpu.roll(low_rim, count_x - 1, 0)
            + pltpu.roll(high_rim, count_x - 2, 0)
        )
        spectrum[...] = dot_split((x_hi[...], x_lo[...]), split(lines), dot)
        half = count_x // 2
        top = gain[0:half, :]
        first_row = lax.broadcasted_iota(jnp.int32, (half, full_y), 0) == 0
        bottom = jnp.where(first_row, gain[half : half + 1, :], top)
        filtered = jnp.concatenate([spectrum[0:half] * top, spectrum[half:] * bottom], axis=0)
        lines = dot_split((xt_hi[...], xt_lo[...]), split(filtered), dot)
        wide = jnp.concatenate(
            [
                lines,
                jnp.where(row == 0, pltpu.roll(lines, 1, 0), 0.0),
                jnp.where(row == 1, pltpu.roll(lines, 2, 0), 0.0),
            ],
            axis=1,
        )
        answer[...] = dot_split(split(wide), (y_hi[...], y_lo[...]), dot_nt).astype(BF16)

        def back_start(k, carry):
            back_copy(lax.rem(me + k, devices)).start()
            return carry

        lax.fori_loop(1, devices, back_start, 0)
        back[mine, :] = answer[my_rows, my_lanes]

    def back_arrive(r, carry):
        @pl.when(r != my_plane)
        def _():
            pltpu.make_async_remote_copy(
                src_ref=answer.at[pl.ds(0, 16), pl.ds(0, 128)],
                dst_ref=back.at[pl.ds(pl.multiple_of(r * 16, 16), 16), :],
                send_sem=back_send.at[0],
                recv_sem=back_recv.at[r],
                device_id=owner(r),
                device_id_type=MESH,
            ).wait_recv()

        return carry

    lax.fori_loop(0, PLANES, back_arrive, 0)
    given = back[...]
    at_atoms = dot(given, y_main[0]) + dot(given, y_main[1])
    back32[...] = given.astype(F32)
    product[...] = at_atoms
    at_low = back32[pl.ds(0, PLANES, 16), :].astype(BF16)
    at_high = back32[pl.ds(1, PLANES, 16), :].astype(BF16)
    at_rim = dot(at_low, y_low[0]) + dot(at_low, y_low[1])
    at_rim = at_rim + dot(at_high, y_high[0]) + dot(at_high, y_high[1])
    gathered = jnp.zeros((8, atoms), F32)
    for r in range(PLANES):
        piece = (
            product[16 * r : 16 * r + 8, :] * sten_x[0:8]
            + product[16 * r + 8 : 16 * r + 16, :] * sten_x[8:16]
        )
        gathered = gathered + piece * waves[r : r + 1]
    value = jnp.sum(gathered, axis=0, keepdims=True) + rim_x * jnp.sum(
        at_rim * waves[:PLANES], axis=0, keepdims=True
    )
    potential_ref[...] = value
    energy_ref[...] = local_ref[0:1, :] + 0.5 * charge * value

    def patch_done(r, carry):
        @pl.when(r != my_plane)
        def _():
            patch_copy(r).wait_send()

        return carry

    lax.fori_loop(0, PLANES, patch_done, 0)

    @pl.when(owns)
    def _():
        def back_done(k, carry):
            back_copy(lax.rem(me + k, devices)).wait_send()
            return carry

        lax.fori_loop(1, devices, back_done, 0)


def mesh_potential(cells, frac, local_rows, tables, counts):
    atoms = cells.shape[-1]
    devices = counts[0] * counts[1]
    full_x = counts[0] * 16
    full_y = counts[1] * 64
    lanes = counts[1] * 128
    dma = pltpu.SemaphoreType.DMA
    vmem = pl.BlockSpec(memory_space=VMEM)
    return pl.pallas_call(
        functools.partial(mesh_kernel, counts),
        out_shape=[jax.ShapeDtypeStruct((1, atoms), F32)] * 2,
        in_specs=[vmem] * 10 + [pl.BlockSpec(memory_space=pl.ANY)],
        out_specs=[vmem] * 2,
        scratch_shapes=[
            VMEM((devices, 1, 128), F32),
            VMEM((PLANES * 16, 128), F32),
            VMEM((PLANES * 16, 128), BF16),
            VMEM((full_x, lanes), BF16),
            VMEM((full_x, full_y), F32),
            VMEM((full_x, lanes), BF16),
            VMEM((PLANES * 16, 128), BF16),
            VMEM((PLANES * 16, 128), F32),
            VMEM((full_x // 2 + 8, full_y), F32),
            VMEM((PLANES * 16, atoms), F32),
            dma((devices,)),
            dma((devices,)),
            dma((PLANES,)),
            dma((devices,)),
            dma((devices,)),
            dma((PLANES,)),
            dma,
        ],
        compiler_params=pltpu.CompilerParams(
            collective_id=1, has_side_effects=True, vmem_limit_bytes=48 << 20
        ),
        name="mesh_potential",
    )(
        cells,
        frac,
        local_rows,
        jnp.asarray(tables["zeta"]),
        *[jnp.asarray(part) for name in ("x", "xt", "y") for part in tables[name]],
        jnp.asarray(tables["gain"]),
    )


def local(
    counts,
    atom_cells,
    atom_frac,
    species,
    nbr_index,
    nbr_count,
    embed,
    radial_in,
    radial_out,
    mix_weight,
    product_weight,
    read_weight,
    charge_weight,
):
    planes = (16, 64)
    tables = host_tables(*counts, *planes, 256)
    cells = atom_cells[0, 0]
    frac = atom_frac[0, 0]
    ext = exchange(cells, frac, species[0], counts)
    rows = message(
        ext,
        nbr_index[0, 0].T,
        nbr_count[0],
        embed,
        radial_in[0],
        radial_out[0],
        mix_weight[0],
        product_weight[0],
        read_weight,
        charge_weight[None],
        planes,
    )
    energy, potential = mesh_potential(cells, frac, rows, tables, counts)
    return (energy[None], potential[None])


def solution(mesh):
    counts = (mesh.shape["domain"], mesh.shape["inner"])
    in_specs = (
        P("domain", "inner", None, None),
        P("domain", "inner", None, None),
        P("domain", "inner", None),
        P("domain", "inner", None, None),
        P("domain", "inner", None),
        P(),
        P(),
        P(),
        P(),
        P(),
        P(),
        P(),
    )
    out_specs = (P("domain", "inner", None), P("domain", "inner", None))
    return jax.shard_map(
        functools.partial(local, counts),
        mesh=mesh,
        in_specs=in_specs,
        out_specs=out_specs,
        check_vma=False,
    )
```

```python
import functools
import math

import jax
import jax.numpy as jnp
import numpy as np
from jax import lax
from jax.experimental import pallas as pl
from jax.experimental.pallas import tpu as pltpu
from jax.sharding import PartitionSpec as P

MESH = pl.DeviceIdType.MESH
VMEM = pltpu.VMEM
F32 = jnp.float32
BF16 = jnp.bfloat16

spacing = 0.55
cutoff = 5.0
smearing = 0.2
coulomb = 14.399645
neighbour_scale = 0.25

Z_LOW = 111
Z_SPAN = 33
PLANES = 2 * Z_SPAN
ROW_LOW = 504 // 128
ROW_HIGH = 4103 // 128

DEGREE = (0, 1, 1, 1, 2, 2, 2, 2, 2)


def dot(a, b):
    return lax.dot_general(a, b, (((1,), (0,)), ((), ())), preferred_element_type=F32)


def dot_nt(a, b):
    return lax.dot_general(a, b, (((1,), (1,)), ((), ())), preferred_element_type=F32)


def split(x):
    high = x.astype(BF16)
    return high, (x - high.astype(F32)).astype(BF16)


def dot_split(a, b, form):
    return form(a[0], b[0]) + (form(a[0], b[1]) + form(a[1], b[0]))


def basis_rows(length, positions):
    half = length // 2
    k = np.arange(half)
    angle = 2.0 * np.pi * ((k[:, None] * positions[None, :]) % length) / length
    cosine = np.cos(angle)
    sine = np.sin(angle)
    sine[0] = np.cos(np.pi * positions)
    return np.concatenate([cosine, sine], axis=0)


@functools.lru_cache(maxsize=None)
def host_tables(domain_count, inner_count, planes_x, planes_y, depth):
    full_x = planes_x * domain_count
    full_y = planes_y * inner_count
    table_x = basis_rows(full_x, np.arange(full_x))
    table_y = np.zeros((inner_count, 128, 3, full_y))
    for i in range(inner_count):
        all_y = basis_rows(full_y, (planes_y * i - 1 + np.arange(planes_y + 1)) % full_y).T
        table_y[i, : planes_y + 1, 0] = all_y
        table_y[i, 65:98, 1] = all_y[:33]
        table_y[i, 65:97, 2] = all_y[33:]
    table_y = table_y.reshape(inner_count * 128, 3 * full_y)

    def squared_freq(length, count):
        return (np.arange(count) / (length * spacing)) ** 2

    def modulus(length, count):
        return (2.0 + np.cos(2.0 * np.pi * np.arange(count) / length)) ** 2 / 9.0

    def twice(length, count):
        k = np.arange(count)
        return np.where((k == 0) | (k == length // 2), 1.0, 2.0)

    cx, cy, cz = full_x // 2 + 1, full_y // 2 + 1, depth // 2 + 1
    squared = (
        squared_freq(full_x, cx)[:, None, None]
        + squared_freq(full_y, cy)[None, :, None]
        + squared_freq(depth, cz)[None, None, :]
    )
    safe = np.where(squared > 0.0, squared, 1.0)
    moduli = (
        modulus(full_x, cx)[:, None, None]
        * modulus(full_y, cy)[None, :, None]
        * modulus(depth, cz)[None, None, :]
    )
    volume = full_x * full_y * depth * spacing**3
    kernel = (
        coulomb
        * np.exp(-2.0 * np.pi**2 * smearing**2 * squared)
        / (np.pi * volume * safe * moduli)
    )
    kernel = np.where(squared > 0.0, kernel, 0.0)
    kernel = kernel * twice(full_x, cx)[:, None, None] * twice(full_y, cy)[None, :, None]
    step = np.arange(Z_SPAN)
    along = np.cos(2.0 * np.pi * np.arange(cz)[:, None] * step[None, :] / depth)
    along = along * twice(depth, cz)[:, None]
    wave = np.cos(np.pi * (2 * np.arange(Z_SPAN)[None, :] + 1) * step[:, None] / (2 * Z_SPAN))
    wave = wave * np.where(step == 0, 1.0, 2.0)[:, None] / Z_SPAN
    gain = np.moveaxis(kernel @ (along @ wave), 2, 0)
    order_y = np.concatenate([np.arange(full_y // 2), [full_y // 2], np.arange(1, full_y // 2)])
    gain = gain[:, :, order_y]
    half = full_x // 2
    padded = np.zeros((Z_SPAN, half + 8, full_y), np.float32)
    padded[:, :half] = gain[:, :half]
    padded[:, half] = gain[:, half]
    plane = np.arange(PLANES)
    angle = (
        np.pi * (2 * (plane // 2)[:, None] + 1) * np.arange(40)[None, :] / (2 * Z_SPAN)
    )
    zeta = np.where(plane[:, None] % 2 == 0, np.cos(angle), np.sin(angle))
    zeta[:, Z_SPAN:] = 0.0
    zeta_full = np.zeros((72, 40), np.float32)
    zeta_full[:PLANES] = zeta
    return dict(
        x=table_x.astype(np.float32),
        xt=np.ascontiguousarray(table_x.T).astype(np.float32),
        y=table_y.astype(np.float32),
        gain=padded,
        zeta=zeta_full,
    )


def half_tanh_silu(x):
    half = 0.5 * x
    return half + half * jnp.tanh(half)


def message_rows(
    planes,
    ext_ref,
    nbr_ref,
    count_ref,
    embed_ref,
    win_ref,
    wout_ref,
    mix_ref,
    prod_ref,
    read_ref,
    charge_ref,
    placed,
    found,
    weight,
    basis,
    onehot,
    radial,
    state,
    total,
):
    atoms = ext_ref.shape[-1]
    slots = nbr_ref.shape[0]
    tiles = atoms // 128
    channels = embed_ref.shape[1]
    for b in range(9):
        row = lax.broadcasted_iota(jnp.int32, (8, atoms), 0)
        shift = jnp.where(
            row == 0, planes[0] * (b // 3 - 1.0), jnp.where(row == 1, planes[1] * (b % 3 - 1.0), 0.0)
        )
        placed[b] = ext_ref[b] + shift

    def gather(t, carry):
        rows = pl.ds(pl.multiple_of((t // tiles) * 8, 8), 8)
        lanes = pl.ds(pl.multiple_of((t % tiles) * 128, 128), 128)
        index = nbr_ref[rows, lanes]
        low = index & 127
        high = index >> 7
        values = [jnp.zeros((8, 128), F32) for _ in range(4)]
        for r in range(ROW_LOW, ROW_HIGH + 1):
            here = high == r
            piece = slice((r % tiles) * 128, (r % tiles) * 128 + 128)
            for c in range(4):
                line = jnp.broadcast_to(placed[r // tiles, c : c + 1, piece], (8, 128))
                picked = jnp.take_along_axis(line, low, axis=1)
                values[c] = jnp.where(here, picked, values[c])
        for c in range(4):
            found[c, rows, lanes] = values[c]
        return carry

    lax.fori_loop(0, (slots // 8) * tiles, gather, 0)

    own = ext_ref[4]
    dx = (found[0] - own[0:1]) * spacing
    dy = (found[1] - own[1:2]) * spacing
    dz = (found[2] - own[2:3]) * spacing
    distance = jnp.sqrt(dx * dx + dy * dy + dz * dz)
    inverse = 1.0 / distance
    ux, uy, uz = dx * inverse, dy * inverse, dz * inverse
    scaled = distance * (1.0 / cutoff)
    scaled_sq = scaled * scaled
    six = scaled_sq * scaled_sq * scaled_sq
    envelope = 1.0 - 28.0 * six + 48.0 * six * scaled - 21.0 * six * scaled_sq
    slot = lax.broadcasted_iota(jnp.int32, (slots, atoms), 0)
    active = (slot < count_ref[...]) & (scaled < 1.0)
    envelope = jnp.where(active, envelope * neighbour_scale, 0.0)
    r3, r5, r15 = math.sqrt(3.0), math.sqrt(5.0), math.sqrt(15.0)
    factors = (
        None,
        r3 * ux,
        r3 * uy,
        r3 * uz,
        r15 * ux * uy,
        r15 * uy * uz,
        0.5 * r5 * (3.0 * uz * uz - 1.0),
        r15 * ux * uz,
        0.5 * r15 * (ux * ux - uy * uy),
    )
    for m, factor in enumerate(factors):
        full = envelope if factor is None else envelope * factor
        for q in range(slots // 8):
            weight[m, q] = full[8 * q : 8 * q + 8]
    theta = (math.pi / cutoff) * distance
    sine = jnp.sin(theta)
    cosine = 2.0 * jnp.cos(theta)
    scale = math.sqrt(2.0 / cutoff) * inverse
    before = jnp.zeros_like(sine)
    species = found[3]
    for n in range(8):
        value = scale * sine
        marks = (species == float(n)).astype(F32)
        for q in range(slots // 8):
            basis[q, 8 * n : 8 * n + 8, :] = value[8 * q : 8 * q + 8]
            onehot[q, 8 * n : 8 * n + 8, :] = marks[8 * q : 8 * q + 8]
        sine, before = cosine * sine - before, sine

    spread_in = (
        lax.broadcasted_iota(jnp.int32, (8, 64), 1) // 8
        == lax.broadcasted_iota(jnp.int32, (8, 64), 0)
    ).astype(BF16)

    def by_slot(matrix_t):
        outputs = matrix_t.shape[0]
        wide = dot(matrix_t.astype(BF16), spread_in)
        full = jnp.concatenate([wide] * 8, axis=0)
        row = lax.broadcasted_iota(jnp.int32, full.shape, 0) // outputs
        column = lax.broadcasted_iota(jnp.int32, full.shape, 1) % 8
        return jnp.where(row == column, full, 0.0).astype(BF16)

    win_wide = by_slot(win_ref[...].astype(F32).T)
    embed_t = embed_ref[...].astype(F32).T
    embed_wide = by_slot(embed_t)
    wout_t = wout_ref[...].astype(F32).T.astype(BF16)
    hidden_size = win_ref.shape[1]
    total[...] = jnp.zeros_like(total)

    def octet(q, carry):
        hidden = dot(win_wide, basis[q].astype(BF16))
        hidden = half_tanh_silu(hidden).astype(BF16)
        state[...] = dot(embed_wide, onehot[q].astype(BF16))
        for k in range(8):
            radial[k] = dot(wout_t, hidden[k * hidden_size : (k + 1) * hidden_size])

        def tile(t, carry):
            lanes = pl.ds(pl.multiple_of((t % tiles) * 128, 128), 128)
            first = pl.multiple_of((t // tiles) * 16, 16)
            sums = [total[m, pl.ds(first, 16), lanes] for m in range(9)]
            for k in range(8):
                near = state[pl.ds(k * channels + first, 16), lanes]
                weighted = [
                    radial[k, pl.ds(l * channels + first, 16), lanes] * near for l in range(3)
                ]
                for m in range(9):
                    line = weight[m, q, k : k + 1, lanes]
                    sums[m] = sums[m] + weighted[DEGREE[m]] * line
            for m in range(9):
                total[m, pl.ds(first, 16), lanes] = sums[m]
            return carry

        lax.fori_loop(0, tiles * (channels // 16), tile, 0)
        return carry

    lax.fori_loop(0, slots // 8, octet, 0)

    invariants = [None, None, None]
    for m in range(9):
        degree = DEGREE[m]
        mix_t = mix_ref[degree].astype(F32).T.astype(BF16)
        mixed = dot(mix_t, total[m].astype(BF16))
        if degree == 0:
            invariants[0] = mixed
        elif invariants[degree] is None:
            invariants[degree] = mixed * mixed
        else:
            invariants[degree] = invariants[degree] + mixed * mixed
    stacked = jnp.concatenate(invariants, axis=0).astype(BF16)
    prod_t = prod_ref[...].astype(F32).T.astype(BF16)
    update = dot(prod_t, stacked)
    update = update / (1.0 + jnp.exp(-update))
    kinds = lax.broadcasted_iota(jnp.int32, (8, atoms), 0).astype(F32)
    own_state = dot(embed_t.astype(BF16), (kinds == own[3:4]).astype(BF16))
    new_state = (own_state + update).astype(BF16)
    rows = jnp.concatenate(
        [read_ref[...], charge_ref[...], jnp.zeros((14, channels), BF16)], axis=0
    )
    return dot(rows, new_state)


def spline_rows(fraction):
    rest = 1.0 - fraction
    square = fraction * fraction
    cube = square * fraction
    return (
        rest * rest * rest * (1.0 / 6.0),
        (3.0 * cube - 6.0 * square + 4.0) * (1.0 / 6.0),
        (-3.0 * cube + 3.0 * square + 3.0 * fraction + 1.0) * (1.0 / 6.0),
        cube * (1.0 / 6.0),
    )


def stencil_rows(rows, first, weights):
    at = lax.broadcasted_iota(jnp.int32, (rows, first.shape[1]), 0) - first
    out = jnp.where(at == 0, weights[0], 0.0)
    for j in range(1, 4):
        out = jnp.where(at == j, weights[j], out)
    return out


def three_parts(x):
    first = x.astype(BF16).astype(F32)
    second = (x - first).astype(BF16).astype(F32)
    third = (x - first - second).astype(BF16).astype(F32)
    return first, second, third


def at_marks(position, parts):
    out = jnp.where(position == 125, parts[0], 0.0)
    out = jnp.where(position == 126, parts[1], out)
    return jnp.where(position == 127, parts[2], out)


WEIGHTS = ("embed", "win", "wout", "mix", "prod", "read", "charge")


def program_kernel(counts, planes, names, *refs):
    ref = dict(zip(names, refs))
    domain_count, inner_count = counts
    devices = domain_count * inner_count
    per_core = devices // 2
    d, i = lax.axis_index("domain"), lax.axis_index("inner")
    me = d * inner_count + i
    at = (d, i)
    slots, atoms = ref["nbr_in"].shape

    def device(t):
        return (t // inner_count, lax.rem(t, inner_count))

    def owner(r):
        rest = lax.rem(r, per_core)
        return (rest // 2, lax.rem(rest, 2) * 2 + r // per_core)

    my_plane = d * 2 + i // 2 + per_core * lax.rem(i, 2)
    owns = my_plane < PLANES

    def rows16(t):
        return pl.ds(pl.multiple_of(t * 16, 16), 16)

    def lanes128(t):
        return pl.ds(pl.multiple_of(t * 128, 128), 128)

    barrier = pltpu.get_barrier_semaphore()

    def greet(k, carry):
        pl.semaphore_signal(
            barrier, inc=1, device_id=device(lax.rem(me + k, devices)), device_id_type=MESH
        )
        return carry

    lax.fori_loop(1, devices, greet, 0)

    def fetch(n, name):
        source = ref[name + "_in"]
        if name == "gain":
            source = source.at[jnp.minimum(my_plane, PLANES - 1) // 2]
        return pltpu.make_async_copy(source, ref[name], ref["fetch_sem"].at[n])

    fetched = ("cells", "frac", "species", "nbr", "count") + WEIGHTS
    fetched = fetched + ("zeta", "y", "x", "xt", "gain")
    fetches = {name: fetch(n, name) for n, name in enumerate(fetched)}
    for name in fetched:
        fetches[name].start()

    moves = [(dx, dy) for dx in (-1, 0, 1) for dy in (-1, 0, 1) if (dx, dy) != (0, 0)]
    mine, ext = ref["mine"], ref["ext"]
    for name in ("cells", "frac", "species"):
        fetches[name].wait()
    cell = [ref["cells"][c] for c in range(3)]
    fraction = [ref["frac"][c] for c in range(3)]
    mine[...] = jnp.zeros_like(mine)
    for c in range(3):
        mine[c : c + 1, :] = cell[c].astype(F32) + fraction[c]
    mine[3:4, :] = ref["species"][0].astype(F32)
    pl.semaphore_wait(barrier, devices - 1)
    copies = []
    for n, (dx, dy) in enumerate(moves):
        copy = pltpu.make_async_remote_copy(
            src_ref=mine,
            dst_ref=ext.at[(1 - dx) * 3 + (1 - dy)],
            send_sem=ref["ext_send"].at[n],
            recv_sem=ref["ext_recv"].at[n],
            device_id=tuple(
                lax.rem(at[a] + counts[a] + (dx, dy)[a], counts[a]) for a in range(2)
            ),
            device_id_type=MESH,
        )
        copy.start()
        copies.append(copy)
    ext[4] = mine[...]

    weights = [spline_rows(f) for f in fraction]
    sten_x = stencil_rows(16, cell[0] - 1, weights[0])
    rim_x = jnp.where(cell[0] == 0, weights[0][0], 0.0)
    sten_z = stencil_rows(40, cell[2] - 1 - Z_LOW, weights[2])
    lane = lax.broadcasted_iota(jnp.int32, (128, atoms), 0)
    y_main = split(stencil_rows(128, cell[1], weights[1]))
    y_low = split(jnp.where(lane <= 97, stencil_rows(128, cell[1] + 65, weights[1]), 0.0))
    y_high = split(jnp.where(lane >= 65, stencil_rows(128, cell[1] + 32, weights[1]), 0.0))
    for n, part in enumerate(y_main + y_low + y_high):
        ref["sten_y"][n] = part
    fetches["zeta"].wait()
    waves = ref["waves"]
    waves[...] = jnp.dot(ref["zeta"][...], sten_z, precision=lax.Precision.HIGHEST)
    sten = ref["sten_x"]
    sten[...] = sten_x
    product, patch32 = ref["product"], ref["patch32"]

    def y_parts(n):
        return ref["sten_y"][2 * n], ref["sten_y"][2 * n + 1]

    def spread(charged):
        for r in range(PLANES):
            product[16 * r : 16 * r + 16, :] = sten[...] * charged[r : r + 1]
        patch32[...] = dot_split(split(product[...]), y_parts(0), dot_nt)
        rim = split(charged * rim_x)
        low = dot_split(rim, y_parts(1), dot_nt)
        high = dot_split(rim, y_parts(2), dot_nt)
        patch32[pl.ds(0, PLANES, 16), :] = patch32[pl.ds(0, PLANES, 16), :] + low[:PLANES]
        patch32[pl.ds(1, PLANES, 16), :] = patch32[pl.ds(1, PLANES, 16), :] + high[:PLANES]

    def to_owners(patch, received, send_sem, recv_sem):
        def start(k, carry):
            r = lax.rem(my_plane + k, PLANES)

            @pl.when(r != my_plane)
            def _():
                pltpu.make_async_remote_copy(
                    src_ref=patch.at[rows16(r), :],
                    dst_ref=received.at[rows16(d), lanes128(i)],
                    send_sem=send_sem,
                    recv_sem=recv_sem,
                    device_id=owner(r),
                    device_id_type=MESH,
                ).start()

            return carry

        lax.fori_loop(0, PLANES, start, 0)

        @pl.when(owns)
        def _():
            pltpu.make_async_copy(
                patch.at[rows16(my_plane), :], received.at[rows16(d), lanes128(i)], recv_sem
            ).start()

    def wait_bytes(buffer, sem):
        pltpu.make_async_copy(buffer, buffer, sem).wait()

    spread(waves[...])
    ref["ones_patch"][...] = patch32[...].astype(BF16)
    to_owners(ref["ones_patch"], ref["ones"], ref["ones_send"], ref["ones_recv"])

    for name in ("nbr", "count") + WEIGHTS:
        fetches[name].wait()
    for copy in copies:
        copy.wait()
    rows = message_rows(
        planes,
        ext,
        ref["nbr"],
        ref["count"],
        *[ref[name] for name in WEIGHTS],
        *[
            ref[name]
            for name in (
                "placed",
                "found",
                "weight",
                "basis",
                "onehot",
                "radial",
                "state",
                "total",
            )
        ],
    )
    energy, latent = rows[0:1], rows[1:2]

    block_mean = jnp.sum(latent, axis=1, keepdims=True) / atoms
    spread(waves[...] * (latent - block_mean))
    position = lax.broadcasted_iota(jnp.int32, (1, 128), 1)
    marks = at_marks(position, three_parts(block_mean))
    patch32[pl.ds(2, PLANES, 16), :] = patch32[pl.ds(2, PLANES, 16), :] + marks
    ref["patch"][...] = patch32[...].astype(BF16)
    to_owners(ref["patch"], ref["received"], ref["patch_send"], ref["patch_recv"])

    for name in ("y", "x", "xt", "gain"):
        fetches[name].wait()
    answer, back = ref["answer"], ref["back"]

    @pl.when(owns)
    def _():
        grid, coefficient = ref["grid"], ref["coefficient"]
        y_table = split(ref["y"][...])
        x_table = split(ref["x"][...])
        xt_table = split(ref["xt"][...])
        wait_bytes(ref["ones"], ref["ones_recv"])
        wait_bytes(ref["received"], ref["patch_recv"])
        tiles = [slice(t * 128, t * 128 + 128) for t in range(inner_count)]
        means = []
        for t in range(inner_count):
            grid[t] = ref["received"][:, tiles[t]].astype(F32)
            marked = grid[t, pl.ds(2, domain_count, 16), :]
            means.append(
                jnp.sum(jnp.where(position >= 125, marked, 0.0), axis=1, keepdims=True)
            )
        mean = jnp.sum(sum(means), axis=0, keepdims=True) / devices
        for t in range(inner_count):
            coefficient[t] = jnp.broadcast_to(means[t] - mean, (domain_count, 128))
            for b in range(domain_count):
                here = slice(16 * b, 16 * b + 16)
                unit = ref["ones"][here, tiles[t]].astype(F32)
                grid[t, here, :] = grid[t, here, :] + unit * coefficient[t, b : b + 1, :]
        whole = jnp.concatenate([grid[t] for t in range(inner_count)], axis=1)
        along_y = dot_split(split(whole), y_table, dot)
        count_x, full_y = along_y.shape[0], along_y.shape[1] // 3
        row = lax.rem(lax.broadcasted_iota(jnp.int32, (count_x, full_y), 0), 16)
        low_rim = jnp.where(row == 0, along_y[:, full_y : 2 * full_y], 0.0)
        high_rim = jnp.where(row == 1, along_y[:, 2 * full_y :], 0.0)
        lines = (
            along_y[:, :full_y]
            + pltpu.roll(low_rim, count_x - 1, 0)
            + pltpu.roll(high_rim, count_x - 2, 0)
        )
        spectrum = dot_split(x_table, split(lines), dot)
        half = count_x // 2
        top = ref["gain"][0:half, :]
        first_row = lax.broadcasted_iota(jnp.int32, (half, full_y), 0) == 0
        bottom = jnp.where(first_row, ref["gain"][half : half + 1, :], top)
        filtered = jnp.concatenate([spectrum[0:half] * top, spectrum[half:] * bottom], axis=0)
        lines = dot_split(xt_table, split(filtered), dot)
        wide = jnp.concatenate(
            [
                lines,
                jnp.where(row == 0, pltpu.roll(lines, 1, 0), 0.0),
                jnp.where(row == 1, pltpu.roll(lines, 2, 0), 0.0),
            ],
            axis=1,
        )
        values = dot_split(split(wide), y_table, dot_nt)
        spot = lax.rem(lax.broadcasted_iota(jnp.int32, (1, values.shape[1]), 1), 128)
        marks = at_marks(spot, three_parts(mean))
        line = lax.rem(lax.broadcasted_iota(jnp.int32, values.shape, 0), 16)
        answer[...] = jnp.where(line == 2, values + marks, values).astype(BF16)

        def back_start(k, carry):
            t = lax.rem(me + k, devices)
            pltpu.make_async_remote_copy(
                src_ref=answer.at[rows16(t // inner_count), lanes128(lax.rem(t, inner_count))],
                dst_ref=back.at[rows16(my_plane), :],
                send_sem=ref["back_send"],
                recv_sem=ref["back_recv"],
                device_id=device(t),
                device_id_type=MESH,
            ).start()
            return carry

        lax.fori_loop(1, devices, back_start, 0)
        pltpu.make_async_copy(
            answer.at[rows16(d), lanes128(i)], back.at[rows16(my_plane), :], ref["back_recv"]
        ).start()

    wait_bytes(back, ref["back_recv"])
    given = back[...]
    main, low, high = y_parts(0), y_parts(1), y_parts(2)
    product[...] = dot(given, main[0]) + dot(given, main[1])
    back32 = patch32
    back32[...] = given.astype(F32)
    mean = jnp.sum(jnp.where(position >= 125, back32[2:3, :], 0.0), axis=1, keepdims=True)
    at_low = back32[pl.ds(0, PLANES, 16), :].astype(BF16)
    at_high = back32[pl.ds(1, PLANES, 16), :].astype(BF16)
    at_rim = dot(at_low, low[0]) + dot(at_low, low[1])
    at_rim = at_rim + dot(at_high, high[0]) + dot(at_high, high[1])
    gathered = jnp.zeros((8, atoms), F32)
    for r in range(PLANES):
        piece = (
            product[16 * r : 16 * r + 8, :] * sten[0:8]
            + product[16 * r + 8 : 16 * r + 16, :] * sten[8:16]
        )
        gathered = gathered + piece * waves[r : r + 1]
    value = jnp.sum(gathered, axis=0, keepdims=True) + rim_x * jnp.sum(
        at_rim * waves[:PLANES], axis=0, keepdims=True
    )
    ref["potential_out"][...] = value
    ref["energy_out"][...] = energy + 0.5 * (latent - mean) * value

    sent = ref["sent"]
    for sem in (ref["ones_send"], ref["patch_send"]):

        @pl.when(owns)
        def _():
            wait_bytes(sent.at[0 : (PLANES - 1) * 16], sem)

        @pl.when(jnp.logical_not(owns))
        def _():
            wait_bytes(sent.at[0 : PLANES * 16], sem)

    @pl.when(owns)
    def _():
        wait_bytes(sent.at[0 : (devices - 1) * 16], ref["back_send"])


def local(
    counts,
    atom_cells,
    atom_frac,
    species,
    nbr_index,
    nbr_count,
    embed,
    radial_in,
    radial_out,
    mix_weight,
    product_weight,
    read_weight,
    charge_weight,
):
    planes = (16, 64)
    devices = counts[0] * counts[1]
    tables = host_tables(*counts, *planes, 256)
    operands = dict(
        cells=atom_cells.transpose(2, 0, 1, 3)[:, 0],
        frac=atom_frac.transpose(2, 0, 1, 3)[:, 0],
        species=species,
        nbr=nbr_index[0, 0].T,
        count=nbr_count[0],
        embed=embed,
        win=radial_in[0],
        wout=radial_out[0],
        mix=mix_weight[0],
        prod=product_weight[0],
        read=read_weight,
        charge=charge_weight[None],
        **{name: jnp.asarray(tables[name]) for name in ("zeta", "y", "x", "xt", "gain")},
    )
    slots, atoms = operands["nbr"].shape
    channels = embed.shape[1]
    octets = slots // 8
    full_x, full_y, lanes = counts[0] * planes[0], counts[1] * planes[1], counts[1] * 128
    dma = pltpu.SemaphoreType.DMA
    scratch = {
        name: VMEM(value.shape[1:] if name == "gain" else value.shape, value.dtype)
        for name, value in operands.items()
    }
    scratch.update(
        mine=VMEM((8, atoms), F32),
        ext=VMEM((9, 8, atoms), F32),
        placed=VMEM((9, 8, atoms), F32),
        found=VMEM((4, slots, atoms), F32),
        weight=VMEM((9, octets, 8, atoms), F32),
        basis=VMEM((octets, 64, atoms), F32),
        onehot=VMEM((octets, 64, atoms), F32),
        radial=VMEM((8, 3 * channels, atoms), F32),
        state=VMEM((8 * channels, atoms), F32),
        total=VMEM((9, channels, atoms), F32),
        sten_x=VMEM((16, atoms), F32),
        sten_y=VMEM((6, 128, atoms), BF16),
        waves=VMEM((72, atoms), F32),
        product=VMEM((PLANES * 16, atoms), F32),
        patch32=VMEM((PLANES * 16, 128), F32),
        ones_patch=VMEM((PLANES * 16, 128), BF16),
        patch=VMEM((PLANES * 16, 128), BF16),
        ones=VMEM((full_x, lanes), BF16),
        received=VMEM((full_x, lanes), BF16),
        grid=VMEM((counts[1], full_x, 128), F32),
        coefficient=VMEM((counts[1], counts[0], 128), F32),
        answer=VMEM((full_x, lanes), BF16),
        back=VMEM((PLANES * 16, 128), BF16),
        sent=VMEM(((devices - 1) * 16, 128), BF16),
        fetch_sem=dma((len(operands),)),
        ext_send=dma((8,)),
        ext_recv=dma((8,)),
        ones_send=dma,
        ones_recv=dma,
        patch_send=dma,
        patch_recv=dma,
        back_send=dma,
        back_recv=dma,
    )
    names = [name + "_in" for name in operands] + ["energy_out", "potential_out"] + list(scratch)
    vmem = pl.BlockSpec(memory_space=VMEM)
    energy, potential = pl.pallas_call(
        functools.partial(program_kernel, counts, planes, names),
        out_shape=[jax.ShapeDtypeStruct((1, atoms), F32)] * 2,
        in_specs=[pl.BlockSpec(memory_space=pl.ANY)] * len(operands),
        out_specs=[vmem] * 2,
        scratch_shapes=list(scratch.values()),
        compiler_params=pltpu.CompilerParams(
            collective_id=0, has_side_effects=True, vmem_limit_bytes=58 << 20
        ),
        name="potential",
    )(*operands.values())
    return (energy[None], potential[None])


def solution(mesh):
    counts = (mesh.shape["domain"], mesh.shape["inner"])
    in_specs = (
        P("domain", "inner", None, None),
        P("domain", "inner", None, None),
        P("domain", "inner", None),
        P("domain", "inner", None, None),
        P("domain", "inner", None),
        P(),
        P(),
        P(),
        P(),
        P(),
        P(),
        P(),
    )
    out_specs = (P("domain", "inner", None), P("domain", "inner", None))
    return jax.shard_map(
        functools.partial(local, counts),
        mesh=mesh,
        in_specs=in_specs,
        out_specs=out_specs,
        check_vma=False,
    )
```

```python
import functools
import math

import jax
import jax.numpy as jnp
import numpy as np
from jax import lax
from jax.experimental import pallas as pl
from jax.experimental.pallas import tpu as pltpu
from jax.sharding import PartitionSpec as P

MESH = pl.DeviceIdType.MESH
VMEM = pltpu.VMEM
F32 = jnp.float32
BF16 = jnp.bfloat16

spacing = 0.55
cutoff = 5.0
smearing = 0.2
coulomb = 14.399645
neighbour_scale = 0.25

Z_LOW = 111
Z_SPAN = 33
PLANES = 2 * Z_SPAN
ROW_LOW = 504 // 128
ROW_HIGH = 4103 // 128

DEGREE = (0, 1, 1, 1, 2, 2, 2, 2, 2)


def dot(a, b):
    return lax.dot_general(a, b, (((1,), (0,)), ((), ())), preferred_element_type=F32)


def dot_nt(a, b):
    return lax.dot_general(a, b, (((1,), (1,)), ((), ())), preferred_element_type=F32)


def split(x):
    high = x.astype(BF16)
    return high, (x - high.astype(F32)).astype(BF16)


def dot_split(a, b, form):
    return form(a[0], b[0]) + (form(a[0], b[1]) + form(a[1], b[0]))


def three_parts(x):
    first = x.astype(BF16).astype(F32)
    second = (x - first).astype(BF16).astype(F32)
    third = (x - first - second).astype(BF16).astype(F32)
    return first, second, third


def basis_rows(length, positions):
    half = length // 2
    k = np.arange(half)
    angle = 2.0 * np.pi * ((k[:, None] * positions[None, :]) % length) / length
    cosine = np.cos(angle)
    sine = np.sin(angle)
    sine[0] = np.cos(np.pi * positions)
    return np.concatenate([cosine, sine], axis=0)


@functools.lru_cache(maxsize=None)
def host_tables(domain_count, inner_count, planes_x, planes_y, depth):
    full_x = planes_x * domain_count
    full_y = planes_y * inner_count
    table_x = basis_rows(full_x, np.arange(full_x))
    table_y = np.zeros((inner_count, 128, 3, full_y))
    for i in range(inner_count):
        all_y = basis_rows(full_y, (planes_y * i - 1 + np.arange(planes_y + 1)) % full_y).T
        table_y[i, : planes_y + 1, 0] = all_y
        table_y[i, 65:98, 1] = all_y[:33]
        table_y[i, 65:97, 2] = all_y[33:]
    table_y = table_y.transpose(2, 0, 1, 3).reshape(3, inner_count * 128, full_y)

    def squared_freq(length, count):
        return (np.arange(count) / (length * spacing)) ** 2

    def modulus(length, count):
        return (2.0 + np.cos(2.0 * np.pi * np.arange(count) / length)) ** 2 / 9.0

    def twice(length, count):
        k = np.arange(count)
        return np.where((k == 0) | (k == length // 2), 1.0, 2.0)

    cx, cy, cz = full_x // 2 + 1, full_y // 2 + 1, depth // 2 + 1
    squared = (
        squared_freq(full_x, cx)[:, None, None]
        + squared_freq(full_y, cy)[None, :, None]
        + squared_freq(depth, cz)[None, None, :]
    )
    safe = np.where(squared > 0.0, squared, 1.0)
    moduli = (
        modulus(full_x, cx)[:, None, None]
        * modulus(full_y, cy)[None, :, None]
        * modulus(depth, cz)[None, None, :]
    )
    volume = full_x * full_y * depth * spacing**3
    kernel = (
        coulomb
        * np.exp(-2.0 * np.pi**2 * smearing**2 * squared)
        / (np.pi * volume * safe * moduli)
    )
    kernel = np.where(squared > 0.0, kernel, 0.0)
    kernel = kernel * twice(full_x, cx)[:, None, None] * twice(full_y, cy)[None, :, None]
    step = np.arange(Z_SPAN)
    along = np.cos(2.0 * np.pi * np.arange(cz)[:, None] * step[None, :] / depth)
    along = along * twice(depth, cz)[:, None]
    wave = np.cos(np.pi * (2 * np.arange(Z_SPAN)[None, :] + 1) * step[:, None] / (2 * Z_SPAN))
    wave = wave * np.where(step == 0, 1.0, 2.0)[:, None] / Z_SPAN
    gain = np.moveaxis(kernel @ (along @ wave), 2, 0)
    order_y = np.concatenate([np.arange(full_y // 2), [full_y // 2], np.arange(1, full_y // 2)])
    gain = gain[:, :, order_y]
    half = full_x // 2
    padded = np.zeros((Z_SPAN, half + 8, full_y), np.float32)
    padded[:, :half] = gain[:, :half]
    padded[:, half] = gain[:, half]
    plane = np.arange(PLANES)
    angle = (
        np.pi * (2 * (plane // 2)[:, None] + 1) * np.arange(40)[None, :] / (2 * Z_SPAN)
    )
    zeta = np.where(plane[:, None] % 2 == 0, np.cos(angle), np.sin(angle))
    zeta[:, Z_SPAN:] = 0.0
    zeta_full = np.zeros((72, 40), np.float32)
    zeta_full[:PLANES] = zeta
    return dict(
        x=table_x.astype(np.float32),
        xt=np.ascontiguousarray(table_x.T).astype(np.float32),
        y=table_y.astype(np.float32),
        gain=padded,
        zeta=zeta_full,
    )


def half_tanh_silu(x):
    half = 0.5 * x
    return half + half * jnp.tanh(half)


def shuffle_matrix(atoms):
    row = lax.broadcasted_iota(jnp.int32, (atoms, atoms), 0)
    column = lax.broadcasted_iota(jnp.int32, (atoms, atoms), 1)
    return (column == row // 8 + (row % 8) * (atoms // 8)).astype(F32).astype(BF16)


def message_weights(species, embed_ref, win_ref, wout_ref, win_wide, pair, shuffle, own_state):
    kinds, channels = embed_ref.shape
    inputs, hidden = win_ref.shape
    atoms = species.shape[1]
    spread_in = (
        lax.broadcasted_iota(jnp.int32, (8, 64), 1) // 8
        == lax.broadcasted_iota(jnp.int32, (8, 64), 0)
    ).astype(F32).astype(BF16)
    wide = dot(win_ref[...].astype(F32).T.astype(BF16), spread_in)
    full = jnp.concatenate([wide] * 8, axis=0)
    row = lax.broadcasted_iota(jnp.int32, full.shape, 0) // hidden
    column = lax.broadcasted_iota(jnp.int32, full.shape, 1) % 8
    win_wide[...] = jnp.where(row == column, full, 0.0).astype(BF16)
    embed = embed_ref[...].astype(F32)
    out = wout_ref[...].astype(F32)
    for degree in range(3):
        part = out[:, degree * channels : (degree + 1) * channels]
        for s in range(kinds):
            pair[degree, s * hidden : (s + 1) * hidden, :] = (part * embed[s : s + 1]).astype(BF16)
    shuffle[...] = shuffle_matrix(atoms)
    kind = lax.broadcasted_iota(jnp.int32, (128, atoms), 0)
    marks = (kind == species).astype(F32).T.astype(BF16)
    padded = jnp.concatenate([embed, jnp.zeros((128 - kinds, channels), F32)], axis=0)
    own_state[...] = dot(shuffle[...], dot(marks, padded.astype(BF16)).astype(BF16))


def message_rows(
    planes,
    ext_ref,
    nbr_ref,
    count_ref,
    mix_ref,
    prod_ref,
    read_ref,
    charge_ref,
    win_wide,
    pair,
    shuffle,
    own_state,
    placed,
    found,
    weight,
    basis,
    kinds,
    moments,
):
    atoms = ext_ref.shape[-1]
    slots = nbr_ref.shape[0]
    tiles = atoms // 128
    channels = mix_ref.shape[-1]
    hidden_size = pair.shape[1] // 8
    for b in range(9):
        row = lax.broadcasted_iota(jnp.int32, (8, atoms), 0)
        shift = jnp.where(
            row == 0, planes[0] * (b // 3 - 1.0), jnp.where(row == 1, planes[1] * (b % 3 - 1.0), 0.0)
        )
        placed[b] = ext_ref[b] + shift

    def gather(t, carry):
        rows = pl.ds(pl.multiple_of((t // tiles) * 8, 8), 8)
        lanes = pl.ds(pl.multiple_of((t % tiles) * 128, 128), 128)
        index = nbr_ref[rows, lanes]
        low = index & 127
        high = index >> 7
        values = [jnp.zeros((8, 128), F32) for _ in range(4)]
        for r in range(ROW_LOW, ROW_HIGH + 1):
            here = high == r
            piece = slice((r % tiles) * 128, (r % tiles) * 128 + 128)
            for c in range(4):
                line = jnp.broadcast_to(placed[r // tiles, c : c + 1, piece], (8, 128))
                picked = jnp.take_along_axis(line, low, axis=1)
                values[c] = jnp.where(here, picked, values[c])
        into = pl.ds(pl.multiple_of((t % tiles) * slots + (t // tiles) * 8, 8), 8)
        for c in range(4):
            found[c, into, :] = values[c]
        return carry

    lax.fori_loop(0, (slots // 8) * tiles, gather, 0)

    own = ext_ref[4]
    slot = lax.broadcasted_iota(jnp.int32, (slots, 128), 0)
    parts = []
    for c in range(4):
        pieces = []
        for j in range(tiles):
            lanes = slice(j * 128, j * 128 + 128)
            value = found[c, slots * j : slots * j + slots, :]
            if c < 3:
                value = (value - own[c : c + 1, lanes]) * spacing
            else:
                value = jnp.where(slot < count_ref[0:1, lanes], value, 8.0)
            pieces.append(value)
        parts.append(jnp.concatenate(pieces, axis=0).T)
    dx, dy, dz, species = parts
    distance = jnp.sqrt(dx * dx + dy * dy + dz * dz)
    inverse = 1.0 / distance
    ux, uy, uz = dx * inverse, dy * inverse, dz * inverse
    scaled = distance * (1.0 / cutoff)
    scaled_sq = scaled * scaled
    six = scaled_sq * scaled_sq * scaled_sq
    envelope = 1.0 - 28.0 * six + 48.0 * six * scaled - 21.0 * six * scaled_sq
    envelope = jnp.where(scaled < 1.0, envelope * neighbour_scale, 0.0)
    r3, r5, r15 = math.sqrt(3.0), math.sqrt(5.0), math.sqrt(15.0)
    factors = (
        None,
        r3 * ux,
        r3 * uy,
        r3 * uz,
        r15 * ux * uy,
        r15 * uy * uz,
        0.5 * r5 * (3.0 * uz * uz - 1.0),
        r15 * ux * uz,
        0.5 * r15 * (ux * ux - uy * uy),
    )
    octets = 8

    def put(target, first, value):
        for o in range(octets):
            target[o, first : first + 8, 0:128] = value[8 * o : 8 * o + 8]
            target[o, first : first + 8, 128:256] = value[64 + 8 * o : 64 + 8 * o + 8]

    for m, factor in enumerate(factors):
        put(weight, 8 * m, envelope if factor is None else envelope * factor)
    put(kinds, 0, species)
    theta = (math.pi / cutoff) * distance
    sine = jnp.sin(theta)
    cosine = 2.0 * jnp.cos(theta)
    scale = math.sqrt(2.0 / cutoff) * inverse
    before = jnp.zeros_like(sine)
    for n in range(8):
        put(basis, 8 * n, scale * sine)
        sine, before = cosine * sine - before, sine

    lane = lax.broadcasted_iota(jnp.int32, (8, 256), 1)
    element = lax.broadcasted_iota(jnp.int32, (8, 256), 0)
    mine = ((lane % 128) // slots) * 2 + lane // 128 == element

    def octet(o, carry):
        hidden = dot(win_wide[...], basis[o].astype(BF16))
        hidden = half_tanh_silu(hidden).astype(BF16)
        for first in range(0, 8, 2):
            sums = []
            for i in (first, first + 1):
                near = hidden[i * hidden_size : (i + 1) * hidden_size]
                kind = kinds[o, i : i + 1, :]
                by_kind = []
                for s in range(8):
                    mark = jnp.broadcast_to((kind == float(s)).astype(F32), (hidden_size, 256))
                    by_kind.append(near * mark.astype(BF16))
                left = [
                    jnp.where(mine, jnp.broadcast_to(weight[o, 8 * m + i : 8 * m + i + 1, :], (8, 256)), 0.0)
                    for m in range(9)
                ]
                left = jnp.concatenate(left, axis=0).astype(BF16)
                sums.append(dot_nt(left, jnp.concatenate(by_kind, axis=0)))
            into = pl.ds(pl.multiple_of(64 * o + 8 * first, 16), 16)
            for m in range(9):
                both = jnp.concatenate([part[8 * m : 8 * m + 8] for part in sums], axis=0)
                moments[m, into, :] = both.astype(BF16)
        return carry

    lax.fori_loop(0, octets, octet, 0)

    invariants = [None, None, None]
    for m in range(9):
        degree = DEGREE[m]
        aggregate = dot(moments[m], pair[degree]).astype(BF16)
        mixed = dot(aggregate, mix_ref[degree])
        if degree == 0:
            invariants[0] = mixed
        elif invariants[degree] is None:
            invariants[degree] = mixed * mixed
        else:
            invariants[degree] = invariants[degree] + mixed * mixed
    stacked = jnp.concatenate(invariants, axis=1).astype(BF16)
    update = dot(stacked, prod_ref[...])
    update = update / (1.0 + jnp.exp(-update))
    new_state = (own_state[...] + update).astype(BF16)
    readout = jnp.concatenate(
        [read_ref[...], charge_ref[...], jnp.zeros((14, channels), BF16)], axis=0
    )
    shuffled = dot_nt(readout, new_state)[0:2]
    stack = jnp.concatenate(three_parts(shuffled) + (jnp.zeros((10, atoms), F32),), axis=0)
    ordered = dot(stack.astype(BF16), shuffle[...])
    return ordered[0:2] + ordered[2:4] + ordered[4:6]


def spline_rows(fraction):
    rest = 1.0 - fraction
    square = fraction * fraction
    cube = square * fraction
    return (
        rest * rest * rest * (1.0 / 6.0),
        (3.0 * cube - 6.0 * square + 4.0) * (1.0 / 6.0),
        (-3.0 * cube + 3.0 * square + 3.0 * fraction + 1.0) * (1.0 / 6.0),
        cube * (1.0 / 6.0),
    )


def stencil_rows(rows, first, weights):
    at = lax.broadcasted_iota(jnp.int32, (rows, first.shape[1]), 0) - first
    out = jnp.where(at == 0, weights[0], 0.0)
    for j in range(1, 4):
        out = jnp.where(at == j, weights[j], out)
    return out


def at_marks(position, parts):
    out = jnp.where(position == 125, parts[0], 0.0)
    out = jnp.where(position == 126, parts[1], out)
    return jnp.where(position == 127, parts[2], out)


WEIGHTS = ("embed", "win", "wout", "mix", "prod", "read", "charge")


def program_kernel(counts, planes, names, *refs):
    ref = dict(zip(names, refs))
    domain_count, inner_count = counts
    devices = domain_count * inner_count
    per_core = devices // 2
    d, i = lax.axis_index("domain"), lax.axis_index("inner")
    me = d * inner_count + i
    at = (d, i)
    slots, atoms = ref["nbr_in"].shape

    def device(t):
        return (t // inner_count, lax.rem(t, inner_count))

    def owner(r):
        rest = lax.rem(r, per_core)
        return (rest // 2, lax.rem(rest, 2) * 2 + r // per_core)

    my_plane = d * 2 + i // 2 + per_core * lax.rem(i, 2)
    owns = my_plane < PLANES

    def rows16(t):
        return pl.ds(pl.multiple_of(t * 16, 16), 16)

    def lanes128(t):
        return pl.ds(pl.multiple_of(t * 128, 128), 128)

    barrier = pltpu.get_barrier_semaphore()

    def greet(k, carry):
        pl.semaphore_signal(
            barrier, inc=1, device_id=device(lax.rem(me + k, devices)), device_id_type=MESH
        )
        return carry

    lax.fori_loop(1, devices, greet, 0)

    def fetch(n, name):
        source = ref[name + "_in"]
        if name == "gain":
            source = source.at[jnp.minimum(my_plane, PLANES - 1) // 2]
        return pltpu.make_async_copy(source, ref[name], ref["fetch_sem"].at[n])

    fetched = ("cells", "frac", "species", "nbr", "count") + WEIGHTS
    fetched = fetched + ("zeta", "y", "x", "xt", "gain")
    fetches = {name: fetch(n, name) for n, name in enumerate(fetched)}
    for name in fetched:
        fetches[name].start()

    moves = [(dx, dy) for dx in (-1, 0, 1) for dy in (-1, 0, 1) if (dx, dy) != (0, 0)]
    mine, ext = ref["mine"], ref["ext"]
    for name in ("cells", "frac", "species"):
        fetches[name].wait()
    cell = [ref["cells"][c] for c in range(3)]
    fraction = [ref["frac"][c] for c in range(3)]
    mine[...] = jnp.zeros_like(mine)
    for c in range(3):
        mine[c : c + 1, :] = cell[c].astype(F32) + fraction[c]
    mine[3:4, :] = ref["species"][0].astype(F32)
    ext[4] = mine[...]

    weights = [spline_rows(f) for f in fraction]
    sten_x = stencil_rows(16, cell[0] - 1, weights[0])
    rim_x = jnp.where(cell[0] == 0, weights[0][0], 0.0)
    sten_z = stencil_rows(40, cell[2] - 1 - Z_LOW, weights[2])
    lane = lax.broadcasted_iota(jnp.int32, (128, atoms), 0)
    y_main = split(stencil_rows(128, cell[1], weights[1]))
    y_low = split(jnp.where(lane <= 97, stencil_rows(128, cell[1] + 65, weights[1]), 0.0))
    y_high = split(jnp.where(lane >= 65, stencil_rows(128, cell[1] + 32, weights[1]), 0.0))
    for n, part in enumerate(y_main + y_low + y_high):
        ref["sten_y"][n] = part
    fetches["zeta"].wait()
    waves = ref["waves"]
    waves[...] = jnp.dot(ref["zeta"][...], sten_z, precision=lax.Precision.HIGHEST)
    sten = ref["sten_x"]
    sten[...] = sten_x
    product, patch32 = ref["product"], ref["patch32"]

    def y_parts(n):
        return ref["sten_y"][2 * n], ref["sten_y"][2 * n + 1]

    def spread(charged):
        for r in range(PLANES):
            product[16 * r : 16 * r + 16, :] = sten[...] * charged[r : r + 1]
        patch32[...] = dot_split(split(product[...]), y_parts(0), dot_nt)
        rim = split(charged * rim_x)
        low = dot_split(rim, y_parts(1), dot_nt)
        high = dot_split(rim, y_parts(2), dot_nt)
        patch32[pl.ds(0, PLANES, 16), :] = patch32[pl.ds(0, PLANES, 16), :] + low[:PLANES]
        patch32[pl.ds(1, PLANES, 16), :] = patch32[pl.ds(1, PLANES, 16), :] + high[:PLANES]

    def to_owners(patch, received, send_sem, recv_sem):
        def start(k, carry):
            r = lax.rem(my_plane + k, PLANES)

            @pl.when(r != my_plane)
            def _():
                pltpu.make_async_remote_copy(
                    src_ref=patch.at[rows16(r), :],
                    dst_ref=received.at[rows16(d), lanes128(i)],
                    send_sem=send_sem,
                    recv_sem=recv_sem,
                    device_id=owner(r),
                    device_id_type=MESH,
                ).start()

            return carry

        lax.fori_loop(0, PLANES, start, 0)

        @pl.when(owns)
        def _():
            pltpu.make_async_copy(
                patch.at[rows16(my_plane), :], received.at[rows16(d), lanes128(i)], recv_sem
            ).start()

    def wait_bytes(buffer, sem):
        pltpu.make_async_copy(buffer, buffer, sem).wait()

    spread(waves[...])
    ref["ones_patch"][...] = patch32[...].astype(BF16)
    for name, source in (("x", "x"), ("xt", "xt"), ("y", "y")):
        fetches[source].wait()
        for n, part in enumerate(split(ref[source][...])):
            ref[name + "_parts"][n] = part

    for name in ("nbr", "count") + WEIGHTS:
        fetches[name].wait()
    message_weights(
        ref["species"][0],
        *[ref[name] for name in ("embed", "win", "wout", "win_wide", "pair", "shuffle", "own_state")],
    )

    pl.semaphore_wait(barrier, devices - 1)
    copies = []
    for n, (dx, dy) in enumerate(moves):
        copy = pltpu.make_async_remote_copy(
            src_ref=mine,
            dst_ref=ext.at[(1 - dx) * 3 + (1 - dy)],
            send_sem=ref["ext_send"].at[n],
            recv_sem=ref["ext_recv"].at[n],
            device_id=tuple(
                lax.rem(at[a] + counts[a] + (dx, dy)[a], counts[a]) for a in range(2)
            ),
            device_id_type=MESH,
        )
        copy.start()
        copies.append(copy)
    to_owners(ref["ones_patch"], ref["ones"], ref["ones_send"], ref["ones_recv"])

    for copy in copies:
        copy.wait()
    rows = message_rows(
        planes,
        ext,
        *[
            ref[name]
            for name in (
                "nbr",
                "count",
                "mix",
                "prod",
                "read",
                "charge",
                "win_wide",
                "pair",
                "shuffle",
                "own_state",
                "placed",
                "found",
                "weight",
                "basis",
                "kinds",
                "moments",
            )
        ],
    )
    energy, latent = rows[0:1], rows[1:2]

    block_mean = jnp.sum(latent, axis=1, keepdims=True) / atoms
    spread(waves[...] * (latent - block_mean))
    position = lax.broadcasted_iota(jnp.int32, (1, 128), 1)
    marks = at_marks(position, three_parts(block_mean))
    patch32[pl.ds(2, PLANES, 16), :] = patch32[pl.ds(2, PLANES, 16), :] + marks
    ref["patch"][...] = patch32[...].astype(BF16)
    to_owners(ref["patch"], ref["received"], ref["patch_send"], ref["patch_recv"])

    fetches["gain"].wait()
    answer, back = ref["answer"], ref["back"]

    @pl.when(owns)
    def _():
        grid, coefficient = ref["grid"], ref["coefficient"]
        x_table = ref["x_parts"][0], ref["x_parts"][1]
        xt_table = ref["xt_parts"][0], ref["xt_parts"][1]

        def y_table(part):
            return ref["y_parts"][0, part], ref["y_parts"][1, part]

        def whole_rows(rows):
            return jnp.concatenate([grid[t, rows, :] for t in range(inner_count)], axis=1)

        def every16(first):
            return pl.ds(first, domain_count, 16)

        wait_bytes(ref["ones"], ref["ones_recv"])
        wait_bytes(ref["received"], ref["patch_recv"])
        tiles = [slice(t * 128, t * 128 + 128) for t in range(inner_count)]
        means = []
        for t in range(inner_count):
            grid[t] = ref["received"][:, tiles[t]].astype(F32)
            marked = grid[t, pl.ds(2, domain_count, 16), :]
            means.append(
                jnp.sum(jnp.where(position >= 125, marked, 0.0), axis=1, keepdims=True)
            )
        mean = jnp.sum(sum(means), axis=0, keepdims=True) / devices
        for t in range(inner_count):
            coefficient[t] = jnp.broadcast_to(means[t] - mean, (domain_count, 128))
            for b in range(domain_count):
                here = slice(16 * b, 16 * b + 16)
                unit = ref["ones"][here, tiles[t]].astype(F32)
                grid[t, here, :] = grid[t, here, :] + unit * coefficient[t, b : b + 1, :]
        along_y = dot_split(split(whole_rows(slice(None))), y_table(0), dot)
        rim = dot_split(split(whole_rows(every16(0))), y_table(1), dot)
        rim = rim + dot_split(split(whole_rows(every16(1))), y_table(2), dot)
        rim = pltpu.roll(rim, domain_count - 1, 0)
        lines_ref = ref["lines"]
        full_y = along_y.shape[1]
        columns = [slice(t * 128, t * 128 + 128) for t in range(full_y // 128)]
        for t, column in enumerate(columns):
            lines_ref[t] = along_y[:, column]
            lines_ref[t, every16(15), :] = lines_ref[t, every16(15), :] + rim[:, column]
        lines = jnp.concatenate([lines_ref[t] for t in range(len(columns))], axis=1)
        spectrum = dot_split(x_table, split(lines), dot)
        half = lines.shape[0] // 2
        top = ref["gain"][0:half, :]
        first_row = lax.broadcasted_iota(jnp.int32, (half, full_y), 0) == 0
        bottom = jnp.where(first_row, ref["gain"][half : half + 1, :], top)
        filtered = jnp.concatenate([spectrum[0:half] * top, spectrum[half:] * bottom], axis=0)
        lines = dot_split(xt_table, split(filtered), dot)
        for t, column in enumerate(columns):
            lines_ref[t] = lines[:, column]
        rim = jnp.concatenate(
            [lines_ref[t, every16(15), :] for t in range(len(columns))], axis=1
        )
        rim = split(pltpu.roll(rim, 1, 0))
        values = dot_split(split(lines), y_table(0), dot_nt)
        low_rim = dot_split(rim, y_table(1), dot_nt)
        high_rim = dot_split(rim, y_table(2), dot_nt)
        marks = at_marks(position, three_parts(mean))
        for t in range(inner_count):
            grid[t] = values[:, tiles[t]]
            grid[t, every16(0), :] = grid[t, every16(0), :] + low_rim[:, tiles[t]]
            grid[t, every16(1), :] = grid[t, every16(1), :] + high_rim[:, tiles[t]]
            grid[t, every16(2), :] = grid[t, every16(2), :] + marks
            answer[:, tiles[t]] = grid[t].astype(BF16)

        def back_start(k, carry):
            t = lax.rem(me + k, devices)
            pltpu.make_async_remote_copy(
                src_ref=answer.at[rows16(t // inner_count), lanes128(lax.rem(t, inner_count))],
                dst_ref=back.at[rows16(my_plane), :],
                send_sem=ref["back_send"],
                recv_sem=ref["back_recv"],
                device_id=device(t),
                device_id_type=MESH,
            ).start()
            return carry

        lax.fori_loop(1, devices, back_start, 0)
        pltpu.make_async_copy(
            answer.at[rows16(d), lanes128(i)], back.at[rows16(my_plane), :], ref["back_recv"]
        ).start()

    wait_bytes(back, ref["back_recv"])
    given = back[...]
    main, low, high = y_parts(0), y_parts(1), y_parts(2)
    product[...] = dot(given, main[0]) + dot(given, main[1])
    back32 = patch32
    back32[...] = given.astype(F32)
    mean = jnp.sum(jnp.where(position >= 125, back32[2:3, :], 0.0), axis=1, keepdims=True)
    at_low = back32[pl.ds(0, PLANES, 16), :].astype(BF16)
    at_high = back32[pl.ds(1, PLANES, 16), :].astype(BF16)
    at_rim = dot(at_low, low[0]) + dot(at_low, low[1])
    at_rim = at_rim + dot(at_high, high[0]) + dot(at_high, high[1])
    gathered = jnp.zeros((8, atoms), F32)
    for r in range(PLANES):
        piece = (
            product[16 * r : 16 * r + 8, :] * sten[0:8]
            + product[16 * r + 8 : 16 * r + 16, :] * sten[8:16]
        )
        gathered = gathered + piece * waves[r : r + 1]
    value = jnp.sum(gathered, axis=0, keepdims=True) + rim_x * jnp.sum(
        at_rim * waves[:PLANES], axis=0, keepdims=True
    )
    ref["out"][0:1] = energy + 0.5 * (latent - mean) * value
    ref["out"][1:2] = value

    sent = ref["sent"]
    for sem in (ref["ones_send"], ref["patch_send"]):

        @pl.when(owns)
        def _():
            wait_bytes(sent.at[0 : (PLANES - 1) * 16], sem)

        @pl.when(jnp.logical_not(owns))
        def _():
            wait_bytes(sent.at[0 : PLANES * 16], sem)

    @pl.when(owns)
    def _():
        wait_bytes(sent.at[0 : (devices - 1) * 16], ref["back_send"])


def part_kernel(both_ref, energy_ref, potential_ref):
    energy_ref[0] = both_ref[0:1, :]
    potential_ref[0] = both_ref[1:2, :]


def local(
    counts,
    atom_cells,
    atom_frac,
    species,
    nbr_index,
    nbr_count,
    embed,
    radial_in,
    radial_out,
    mix_weight,
    product_weight,
    read_weight,
    charge_weight,
):
    planes = (16, 64)
    devices = counts[0] * counts[1]
    tables = host_tables(*counts, *planes, 256)
    operands = dict(
        cells=atom_cells.transpose(2, 0, 1, 3)[:, 0],
        frac=atom_frac.transpose(2, 0, 1, 3)[:, 0],
        species=species,
        nbr=nbr_index[0, 0].T,
        count=nbr_count[0],
        embed=embed,
        win=radial_in[0],
        wout=radial_out[0],
        mix=mix_weight[0],
        prod=product_weight[0],
        read=read_weight,
        charge=charge_weight[None],
        **{name: jnp.asarray(tables[name]) for name in ("zeta", "y", "x", "xt", "gain")},
    )
    slots, atoms = operands["nbr"].shape
    channels = embed.shape[1]
    hidden = radial_in.shape[-1]
    full_x, full_y, lanes = counts[0] * planes[0], counts[1] * planes[1], counts[1] * 128
    dma = pltpu.SemaphoreType.DMA
    scratch = {
        name: VMEM(value.shape[1:] if name == "gain" else value.shape, value.dtype)
        for name, value in operands.items()
    }
    scratch.update(
        mine=VMEM((8, atoms), F32),
        ext=VMEM((9, 8, atoms), F32),
        placed=VMEM((9, 8, atoms), F32),
        found=VMEM((4, atoms // 128 * slots, 128), F32),
        weight=VMEM((8, 72, 256), F32),
        basis=VMEM((8, 64, 256), F32),
        kinds=VMEM((8, 8, 256), F32),
        moments=VMEM((9, atoms, 8 * hidden), BF16),
        win_wide=VMEM((8 * hidden, 64), BF16),
        pair=VMEM((3, 8 * hidden, channels), BF16),
        shuffle=VMEM((atoms, atoms), BF16),
        own_state=VMEM((atoms, channels), F32),
        sten_x=VMEM((16, atoms), F32),
        sten_y=VMEM((6, 128, atoms), BF16),
        waves=VMEM((72, atoms), F32),
        product=VMEM((PLANES * 16, atoms), F32),
        patch32=VMEM((PLANES * 16, 128), F32),
        ones_patch=VMEM((PLANES * 16, 128), BF16),
        patch=VMEM((PLANES * 16, 128), BF16),
        ones=VMEM((full_x, lanes), BF16),
        received=VMEM((full_x, lanes), BF16),
        grid=VMEM((counts[1], full_x, 128), F32),
        coefficient=VMEM((counts[1], counts[0], 128), F32),
        lines=VMEM((full_y // 128, full_x, 128), F32),
        x_parts=VMEM((2, full_x, full_x), BF16),
        xt_parts=VMEM((2, full_x, full_x), BF16),
        y_parts=VMEM((2, 3, lanes, full_y), BF16),
        answer=VMEM((full_x, lanes), BF16),
        back=VMEM((PLANES * 16, 128), BF16),
        sent=VMEM(((devices - 1) * 16, 128), BF16),
        fetch_sem=dma((len(operands),)),
        ext_send=dma((8,)),
        ext_recv=dma((8,)),
        ones_send=dma,
        ones_recv=dma,
        patch_send=dma,
        patch_recv=dma,
        back_send=dma,
        back_recv=dma,
    )
    names = [name + "_in" for name in operands] + ["out"] + list(scratch)
    vmem = pl.BlockSpec(memory_space=VMEM)
    both = pl.pallas_call(
        functools.partial(program_kernel, counts, planes, names),
        out_shape=jax.ShapeDtypeStruct((2, atoms), F32),
        in_specs=[pl.BlockSpec(memory_space=pl.ANY)] * len(operands),
        out_specs=vmem,
        scratch_shapes=list(scratch.values()),
        compiler_params=pltpu.CompilerParams(
            collective_id=0, has_side_effects=True, vmem_limit_bytes=58 << 20
        ),
        name="potential",
    )(*operands.values())
    return tuple(
        pl.pallas_call(
            part_kernel,
            out_shape=[jax.ShapeDtypeStruct((1, 1, atoms), F32)] * 2,
            in_specs=[vmem],
            out_specs=[vmem] * 2,
            name="outputs",
        )(both)
    )


def solution(mesh):
    counts = (mesh.shape["domain"], mesh.shape["inner"])
    in_specs = (
        P("domain", "inner", None, None),
        P("domain", "inner", None, None),
        P("domain", "inner", None),
        P("domain", "inner", None, None),
        P("domain", "inner", None),
        P(),
        P(),
        P(),
        P(),
        P(),
        P(),
        P(),
    )
    out_specs = (P("domain", "inner", None), P("domain", "inner", None))
    return jax.shard_map(
        functools.partial(local, counts),
        mesh=mesh,
        in_specs=in_specs,
        out_specs=out_specs,
        check_vma=False,
    )
```

```python
import functools
import math

import jax
import jax.numpy as jnp
import numpy as np
from jax import lax
from jax.experimental import pallas as pl
from jax.experimental.pallas import tpu as pltpu
from jax.sharding import PartitionSpec as P

MESH = pl.DeviceIdType.MESH
VMEM = pltpu.VMEM
F32 = jnp.float32
BF16 = jnp.bfloat16

spacing = 0.55
cutoff = 5.0
smearing = 0.2
coulomb = 14.399645
neighbour_scale = 0.25

Z_LOW = 111
Z_SPAN = 33
PLANES = 2 * Z_SPAN
ROW_LOW = 504 // 128
ROW_HIGH = 4103 // 128

DEGREE = (0, 1, 1, 1, 2, 2, 2, 2, 2)


def dot(a, b):
    return lax.dot_general(a, b, (((1,), (0,)), ((), ())), preferred_element_type=F32)


def dot_nt(a, b):
    return lax.dot_general(a, b, (((1,), (1,)), ((), ())), preferred_element_type=F32)


def split(x):
    high = x.astype(BF16)
    return high, (x - high.astype(F32)).astype(BF16)


def dot_split(a, b, form):
    return form(a[0], b[0]) + (form(a[0], b[1]) + form(a[1], b[0]))


def three_parts(x):
    first = x.astype(BF16).astype(F32)
    second = (x - first).astype(BF16).astype(F32)
    third = (x - first - second).astype(BF16).astype(F32)
    return first, second, third


def basis_rows(length, positions):
    half = length // 2
    k = np.arange(half)
    angle = 2.0 * np.pi * ((k[:, None] * positions[None, :]) % length) / length
    cosine = np.cos(angle)
    sine = np.sin(angle)
    sine[0] = np.cos(np.pi * positions)
    return np.concatenate([cosine, sine], axis=0)


@functools.lru_cache(maxsize=None)
def host_tables(domain_count, inner_count, planes_x, planes_y, depth):
    full_x = planes_x * domain_count
    full_y = planes_y * inner_count
    table_x = basis_rows(full_x, np.arange(full_x))
    table_y = np.zeros((inner_count, 128, 3, full_y))
    for i in range(inner_count):
        all_y = basis_rows(full_y, (planes_y * i - 1 + np.arange(planes_y + 1)) % full_y).T
        table_y[i, : planes_y + 1, 0] = all_y
        table_y[i, 65:98, 1] = all_y[:33]
        table_y[i, 65:97, 2] = all_y[33:]
    table_y = table_y.transpose(2, 0, 1, 3).reshape(3, inner_count * 128, full_y)

    def squared_freq(length, count):
        return (np.arange(count) / (length * spacing)) ** 2

    def modulus(length, count):
        return (2.0 + np.cos(2.0 * np.pi * np.arange(count) / length)) ** 2 / 9.0

    def twice(length, count):
        k = np.arange(count)
        return np.where((k == 0) | (k == length // 2), 1.0, 2.0)

    cx, cy, cz = full_x // 2 + 1, full_y // 2 + 1, depth // 2 + 1
    squared = (
        squared_freq(full_x, cx)[:, None, None]
        + squared_freq(full_y, cy)[None, :, None]
        + squared_freq(depth, cz)[None, None, :]
    )
    safe = np.where(squared > 0.0, squared, 1.0)
    moduli = (
        modulus(full_x, cx)[:, None, None]
        * modulus(full_y, cy)[None, :, None]
        * modulus(depth, cz)[None, None, :]
    )
    volume = full_x * full_y * depth * spacing**3
    kernel = (
        coulomb
        * np.exp(-2.0 * np.pi**2 * smearing**2 * squared)
        / (np.pi * volume * safe * moduli)
    )
    kernel = np.where(squared > 0.0, kernel, 0.0)
    kernel = kernel * twice(full_x, cx)[:, None, None] * twice(full_y, cy)[None, :, None]
    step = np.arange(Z_SPAN)
    along = np.cos(2.0 * np.pi * np.arange(cz)[:, None] * step[None, :] / depth)
    along = along * twice(depth, cz)[:, None]
    wave = np.cos(np.pi * (2 * np.arange(Z_SPAN)[None, :] + 1) * step[:, None] / (2 * Z_SPAN))
    wave = wave * np.where(step == 0, 1.0, 2.0)[:, None] / Z_SPAN
    gain = np.moveaxis(kernel @ (along @ wave), 2, 0)
    order_y = np.concatenate([np.arange(full_y // 2), [full_y // 2], np.arange(1, full_y // 2)])
    gain = gain[:, :, order_y]
    half = full_x // 2
    padded = np.zeros((Z_SPAN, half + 8, full_y), np.float32)
    padded[:, :half] = gain[:, :half]
    padded[:, half] = gain[:, half]
    plane = np.arange(PLANES)
    angle = (
        np.pi * (2 * (plane // 2)[:, None] + 1) * np.arange(40)[None, :] / (2 * Z_SPAN)
    )
    zeta = np.where(plane[:, None] % 2 == 0, np.cos(angle), np.sin(angle))
    zeta[:, Z_SPAN:] = 0.0
    zeta_full = np.zeros((72, 40), np.float32)
    zeta_full[:PLANES] = zeta
    return dict(
        x=table_x.astype(np.float32),
        xt=np.ascontiguousarray(table_x.T).astype(np.float32),
        y=table_y.astype(np.float32),
        gain=padded,
        zeta=zeta_full,
    )


def half_tanh_silu(x):
    half = 0.5 * x
    return half + half * jnp.tanh(half)


def shuffle_matrix(atoms):
    row = lax.broadcasted_iota(jnp.int32, (atoms, atoms), 0)
    column = lax.broadcasted_iota(jnp.int32, (atoms, atoms), 1)
    return (column == row // 8 + (row % 8) * (atoms // 8)).astype(F32).astype(BF16)


def message_weights(species, embed_ref, win_ref, wout_ref, win_wide, pair, shuffle, own_state):
    kinds, channels = embed_ref.shape
    inputs, hidden = win_ref.shape
    atoms = species.shape[1]
    spread_in = (
        lax.broadcasted_iota(jnp.int32, (8, 64), 1) // 8
        == lax.broadcasted_iota(jnp.int32, (8, 64), 0)
    ).astype(F32).astype(BF16)
    wide = dot(win_ref[...].astype(F32).T.astype(BF16), spread_in)
    full = jnp.concatenate([wide] * 8, axis=0)
    row = lax.broadcasted_iota(jnp.int32, full.shape, 0) // hidden
    column = lax.broadcasted_iota(jnp.int32, full.shape, 1) % 8
    win_wide[...] = jnp.where(row == column, full, 0.0).astype(BF16)
    embed = embed_ref[...].astype(F32)
    out = wout_ref[...].astype(F32)
    for degree in range(3):
        part = out[:, degree * channels : (degree + 1) * channels]
        for s in range(kinds):
            pair[degree, s * hidden : (s + 1) * hidden, :] = (part * embed[s : s + 1]).astype(BF16)
    shuffle[...] = shuffle_matrix(atoms)
    kind = lax.broadcasted_iota(jnp.int32, (128, atoms), 0)
    marks = (kind == species).astype(F32).T.astype(BF16)
    padded = jnp.concatenate([embed, jnp.zeros((128 - kinds, channels), F32)], axis=0)
    own_state[...] = dot(shuffle[...], dot(marks, padded.astype(BF16)).astype(BF16))


def message_rows(
    planes,
    ext_ref,
    nbr_ref,
    count_ref,
    mix_ref,
    prod_ref,
    read_ref,
    charge_ref,
    win_wide,
    pair,
    shuffle,
    own_state,
    placed,
    found,
    weight,
    basis,
    kinds,
    moments,
):
    atoms = ext_ref.shape[-1]
    slots = nbr_ref.shape[0]
    tiles = atoms // 128
    channels = mix_ref.shape[-1]
    hidden_size = pair.shape[1] // 8
    for b in range(9):
        row = lax.broadcasted_iota(jnp.int32, (8, atoms), 0)
        shift = jnp.where(
            row == 0, planes[0] * (b // 3 - 1.0), jnp.where(row == 1, planes[1] * (b % 3 - 1.0), 0.0)
        )
        placed[b] = ext_ref[b] + shift

    def gather(t, carry):
        rows = pl.ds(pl.multiple_of((t // tiles) * 8, 8), 8)
        lanes = pl.ds(pl.multiple_of((t % tiles) * 128, 128), 128)
        index = nbr_ref[rows, lanes]
        low = index & 127
        high = index >> 7
        values = [jnp.zeros((8, 128), F32) for _ in range(4)]
        for r in range(ROW_LOW, ROW_HIGH + 1):
            here = high == r
            piece = slice((r % tiles) * 128, (r % tiles) * 128 + 128)
            for c in range(4):
                line = jnp.broadcast_to(placed[r // tiles, c : c + 1, piece], (8, 128))
                picked = jnp.take_along_axis(line, low, axis=1)
                values[c] = jnp.where(here, picked, values[c])
        into = pl.ds(pl.multiple_of((t % tiles) * slots + (t // tiles) * 8, 8), 8)
        for c in range(4):
            found[c, into, :] = values[c]
        return carry

    lax.fori_loop(0, (slots // 8) * tiles, gather, 0)

    own = ext_ref[4]
    slot = lax.broadcasted_iota(jnp.int32, (slots, 128), 0)
    parts = []
    for c in range(4):
        pieces = []
        for j in range(tiles):
            lanes = slice(j * 128, j * 128 + 128)
            value = found[c, slots * j : slots * j + slots, :]
            if c < 3:
                value = (value - own[c : c + 1, lanes]) * spacing
            else:
                value = jnp.where(slot < count_ref[0:1, lanes], value, 8.0)
            pieces.append(value)
        parts.append(jnp.concatenate(pieces, axis=0).T)
    dx, dy, dz, species = parts
    distance = jnp.sqrt(dx * dx + dy * dy + dz * dz)
    inverse = 1.0 / distance
    ux, uy, uz = dx * inverse, dy * inverse, dz * inverse
    scaled = distance * (1.0 / cutoff)
    scaled_sq = scaled * scaled
    six = scaled_sq * scaled_sq * scaled_sq
    envelope = 1.0 - 28.0 * six + 48.0 * six * scaled - 21.0 * six * scaled_sq
    envelope = jnp.where(scaled < 1.0, envelope * neighbour_scale, 0.0)
    r3, r5, r15 = math.sqrt(3.0), math.sqrt(5.0), math.sqrt(15.0)
    factors = (
        None,
        r3 * ux,
        r3 * uy,
        r3 * uz,
        r15 * ux * uy,
        r15 * uy * uz,
        0.5 * r5 * (3.0 * uz * uz - 1.0),
        r15 * ux * uz,
        0.5 * r15 * (ux * ux - uy * uy),
    )
    octets = 8

    def put(target, first, value):
        for o in range(octets):
            target[o, first : first + 8, 0:128] = value[8 * o : 8 * o + 8]
            target[o, first : first + 8, 128:256] = value[64 + 8 * o : 64 + 8 * o + 8]

    for m, factor in enumerate(factors):
        put(weight, 8 * m, envelope if factor is None else envelope * factor)
    put(kinds, 0, species)
    theta = (math.pi / cutoff) * distance
    sine = jnp.sin(theta)
    cosine = 2.0 * jnp.cos(theta)
    scale = math.sqrt(2.0 / cutoff) * inverse
    before = jnp.zeros_like(sine)
    for n in range(8):
        put(basis, 8 * n, scale * sine)
        sine, before = cosine * sine - before, sine

    lane = lax.broadcasted_iota(jnp.int32, (8, 256), 1)
    element = lax.broadcasted_iota(jnp.int32, (8, 256), 0)
    mine = ((lane % 128) // slots) * 2 + lane // 128 == element

    def octet(o, carry):
        hidden = dot(win_wide[...], basis[o].astype(BF16))
        hidden = half_tanh_silu(hidden).astype(BF16)
        for first in range(0, 8, 2):
            sums = []
            for i in (first, first + 1):
                near = hidden[i * hidden_size : (i + 1) * hidden_size]
                kind = kinds[o, i : i + 1, :]
                by_kind = []
                for s in range(8):
                    mark = jnp.broadcast_to((kind == float(s)).astype(F32), (16, 256)).astype(BF16)
                    by_kind.append(near * jnp.concatenate([mark] * (hidden_size // 16), axis=0))
                left = [
                    jnp.where(mine, jnp.broadcast_to(weight[o, 8 * m + i : 8 * m + i + 1, :], (8, 256)), 0.0)
                    for m in range(9)
                ]
                left = jnp.concatenate(left, axis=0).astype(BF16)
                sums.append(dot_nt(left, jnp.concatenate(by_kind, axis=0)))
            into = pl.ds(pl.multiple_of(64 * o + 8 * first, 16), 16)
            for m in range(9):
                both = jnp.concatenate([part[8 * m : 8 * m + 8] for part in sums], axis=0)
                moments[m, into, :] = both.astype(BF16)
        return carry

    lax.fori_loop(0, octets, octet, 0)

    invariants = []
    for degree, (first, last) in enumerate(((0, 1), (1, 4), (4, 9))):
        rows = moments[first:last].reshape((last - first) * atoms, moments.shape[2])
        aggregate = dot(rows, pair[degree]).astype(BF16)
        mixed = dot(aggregate, mix_ref[degree])
        if degree > 0:
            mixed = mixed * mixed
            mixed = sum(mixed[n * atoms : (n + 1) * atoms] for n in range(last - first))
        invariants.append(mixed)
    stacked = jnp.concatenate(invariants, axis=1).astype(BF16)
    update = dot(stacked, prod_ref[...])
    update = update / (1.0 + jnp.exp(-update))
    new_state = (own_state[...] + update).astype(BF16)
    readout = jnp.concatenate(
        [read_ref[...], charge_ref[...], jnp.zeros((14, channels), BF16)], axis=0
    )
    shuffled = dot_nt(readout, new_state)[0:2]
    stack = jnp.concatenate(three_parts(shuffled) + (jnp.zeros((10, atoms), F32),), axis=0)
    ordered = dot(stack.astype(BF16), shuffle[...])
    return ordered[0:2] + ordered[2:4] + ordered[4:6]


def spline_rows(fraction):
    rest = 1.0 - fraction
    square = fraction * fraction
    cube = square * fraction
    return (
        rest * rest * rest * (1.0 / 6.0),
        (3.0 * cube - 6.0 * square + 4.0) * (1.0 / 6.0),
        (-3.0 * cube + 3.0 * square + 3.0 * fraction + 1.0) * (1.0 / 6.0),
        cube * (1.0 / 6.0),
    )


def stencil_rows(rows, first, weights):
    at = lax.broadcasted_iota(jnp.int32, (rows, first.shape[1]), 0) - first
    out = jnp.where(at == 0, weights[0], 0.0)
    for j in range(1, 4):
        out = jnp.where(at == j, weights[j], out)
    return out


def at_marks(position, parts):
    out = jnp.where(position == 125, parts[0], 0.0)
    out = jnp.where(position == 126, parts[1], out)
    return jnp.where(position == 127, parts[2], out)


def several(first, last, unroll, step):
    def turn(n, carry):
        for k in range(unroll):
            step(first + n * unroll + k)
        return carry

    turns = (last - first) // unroll
    lax.fori_loop(0, turns, turn, 0)
    for k in range(first + turns * unroll, last):
        step(k)


WEIGHTS = ("embed", "win", "wout", "mix", "prod", "read", "charge")


def program_kernel(counts, planes, names, *refs):
    ref = dict(zip(names, refs))
    domain_count, inner_count = counts
    devices = domain_count * inner_count
    per_core = devices // 2
    d, i = lax.axis_index("domain"), lax.axis_index("inner")
    me = d * inner_count + i
    at = (d, i)
    slots, atoms = ref["nbr_in"].shape

    def device(t):
        return (t // inner_count, lax.rem(t, inner_count))

    def owner(r):
        rest = lax.rem(r, per_core)
        return (rest // 2, lax.rem(rest, 2) * 2 + r // per_core)

    my_plane = d * 2 + i // 2 + per_core * lax.rem(i, 2)
    owns = my_plane < PLANES

    def rows16(t):
        return pl.ds(pl.multiple_of(t * 16, 16), 16)

    def lanes128(t):
        return pl.ds(pl.multiple_of(t * 128, 128), 128)

    barrier = pltpu.get_barrier_semaphore()

    def greet(k):
        pl.semaphore_signal(
            barrier, inc=1, device_id=device(lax.rem(me + k, devices)), device_id_type=MESH
        )

    several(1, devices, 7, greet)

    def fetch(n, name):
        source = ref[name + "_in"]
        if name == "gain":
            source = source.at[jnp.minimum(my_plane, PLANES - 1) // 2]
        return pltpu.make_async_copy(source, ref[name], ref["fetch_sem"].at[n])

    fetched = ("cells", "frac", "species", "nbr", "count") + WEIGHTS
    fetched = fetched + ("zeta", "y", "x", "xt", "gain")
    fetches = {name: fetch(n, name) for n, name in enumerate(fetched)}
    for name in fetched:
        fetches[name].start()

    moves = [(dx, dy) for dx in (-1, 0, 1) for dy in (-1, 0, 1) if (dx, dy) != (0, 0)]
    mine, ext = ref["mine"], ref["ext"]
    for name in ("cells", "frac", "species"):
        fetches[name].wait()
    cell = [ref["cells"][c] for c in range(3)]
    fraction = [ref["frac"][c] for c in range(3)]
    mine[...] = jnp.zeros_like(mine)
    for c in range(3):
        mine[c : c + 1, :] = cell[c].astype(F32) + fraction[c]
    mine[3:4, :] = ref["species"][0].astype(F32)
    ext[4] = mine[...]

    weights = [spline_rows(f) for f in fraction]
    sten_x = stencil_rows(16, cell[0] - 1, weights[0])
    rim_x = jnp.where(cell[0] == 0, weights[0][0], 0.0)
    sten_z = stencil_rows(40, cell[2] - 1 - Z_LOW, weights[2])
    lane = lax.broadcasted_iota(jnp.int32, (128, atoms), 0)
    y_main = split(stencil_rows(128, cell[1], weights[1]))
    y_low = split(jnp.where(lane <= 97, stencil_rows(128, cell[1] + 65, weights[1]), 0.0))
    y_high = split(jnp.where(lane >= 65, stencil_rows(128, cell[1] + 32, weights[1]), 0.0))
    for n, part in enumerate(y_main + y_low + y_high):
        ref["sten_y"][n] = part
    fetches["zeta"].wait()
    waves = ref["waves"]
    waves[...] = jnp.dot(ref["zeta"][...], sten_z, precision=lax.Precision.HIGHEST)
    sten = ref["sten_x"]
    sten[...] = sten_x
    product, patch32 = ref["product"], ref["patch32"]

    def y_parts(n):
        return ref["sten_y"][2 * n], ref["sten_y"][2 * n + 1]

    def spread(charged):
        for r in range(PLANES):
            product[16 * r : 16 * r + 16, :] = sten[...] * charged[r : r + 1]
        patch32[...] = dot_split(split(product[...]), y_parts(0), dot_nt)
        rim = split(charged * rim_x)
        low = dot_split(rim, y_parts(1), dot_nt)
        high = dot_split(rim, y_parts(2), dot_nt)
        patch32[pl.ds(0, PLANES, 16), :] = patch32[pl.ds(0, PLANES, 16), :] + low[:PLANES]
        patch32[pl.ds(1, PLANES, 16), :] = patch32[pl.ds(1, PLANES, 16), :] + high[:PLANES]

    def to_owners(patch, received, send_sem, recv_sem):
        def start(k):
            r = lax.rem(my_plane + k, PLANES)
            pltpu.make_async_remote_copy(
                src_ref=patch.at[rows16(r), :],
                dst_ref=received.at[rows16(d), lanes128(i)],
                send_sem=send_sem,
                recv_sem=recv_sem,
                device_id=owner(r),
                device_id_type=MESH,
            ).start()

        several(1, PLANES, 5, start)

        @pl.when(jnp.logical_not(owns))
        def _():
            start(PLANES)

        @pl.when(owns)
        def _():
            pltpu.make_async_copy(
                patch.at[rows16(my_plane), :], received.at[rows16(d), lanes128(i)], recv_sem
            ).start()

    def wait_bytes(buffer, sem):
        pltpu.make_async_copy(buffer, buffer, sem).wait()

    spread(waves[...])
    ref["ones_patch"][...] = patch32[...].astype(BF16)
    for name, source in (("x", "x"), ("xt", "xt"), ("y", "y")):
        fetches[source].wait()
        for n, part in enumerate(split(ref[source][...])):
            ref[name + "_parts"][n] = part

    for name in ("nbr", "count") + WEIGHTS:
        fetches[name].wait()
    message_weights(
        ref["species"][0],
        *[ref[name] for name in ("embed", "win", "wout", "win_wide", "pair", "shuffle", "own_state")],
    )

    pl.semaphore_wait(barrier, devices - 1)
    copies = []
    for n, (dx, dy) in enumerate(moves):
        copy = pltpu.make_async_remote_copy(
            src_ref=mine,
            dst_ref=ext.at[(1 - dx) * 3 + (1 - dy)],
            send_sem=ref["ext_send"].at[n],
            recv_sem=ref["ext_recv"].at[n],
            device_id=tuple(
                lax.rem(at[a] + counts[a] + (dx, dy)[a], counts[a]) for a in range(2)
            ),
            device_id_type=MESH,
        )
        copy.start()
        copies.append(copy)
    to_owners(ref["ones_patch"], ref["ones"], ref["ones_send"], ref["ones_recv"])

    for copy in copies:
        copy.wait()
    rows = message_rows(
        planes,
        ext,
        *[
            ref[name]
            for name in (
                "nbr",
                "count",
                "mix",
                "prod",
                "read",
                "charge",
                "win_wide",
                "pair",
                "shuffle",
                "own_state",
                "placed",
                "found",
                "weight",
                "basis",
                "kinds",
                "moments",
            )
        ],
    )
    energy, latent = rows[0:1], rows[1:2]

    block_mean = jnp.sum(latent, axis=1, keepdims=True) / atoms
    spread(waves[...] * (latent - block_mean))
    position = lax.broadcasted_iota(jnp.int32, (1, 128), 1)
    marks = at_marks(position, three_parts(block_mean))
    patch32[pl.ds(2, PLANES, 16), :] = patch32[pl.ds(2, PLANES, 16), :] + marks
    ref["patch"][...] = patch32[...].astype(BF16)
    to_owners(ref["patch"], ref["received"], ref["patch_send"], ref["patch_recv"])

    fetches["gain"].wait()
    answer, back = ref["answer"], ref["back"]

    @pl.when(owns)
    def _():
        grid, coefficient = ref["grid"], ref["coefficient"]
        x_table = ref["x_parts"][0], ref["x_parts"][1]
        xt_table = ref["xt_parts"][0], ref["xt_parts"][1]

        def y_table(part):
            return ref["y_parts"][0, part], ref["y_parts"][1, part]

        def whole_rows(rows):
            return jnp.concatenate([grid[t, rows, :] for t in range(inner_count)], axis=1)

        def every16(first):
            return pl.ds(first, domain_count, 16)

        wait_bytes(ref["ones"], ref["ones_recv"])
        wait_bytes(ref["received"], ref["patch_recv"])
        tiles = [slice(t * 128, t * 128 + 128) for t in range(inner_count)]
        means = []
        for t in range(inner_count):
            grid[t] = ref["received"][:, tiles[t]].astype(F32)
            marked = grid[t, pl.ds(2, domain_count, 16), :]
            means.append(
                jnp.sum(jnp.where(position >= 125, marked, 0.0), axis=1, keepdims=True)
            )
        mean = jnp.sum(sum(means), axis=0, keepdims=True) / devices
        for t in range(inner_count):
            coefficient[t] = jnp.broadcast_to(means[t] - mean, (domain_count, 128))
            for b in range(domain_count):
                here = slice(16 * b, 16 * b + 16)
                unit = ref["ones"][here, tiles[t]].astype(F32)
                grid[t, here, :] = grid[t, here, :] + unit * coefficient[t, b : b + 1, :]
        along_y = dot_split(split(whole_rows(slice(None))), y_table(0), dot)
        rim = dot_split(split(whole_rows(every16(0))), y_table(1), dot)
        rim = rim + dot_split(split(whole_rows(every16(1))), y_table(2), dot)
        rim = pltpu.roll(rim, domain_count - 1, 0)
        lines_ref = ref["lines"]
        full_y = along_y.shape[1]
        columns = [slice(t * 128, t * 128 + 128) for t in range(full_y // 128)]
        for t, column in enumerate(columns):
            lines_ref[t] = along_y[:, column]
            lines_ref[t, every16(15), :] = lines_ref[t, every16(15), :] + rim[:, column]
        lines = jnp.concatenate([lines_ref[t] for t in range(len(columns))], axis=1)
        spectrum = dot_split(x_table, split(lines), dot)
        half = lines.shape[0] // 2
        top = ref["gain"][0:half, :]
        first_row = lax.broadcasted_iota(jnp.int32, (half, full_y), 0) == 0
        bottom = jnp.where(first_row, ref["gain"][half : half + 1, :], top)
        filtered = jnp.concatenate([spectrum[0:half] * top, spectrum[half:] * bottom], axis=0)
        lines = dot_split(xt_table, split(filtered), dot)
        for t, column in enumerate(columns):
            lines_ref[t] = lines[:, column]
        rim = jnp.concatenate(
            [lines_ref[t, every16(15), :] for t in range(len(columns))], axis=1
        )
        rim = split(pltpu.roll(rim, 1, 0))
        values = dot_split(split(lines), y_table(0), dot_nt)
        low_rim = dot_split(rim, y_table(1), dot_nt)
        high_rim = dot_split(rim, y_table(2), dot_nt)
        marks = at_marks(position, three_parts(mean))
        for t in range(inner_count):
            grid[t] = values[:, tiles[t]]
            grid[t, every16(0), :] = grid[t, every16(0), :] + low_rim[:, tiles[t]]
            grid[t, every16(1), :] = grid[t, every16(1), :] + high_rim[:, tiles[t]]
            grid[t, every16(2), :] = grid[t, every16(2), :] + marks
            answer[:, tiles[t]] = grid[t].astype(BF16)

        def back_start(k):
            t = lax.rem(me + k, devices)
            pltpu.make_async_remote_copy(
                src_ref=answer.at[rows16(t // inner_count), lanes128(lax.rem(t, inner_count))],
                dst_ref=back.at[rows16(my_plane), :],
                send_sem=ref["back_send"],
                recv_sem=ref["back_recv"],
                device_id=device(t),
                device_id_type=MESH,
            ).start()

        several(1, devices, 7, back_start)
        pltpu.make_async_copy(
            answer.at[rows16(d), lanes128(i)], back.at[rows16(my_plane), :], ref["back_recv"]
        ).start()

    wait_bytes(back, ref["back_recv"])
    given = back[...]
    main, low, high = y_parts(0), y_parts(1), y_parts(2)
    product[...] = dot(given, main[0]) + dot(given, main[1])
    back32 = patch32
    back32[...] = given.astype(F32)
    mean = jnp.sum(jnp.where(position >= 125, back32[2:3, :], 0.0), axis=1, keepdims=True)
    at_low = back32[pl.ds(0, PLANES, 16), :].astype(BF16)
    at_high = back32[pl.ds(1, PLANES, 16), :].astype(BF16)
    at_rim = dot(at_low, low[0]) + dot(at_low, low[1])
    at_rim = at_rim + dot(at_high, high[0]) + dot(at_high, high[1])
    gathered = jnp.zeros((8, atoms), F32)
    for r in range(PLANES):
        piece = (
            product[16 * r : 16 * r + 8, :] * sten[0:8]
            + product[16 * r + 8 : 16 * r + 16, :] * sten[8:16]
        )
        gathered = gathered + piece * waves[r : r + 1]
    value = jnp.sum(gathered, axis=0, keepdims=True) + rim_x * jnp.sum(
        at_rim * waves[:PLANES], axis=0, keepdims=True
    )
    ref["out"][0:1] = energy + 0.5 * (latent - mean) * value
    ref["out"][1:2] = value

    sent = ref["sent"]
    for sem in (ref["ones_send"], ref["patch_send"]):

        @pl.when(owns)
        def _():
            wait_bytes(sent.at[0 : (PLANES - 1) * 16], sem)

        @pl.when(jnp.logical_not(owns))
        def _():
            wait_bytes(sent.at[0 : PLANES * 16], sem)

    @pl.when(owns)
    def _():
        wait_bytes(sent.at[0 : (devices - 1) * 16], ref["back_send"])


def part_kernel(both_ref, energy_ref, potential_ref):
    energy_ref[0] = both_ref[0:1, :]
    potential_ref[0] = both_ref[1:2, :]


def local(
    counts,
    atom_cells,
    atom_frac,
    species,
    nbr_index,
    nbr_count,
    embed,
    radial_in,
    radial_out,
    mix_weight,
    product_weight,
    read_weight,
    charge_weight,
):
    planes = (16, 64)
    devices = counts[0] * counts[1]
    tables = host_tables(*counts, *planes, 256)
    operands = dict(
        cells=atom_cells.transpose(2, 0, 1, 3)[:, 0],
        frac=atom_frac.transpose(2, 0, 1, 3)[:, 0],
        species=species,
        nbr=nbr_index[0, 0].T,
        count=nbr_count[0],
        embed=embed,
        win=radial_in[0],
        wout=radial_out[0],
        mix=mix_weight[0],
        prod=product_weight[0],
        read=read_weight,
        charge=charge_weight[None],
        **{name: jnp.asarray(tables[name]) for name in ("zeta", "y", "x", "xt", "gain")},
    )
    slots, atoms = operands["nbr"].shape
    channels = embed.shape[1]
    hidden = radial_in.shape[-1]
    full_x, full_y, lanes = counts[0] * planes[0], counts[1] * planes[1], counts[1] * 128
    dma = pltpu.SemaphoreType.DMA
    scratch = {
        name: VMEM(value.shape[1:] if name == "gain" else value.shape, value.dtype)
        for name, value in operands.items()
    }
    scratch.update(
        mine=VMEM((8, atoms), F32),
        ext=VMEM((9, 8, atoms), F32),
        placed=VMEM((9, 8, atoms), F32),
        found=VMEM((4, atoms // 128 * slots, 128), F32),
        weight=VMEM((8, 72, 256), F32),
        basis=VMEM((8, 64, 256), F32),
        kinds=VMEM((8, 8, 256), F32),
        moments=VMEM((9, atoms, 8 * hidden), BF16),
        win_wide=VMEM((8 * hidden, 64), BF16),
        pair=VMEM((3, 8 * hidden, channels), BF16),
        shuffle=VMEM((atoms, atoms), BF16),
        own_state=VMEM((atoms, channels), F32),
        sten_x=VMEM((16, atoms), F32),
        sten_y=VMEM((6, 128, atoms), BF16),
        waves=VMEM((72, atoms), F32),
        product=VMEM((PLANES * 16, atoms), F32),
        patch32=VMEM((PLANES * 16, 128), F32),
        ones_patch=VMEM((PLANES * 16, 128), BF16),
        patch=VMEM((PLANES * 16, 128), BF16),
        ones=VMEM((full_x, lanes), BF16),
        received=VMEM((full_x, lanes), BF16),
        grid=VMEM((counts[1], full_x, 128), F32),
        coefficient=VMEM((counts[1], counts[0], 128), F32),
        lines=VMEM((full_y // 128, full_x, 128), F32),
        x_parts=VMEM((2, full_x, full_x), BF16),
        xt_parts=VMEM((2, full_x, full_x), BF16),
        y_parts=VMEM((2, 3, lanes, full_y), BF16),
        answer=VMEM((full_x, lanes), BF16),
        back=VMEM((PLANES * 16, 128), BF16),
        sent=VMEM(((devices - 1) * 16, 128), BF16),
        fetch_sem=dma((len(operands),)),
        ext_send=dma((8,)),
        ext_recv=dma((8,)),
        ones_send=dma,
        ones_recv=dma,
        patch_send=dma,
        patch_recv=dma,
        back_send=dma,
        back_recv=dma,
    )
    names = [name + "_in" for name in operands] + ["out"] + list(scratch)
    vmem = pl.BlockSpec(memory_space=VMEM)
    both = pl.pallas_call(
        functools.partial(program_kernel, counts, planes, names),
        out_shape=jax.ShapeDtypeStruct((2, atoms), F32),
        in_specs=[pl.BlockSpec(memory_space=pl.ANY)] * len(operands),
        out_specs=vmem,
        scratch_shapes=list(scratch.values()),
        compiler_params=pltpu.CompilerParams(
            collective_id=0, has_side_effects=True, vmem_limit_bytes=58 << 20
        ),
        name="potential",
    )(*operands.values())
    return tuple(
        pl.pallas_call(
            part_kernel,
            out_shape=[jax.ShapeDtypeStruct((1, 1, atoms), F32)] * 2,
            in_specs=[vmem],
            out_specs=[vmem] * 2,
            name="outputs",
        )(both)
    )


def solution(mesh):
    counts = (mesh.shape["domain"], mesh.shape["inner"])
    in_specs = (
        P("domain", "inner", None, None),
        P("domain", "inner", None, None),
        P("domain", "inner", None),
        P("domain", "inner", None, None),
        P("domain", "inner", None),
        P(),
        P(),
        P(),
        P(),
        P(),
        P(),
        P(),
    )
    out_specs = (P("domain", "inner", None), P("domain", "inner", None))
    return jax.shard_map(
        functools.partial(local, counts),
        mesh=mesh,
        in_specs=in_specs,
        out_specs=out_specs,
        check_vma=False,
    )
```

```python
import functools
import math

import jax
import jax.numpy as jnp
import numpy as np
from jax import lax
from jax.experimental import pallas as pl
from jax.experimental.pallas import tpu as pltpu
from jax.sharding import PartitionSpec as P

MESH = pl.DeviceIdType.MESH
VMEM = pltpu.VMEM
F32 = jnp.float32
BF16 = jnp.bfloat16

spacing = 0.55
cutoff = 5.0
smearing = 0.2
coulomb = 14.399645
neighbour_scale = 0.25

Z_LOW = 111
Z_SPAN = 33
PLANES = 2 * Z_SPAN
ROW_LOW = 504 // 128
ROW_HIGH = 4103 // 128

DEGREE = (0, 1, 1, 1, 2, 2, 2, 2, 2)


def dot(a, b):
    return lax.dot_general(a, b, (((1,), (0,)), ((), ())), preferred_element_type=F32)


def dot_nt(a, b):
    return lax.dot_general(a, b, (((1,), (1,)), ((), ())), preferred_element_type=F32)


def split(x):
    high = x.astype(BF16)
    return high, (x - high.astype(F32)).astype(BF16)


def dot_left(a, b, form):
    rounded = a.astype(BF16)
    return form(rounded, b[0]) + form(rounded, b[1])


def dot_split(a, b, form):
    return form(a[0], b[0]) + (form(a[0], b[1]) + form(a[1], b[0]))


def three_parts(x):
    first = x.astype(BF16).astype(F32)
    second = (x - first).astype(BF16).astype(F32)
    third = (x - first - second).astype(BF16).astype(F32)
    return first, second, third


def basis_rows(length, positions):
    half = length // 2
    k = np.arange(half)
    angle = 2.0 * np.pi * ((k[:, None] * positions[None, :]) % length) / length
    cosine = np.cos(angle)
    sine = np.sin(angle)
    sine[0] = np.cos(np.pi * positions)
    return np.concatenate([cosine, sine], axis=0)


@functools.lru_cache(maxsize=None)
def host_tables(domain_count, inner_count, planes_x, planes_y, depth):
    full_x = planes_x * domain_count
    full_y = planes_y * inner_count
    table_x = basis_rows(full_x, np.arange(full_x))
    table_y = np.zeros((inner_count, 128, 3, full_y))
    for i in range(inner_count):
        all_y = basis_rows(full_y, (planes_y * i - 1 + np.arange(planes_y + 1)) % full_y).T
        table_y[i, : planes_y + 1, 0] = all_y
        table_y[i, 65:98, 1] = all_y[:33]
        table_y[i, 65:97, 2] = all_y[33:]
    table_y = table_y.transpose(2, 0, 1, 3).reshape(3, inner_count * 128, full_y)

    def squared_freq(length, count):
        return (np.arange(count) / (length * spacing)) ** 2

    def modulus(length, count):
        return (2.0 + np.cos(2.0 * np.pi * np.arange(count) / length)) ** 2 / 9.0

    def twice(length, count):
        k = np.arange(count)
        return np.where((k == 0) | (k == length // 2), 1.0, 2.0)

    cx, cy, cz = full_x // 2 + 1, full_y // 2 + 1, depth // 2 + 1
    squared = (
        squared_freq(full_x, cx)[:, None, None]
        + squared_freq(full_y, cy)[None, :, None]
        + squared_freq(depth, cz)[None, None, :]
    )
    safe = np.where(squared > 0.0, squared, 1.0)
    moduli = (
        modulus(full_x, cx)[:, None, None]
        * modulus(full_y, cy)[None, :, None]
        * modulus(depth, cz)[None, None, :]
    )
    volume = full_x * full_y * depth * spacing**3
    kernel = (
        coulomb
        * np.exp(-2.0 * np.pi**2 * smearing**2 * squared)
        / (np.pi * volume * safe * moduli)
    )
    kernel = np.where(squared > 0.0, kernel, 0.0)
    kernel = kernel * twice(full_x, cx)[:, None, None] * twice(full_y, cy)[None, :, None]
    step = np.arange(Z_SPAN)
    along = np.cos(2.0 * np.pi * np.arange(cz)[:, None] * step[None, :] / depth)
    along = along * twice(depth, cz)[:, None]
    wave = np.cos(np.pi * (2 * np.arange(Z_SPAN)[None, :] + 1) * step[:, None] / (2 * Z_SPAN))
    wave = wave * np.where(step == 0, 1.0, 2.0)[:, None] / Z_SPAN
    gain = np.moveaxis(kernel @ (along @ wave), 2, 0)
    order_y = np.concatenate([np.arange(full_y // 2), [full_y // 2], np.arange(1, full_y // 2)])
    gain = gain[:, :, order_y]
    half = full_x // 2
    padded = np.zeros((Z_SPAN, half + 8, full_y), np.float32)
    padded[:, :half] = gain[:, :half]
    padded[:, half] = gain[:, half]
    plane = np.arange(PLANES)
    angle = (
        np.pi * (2 * (plane // 2)[:, None] + 1) * np.arange(40)[None, :] / (2 * Z_SPAN)
    )
    zeta = np.where(plane[:, None] % 2 == 0, np.cos(angle), np.sin(angle))
    zeta[:, Z_SPAN:] = 0.0
    zeta_full = np.zeros((72, 40), np.float32)
    zeta_full[:PLANES] = zeta
    return dict(
        x=table_x.astype(np.float32),
        xt=np.ascontiguousarray(table_x.T).astype(np.float32),
        y=table_y.astype(np.float32),
        gain=padded,
        zeta=zeta_full,
    )


def half_tanh_silu(x):
    half = 0.5 * x
    return half + half * jnp.tanh(half)


def shuffle_matrix(atoms):
    row = lax.broadcasted_iota(jnp.int32, (atoms, atoms), 0)
    column = lax.broadcasted_iota(jnp.int32, (atoms, atoms), 1)
    return (column == row // 8 + (row % 8) * (atoms // 8)).astype(F32).astype(BF16)


def message_weights(species, embed_ref, win_ref, wout_ref, win_wide, pair, shuffle, own_state):
    kinds, channels = embed_ref.shape
    inputs, hidden = win_ref.shape
    atoms = species.shape[1]
    spread_in = (
        lax.broadcasted_iota(jnp.int32, (8, 64), 1) // 8
        == lax.broadcasted_iota(jnp.int32, (8, 64), 0)
    ).astype(F32).astype(BF16)
    wide = dot(win_ref[...].astype(F32).T.astype(BF16), spread_in)
    full = jnp.concatenate([wide] * 8, axis=0)
    row = lax.broadcasted_iota(jnp.int32, full.shape, 0) // hidden
    column = lax.broadcasted_iota(jnp.int32, full.shape, 1) % 8
    win_wide[...] = jnp.where(row == column, full, 0.0).astype(BF16)
    embed = embed_ref[...].astype(F32)
    out = wout_ref[...].astype(F32)
    for degree in range(3):
        part = out[:, degree * channels : (degree + 1) * channels]
        for s in range(kinds):
            pair[degree, s * hidden : (s + 1) * hidden, :] = (part * embed[s : s + 1]).astype(BF16)
    shuffle[...] = shuffle_matrix(atoms)
    kind = lax.broadcasted_iota(jnp.int32, (128, atoms), 0)
    marks = (kind == species).astype(F32).T.astype(BF16)
    padded = jnp.concatenate([embed, jnp.zeros((128 - kinds, channels), F32)], axis=0)
    own_state[...] = dot(shuffle[...], dot(marks, padded.astype(BF16)).astype(BF16))


def message_rows(
    planes,
    ext_ref,
    nbr_ref,
    count_ref,
    mix_ref,
    prod_ref,
    read_ref,
    charge_ref,
    win_wide,
    pair,
    shuffle,
    own_state,
    placed,
    found,
    weight,
    basis,
    kinds,
    moments,
):
    atoms = ext_ref.shape[-1]
    slots = nbr_ref.shape[0]
    tiles = atoms // 128
    channels = mix_ref.shape[-1]
    hidden_size = pair.shape[1] // 8
    for b in range(9):
        row = lax.broadcasted_iota(jnp.int32, (8, atoms), 0)
        shift = jnp.where(
            row == 0, planes[0] * (b // 3 - 1.0), jnp.where(row == 1, planes[1] * (b % 3 - 1.0), 0.0)
        )
        block = ext_ref[b] + shift
        placed[b] = jnp.where(row == 0, block + 64.0 * ext_ref[b, 3:4, :], block)

    def gather(t, carry):
        rows = pl.ds(pl.multiple_of((t // tiles) * 8, 8), 8)
        lanes = pl.ds(pl.multiple_of((t % tiles) * 128, 128), 128)
        index = nbr_ref[rows, lanes]
        low = index & 127
        high = index >> 7
        values = [jnp.zeros((8, 128), F32) for _ in range(3)]
        for r in range(ROW_LOW, ROW_HIGH + 1):
            here = high == r
            piece = slice((r % tiles) * 128, (r % tiles) * 128 + 128)
            for c in range(3):
                line = jnp.broadcast_to(placed[r // tiles, c : c + 1, piece], (8, 128))
                picked = jnp.take_along_axis(line, low, axis=1)
                values[c] = jnp.where(here, picked, values[c])
        into = pl.ds(pl.multiple_of((t % tiles) * slots + (t // tiles) * 8, 8), 8)
        kind = jnp.floor((values[0] + 32.0) * (1.0 / 64.0))
        found[0, into, :] = values[0] - 64.0 * kind
        found[1, into, :] = values[1]
        found[2, into, :] = values[2]
        found[3, into, :] = kind
        return carry

    lax.fori_loop(0, (slots // 8) * tiles, gather, 0)

    own = ext_ref[4]
    slot = lax.broadcasted_iota(jnp.int32, (slots, 128), 0)
    parts = []
    for c in range(4):
        pieces = []
        for j in range(tiles):
            lanes = slice(j * 128, j * 128 + 128)
            value = found[c, slots * j : slots * j + slots, :]
            if c < 3:
                value = (value - own[c : c + 1, lanes]) * spacing
            else:
                value = jnp.where(slot < count_ref[0:1, lanes], value, 8.0)
            pieces.append(value)
        parts.append(jnp.concatenate(pieces, axis=0).T)
    dx, dy, dz, species = parts
    distance = jnp.sqrt(dx * dx + dy * dy + dz * dz)
    inverse = 1.0 / distance
    ux, uy, uz = dx * inverse, dy * inverse, dz * inverse
    scaled = distance * (1.0 / cutoff)
    scaled_sq = scaled * scaled
    six = scaled_sq * scaled_sq * scaled_sq
    envelope = 1.0 - 28.0 * six + 48.0 * six * scaled - 21.0 * six * scaled_sq
    envelope = jnp.where(scaled < 1.0, envelope * neighbour_scale, 0.0)
    r3, r5, r15 = math.sqrt(3.0), math.sqrt(5.0), math.sqrt(15.0)
    factors = (
        None,
        r3 * ux,
        r3 * uy,
        r3 * uz,
        r15 * ux * uy,
        r15 * uy * uz,
        0.5 * r5 * (3.0 * uz * uz - 1.0),
        r15 * ux * uz,
        0.5 * r15 * (ux * ux - uy * uy),
    )
    octets = 8

    def put(target, first, value):
        for o in range(octets):
            target[o, first : first + 8, 0:128] = value[8 * o : 8 * o + 8]
            target[o, first : first + 8, 128:256] = value[64 + 8 * o : 64 + 8 * o + 8]

    for m, factor in enumerate(factors):
        put(weight, 8 * m, envelope if factor is None else envelope * factor)
    put(kinds, 0, species)
    theta = (math.pi / cutoff) * distance
    sine = jnp.sin(theta)
    cosine = 2.0 * jnp.cos(theta)
    scale = math.sqrt(2.0 / cutoff) * inverse
    before = jnp.zeros_like(sine)
    for n in range(8):
        put(basis, 8 * n, scale * sine)
        sine, before = cosine * sine - before, sine

    lane = lax.broadcasted_iota(jnp.int32, (8, 256), 1)
    element = lax.broadcasted_iota(jnp.int32, (8, 256), 0)
    mine = ((lane % 128) // slots) * 2 + lane // 128 == element

    def octet(o, carry):
        hidden = dot(win_wide[...], basis[o].astype(BF16))
        hidden = half_tanh_silu(hidden).astype(BF16)
        for first in range(0, 8, 2):
            sums = []
            for i in (first, first + 1):
                near = hidden[i * hidden_size : (i + 1) * hidden_size]
                kind = kinds[o, i : i + 1, :]
                by_kind = []
                for s in range(8):
                    mark = jnp.broadcast_to((kind == float(s)).astype(F32), (16, 256)).astype(BF16)
                    by_kind.append(near * jnp.concatenate([mark] * (hidden_size // 16), axis=0))
                left = [
                    jnp.where(mine, jnp.broadcast_to(weight[o, 8 * m + i : 8 * m + i + 1, :], (8, 256)), 0.0)
                    for m in range(9)
                ]
                left = jnp.concatenate(left, axis=0).astype(BF16)
                sums.append(dot_nt(left, jnp.concatenate(by_kind, axis=0)))
            into = pl.ds(pl.multiple_of(64 * o + 8 * first, 16), 16)
            for m in range(9):
                both = jnp.concatenate([part[8 * m : 8 * m + 8] for part in sums], axis=0)
                moments[m, into, :] = both.astype(BF16)
        return carry

    lax.fori_loop(0, octets, octet, 0)

    invariants = []
    for degree, (first, last) in enumerate(((0, 1), (1, 4), (4, 9))):
        rows = moments[first:last].reshape((last - first) * atoms, moments.shape[2])
        aggregate = dot(rows, pair[degree]).astype(BF16)
        mixed = dot(aggregate, mix_ref[degree])
        if degree > 0:
            mixed = mixed * mixed
            mixed = sum(mixed[n * atoms : (n + 1) * atoms] for n in range(last - first))
        invariants.append(mixed)
    stacked = jnp.concatenate(invariants, axis=1).astype(BF16)
    update = dot(stacked, prod_ref[...])
    update = update / (1.0 + jnp.exp(-update))
    new_state = (own_state[...] + update).astype(BF16)
    readout = jnp.concatenate(
        [read_ref[...], charge_ref[...], jnp.zeros((14, channels), BF16)], axis=0
    )
    shuffled = dot_nt(readout, new_state)[0:2]
    stack = jnp.concatenate(three_parts(shuffled) + (jnp.zeros((10, atoms), F32),), axis=0)
    ordered = dot(stack.astype(BF16), shuffle[...])
    return ordered[0:2] + ordered[2:4] + ordered[4:6]


def spline_rows(fraction):
    rest = 1.0 - fraction
    square = fraction * fraction
    cube = square * fraction
    return (
        rest * rest * rest * (1.0 / 6.0),
        (3.0 * cube - 6.0 * square + 4.0) * (1.0 / 6.0),
        (-3.0 * cube + 3.0 * square + 3.0 * fraction + 1.0) * (1.0 / 6.0),
        cube * (1.0 / 6.0),
    )


def stencil_rows(rows, first, weights):
    at = lax.broadcasted_iota(jnp.int32, (rows, first.shape[1]), 0) - first
    out = jnp.where(at == 0, weights[0], 0.0)
    for j in range(1, 4):
        out = jnp.where(at == j, weights[j], out)
    return out


def at_marks(position, parts):
    out = jnp.where(position == 125, parts[0], 0.0)
    out = jnp.where(position == 126, parts[1], out)
    return jnp.where(position == 127, parts[2], out)


def several(first, last, unroll, step):
    def turn(n, carry):
        for k in range(unroll):
            step(first + n * unroll + k)
        return carry

    turns = (last - first) // unroll
    lax.fori_loop(0, turns, turn, 0)
    for k in range(first + turns * unroll, last):
        step(k)


WEIGHTS = ("embed", "win", "wout", "mix", "prod", "read", "charge")


def program_kernel(counts, planes, names, *refs):
    ref = dict(zip(names, refs))
    domain_count, inner_count = counts
    devices = domain_count * inner_count
    per_core = devices // 2
    d, i = lax.axis_index("domain"), lax.axis_index("inner")
    me = d * inner_count + i
    at = (d, i)
    slots, atoms = ref["nbr_in"].shape

    def device(t):
        return (t // inner_count, lax.rem(t, inner_count))

    def owner(r):
        rest = lax.rem(r, per_core)
        return (rest // 2, lax.rem(rest, 2) * 2 + r // per_core)

    my_plane = d * 2 + i // 2 + per_core * lax.rem(i, 2)
    owns = my_plane < PLANES

    def rows16(t):
        return pl.ds(pl.multiple_of(t * 16, 16), 16)

    def lanes128(t):
        return pl.ds(pl.multiple_of(t * 128, 128), 128)

    barrier = pltpu.get_barrier_semaphore()

    def greet(k):
        pl.semaphore_signal(
            barrier, inc=1, device_id=device(lax.rem(me + k, devices)), device_id_type=MESH
        )

    several(1, devices, 7, greet)

    def fetch(n, name):
        source = ref[name + "_in"]
        if name == "gain":
            source = source.at[jnp.minimum(my_plane, PLANES - 1) // 2]
        return pltpu.make_async_copy(source, ref[name], ref["fetch_sem"].at[n])

    fetched = ("cells", "frac", "species", "nbr", "count") + WEIGHTS
    fetched = fetched + ("zeta", "y", "x", "xt", "gain")
    fetches = {name: fetch(n, name) for n, name in enumerate(fetched)}
    for name in fetched:
        fetches[name].start()

    moves = [(dx, dy) for dx in (-1, 0, 1) for dy in (-1, 0, 1) if (dx, dy) != (0, 0)]
    mine, ext = ref["mine"], ref["ext"]
    for name in ("cells", "frac", "species"):
        fetches[name].wait()
    cell = [ref["cells"][c] for c in range(3)]
    fraction = [ref["frac"][c] for c in range(3)]
    mine[...] = jnp.zeros_like(mine)
    for c in range(3):
        mine[c : c + 1, :] = cell[c].astype(F32) + fraction[c]
    mine[3:4, :] = ref["species"][0].astype(F32)
    ext[4] = mine[...]

    weights = [spline_rows(f) for f in fraction]
    sten_x = stencil_rows(16, cell[0] - 1, weights[0])
    rim_x = jnp.where(cell[0] == 0, weights[0][0], 0.0)
    sten_z = stencil_rows(40, cell[2] - 1 - Z_LOW, weights[2])
    lane = lax.broadcasted_iota(jnp.int32, (128, atoms), 0)
    y_main = split(stencil_rows(128, cell[1], weights[1]))
    y_low = split(jnp.where(lane <= 97, stencil_rows(128, cell[1] + 65, weights[1]), 0.0))
    y_high = split(jnp.where(lane >= 65, stencil_rows(128, cell[1] + 32, weights[1]), 0.0))
    for n, part in enumerate(y_main + y_low + y_high):
        ref["sten_y"][n] = part
    fetches["zeta"].wait()
    waves = ref["waves"]
    waves[...] = jnp.dot(ref["zeta"][...], sten_z, precision=lax.Precision.HIGHEST)
    sten = ref["sten_x"]
    sten[...] = sten_x
    product, patch32 = ref["product"], ref["patch32"]

    def y_parts(n):
        return ref["sten_y"][2 * n], ref["sten_y"][2 * n + 1]

    def spread(charged):
        for r in range(PLANES):
            product[16 * r : 16 * r + 16, :] = sten[...] * charged[r : r + 1]
        patch32[...] = dot_split(split(product[...]), y_parts(0), dot_nt)
        rim = split(charged * rim_x)
        low = dot_split(rim, y_parts(1), dot_nt)
        high = dot_split(rim, y_parts(2), dot_nt)
        patch32[pl.ds(0, PLANES, 16), :] = patch32[pl.ds(0, PLANES, 16), :] + low[:PLANES]
        patch32[pl.ds(1, PLANES, 16), :] = patch32[pl.ds(1, PLANES, 16), :] + high[:PLANES]

    def to_owners(patch, received, send_sem, recv_sem):
        def start(k):
            r = lax.rem(my_plane + k, PLANES)
            pltpu.make_async_remote_copy(
                src_ref=patch.at[rows16(r), :],
                dst_ref=received.at[rows16(d), lanes128(i)],
                send_sem=send_sem,
                recv_sem=recv_sem,
                device_id=owner(r),
                device_id_type=MESH,
            ).start()

        several(1, PLANES, 5, start)

        @pl.when(jnp.logical_not(owns))
        def _():
            start(PLANES)

        @pl.when(owns)
        def _():
            pltpu.make_async_copy(
                patch.at[rows16(my_plane), :], received.at[rows16(d), lanes128(i)], recv_sem
            ).start()

    def wait_bytes(buffer, sem):
        pltpu.make_async_copy(buffer, buffer, sem).wait()

    spread(waves[...])
    ref["ones_patch"][...] = patch32[...].astype(BF16)
    for name, source in (("x", "x"), ("xt", "xt"), ("y", "y")):
        fetches[source].wait()
        for n, part in enumerate(split(ref[source][...])):
            ref[name + "_parts"][n] = part

    for name in ("nbr", "count") + WEIGHTS:
        fetches[name].wait()
    message_weights(
        ref["species"][0],
        *[ref[name] for name in ("embed", "win", "wout", "win_wide", "pair", "shuffle", "own_state")],
    )

    pl.semaphore_wait(barrier, devices - 1)
    copies = []
    for n, (dx, dy) in enumerate(moves):
        copy = pltpu.make_async_remote_copy(
            src_ref=mine,
            dst_ref=ext.at[(1 - dx) * 3 + (1 - dy)],
            send_sem=ref["ext_send"].at[n],
            recv_sem=ref["ext_recv"].at[n],
            device_id=tuple(
                lax.rem(at[a] + counts[a] + (dx, dy)[a], counts[a]) for a in range(2)
            ),
            device_id_type=MESH,
        )
        copy.start()
        copies.append(copy)
    to_owners(ref["ones_patch"], ref["ones"], ref["ones_send"], ref["ones_recv"])

    for copy in copies:
        copy.wait()
    rows = message_rows(
        planes,
        ext,
        *[
            ref[name]
            for name in (
                "nbr",
                "count",
                "mix",
                "prod",
                "read",
                "charge",
                "win_wide",
                "pair",
                "shuffle",
                "own_state",
                "placed",
                "found",
                "weight",
                "basis",
                "kinds",
                "moments",
            )
        ],
    )
    energy, latent = rows[0:1], rows[1:2]

    block_mean = jnp.sum(latent, axis=1, keepdims=True) / atoms
    spread(waves[...] * (latent - block_mean))
    position = lax.broadcasted_iota(jnp.int32, (1, 128), 1)
    marks = at_marks(position, three_parts(block_mean))
    patch32[pl.ds(2, PLANES, 16), :] = patch32[pl.ds(2, PLANES, 16), :] + marks
    ref["patch"][...] = patch32[...].astype(BF16)
    to_owners(ref["patch"], ref["received"], ref["patch_send"], ref["patch_recv"])

    fetches["gain"].wait()
    answer, back = ref["answer"], ref["back"]

    @pl.when(owns)
    def _():
        grid, coefficient = ref["grid"], ref["coefficient"]
        x_table = ref["x_parts"][0], ref["x_parts"][1]
        xt_table = ref["xt_parts"][0], ref["xt_parts"][1]

        def y_table(part):
            return ref["y_parts"][0, part], ref["y_parts"][1, part]

        def whole_rows(rows):
            return jnp.concatenate([grid[t, rows, :] for t in range(inner_count)], axis=1)

        def every16(first):
            return pl.ds(first, domain_count, 16)

        wait_bytes(ref["ones"], ref["ones_recv"])
        wait_bytes(ref["received"], ref["patch_recv"])
        tiles = [slice(t * 128, t * 128 + 128) for t in range(inner_count)]
        means = []
        for t in range(inner_count):
            grid[t] = ref["received"][:, tiles[t]].astype(F32)
            marked = grid[t, pl.ds(2, domain_count, 16), :]
            means.append(
                jnp.sum(jnp.where(position >= 125, marked, 0.0), axis=1, keepdims=True)
            )
        mean = jnp.sum(sum(means), axis=0, keepdims=True) / devices
        for t in range(inner_count):
            coefficient[t] = jnp.broadcast_to(means[t] - mean, (domain_count, 128))
            for b in range(domain_count):
                here = slice(16 * b, 16 * b + 16)
                unit = ref["ones"][here, tiles[t]].astype(F32)
                grid[t, here, :] = grid[t, here, :] + unit * coefficient[t, b : b + 1, :]
        along_y = dot_left(whole_rows(slice(None)), y_table(0), dot)
        rim = dot_left(whole_rows(every16(0)), y_table(1), dot)
        rim = rim + dot_left(whole_rows(every16(1)), y_table(2), dot)
        rim = pltpu.roll(rim, domain_count - 1, 0)
        lines_ref = ref["lines"]
        full_y = along_y.shape[1]
        columns = [slice(t * 128, t * 128 + 128) for t in range(full_y // 128)]
        for t, column in enumerate(columns):
            lines_ref[t] = along_y[:, column]
            lines_ref[t, every16(15), :] = lines_ref[t, every16(15), :] + rim[:, column]
        lines = jnp.concatenate([lines_ref[t] for t in range(len(columns))], axis=1)
        spectrum = dot_split(x_table, split(lines), dot)
        half = lines.shape[0] // 2
        top = ref["gain"][0:half, :]
        first_row = lax.broadcasted_iota(jnp.int32, (half, full_y), 0) == 0
        bottom = jnp.where(first_row, ref["gain"][half : half + 1, :], top)
        filtered = jnp.concatenate([spectrum[0:half] * top, spectrum[half:] * bottom], axis=0)
        lines = dot_split(xt_table, split(filtered), dot)
        for t, column in enumerate(columns):
            lines_ref[t] = lines[:, column]
        rim = jnp.concatenate(
            [lines_ref[t, every16(15), :] for t in range(len(columns))], axis=1
        )
        rim = pltpu.roll(rim, 1, 0)
        values = dot_left(lines, y_table(0), dot_nt)
        low_rim = dot_left(rim, y_table(1), dot_nt)
        high_rim = dot_left(rim, y_table(2), dot_nt)
        marks = at_marks(position, three_parts(mean))
        for t in range(inner_count):
            grid[t] = values[:, tiles[t]]
            grid[t, every16(0), :] = grid[t, every16(0), :] + low_rim[:, tiles[t]]
            grid[t, every16(1), :] = grid[t, every16(1), :] + high_rim[:, tiles[t]]
            grid[t, every16(2), :] = grid[t, every16(2), :] + marks
            answer[:, tiles[t]] = grid[t].astype(BF16)

        def back_start(k):
            t = lax.rem(me + k, devices)
            pltpu.make_async_remote_copy(
                src_ref=answer.at[rows16(t // inner_count), lanes128(lax.rem(t, inner_count))],
                dst_ref=back.at[rows16(my_plane), :],
                send_sem=ref["back_send"],
                recv_sem=ref["back_recv"],
                device_id=device(t),
                device_id_type=MESH,
            ).start()

        several(1, devices, 7, back_start)
        pltpu.make_async_copy(
            answer.at[rows16(d), lanes128(i)], back.at[rows16(my_plane), :], ref["back_recv"]
        ).start()

    wait_bytes(back, ref["back_recv"])
    given = back[...]
    main, low, high = y_parts(0), y_parts(1), y_parts(2)
    product[...] = dot(given, main[0]) + dot(given, main[1])
    back32 = patch32
    back32[...] = given.astype(F32)
    mean = jnp.sum(jnp.where(position >= 125, back32[2:3, :], 0.0), axis=1, keepdims=True)
    at_low = back32[pl.ds(0, PLANES, 16), :].astype(BF16)
    at_high = back32[pl.ds(1, PLANES, 16), :].astype(BF16)
    at_rim = dot(at_low, low[0]) + dot(at_low, low[1])
    at_rim = at_rim + dot(at_high, high[0]) + dot(at_high, high[1])
    gathered = jnp.zeros((8, atoms), F32)
    for r in range(PLANES):
        piece = (
            product[16 * r : 16 * r + 8, :] * sten[0:8]
            + product[16 * r + 8 : 16 * r + 16, :] * sten[8:16]
        )
        gathered = gathered + piece * waves[r : r + 1]
    value = jnp.sum(gathered, axis=0, keepdims=True) + rim_x * jnp.sum(
        at_rim * waves[:PLANES], axis=0, keepdims=True
    )
    ref["out"][0:1] = energy + 0.5 * (latent - mean) * value
    ref["out"][1:2] = value

    sent = ref["sent"]
    for sem in (ref["ones_send"], ref["patch_send"]):

        @pl.when(owns)
        def _():
            wait_bytes(sent.at[0 : (PLANES - 1) * 16], sem)

        @pl.when(jnp.logical_not(owns))
        def _():
            wait_bytes(sent.at[0 : PLANES * 16], sem)

    @pl.when(owns)
    def _():
        wait_bytes(sent.at[0 : (devices - 1) * 16], ref["back_send"])


def part_kernel(both_ref, energy_ref, potential_ref):
    energy_ref[0] = both_ref[0:1, :]
    potential_ref[0] = both_ref[1:2, :]


def local(
    counts,
    atom_cells,
    atom_frac,
    species,
    nbr_index,
    nbr_count,
    embed,
    radial_in,
    radial_out,
    mix_weight,
    product_weight,
    read_weight,
    charge_weight,
):
    planes = (16, 64)
    devices = counts[0] * counts[1]
    tables = host_tables(*counts, *planes, 256)
    operands = dict(
        cells=atom_cells.transpose(2, 0, 1, 3)[:, 0],
        frac=atom_frac.transpose(2, 0, 1, 3)[:, 0],
        species=species,
        nbr=nbr_index[0, 0].T,
        count=nbr_count[0],
        embed=embed,
        win=radial_in[0],
        wout=radial_out[0],
        mix=mix_weight[0],
        prod=product_weight[0],
        read=read_weight,
        charge=charge_weight[None],
        **{name: jnp.asarray(tables[name]) for name in ("zeta", "y", "x", "xt", "gain")},
    )
    slots, atoms = operands["nbr"].shape
    channels = embed.shape[1]
    hidden = radial_in.shape[-1]
    full_x, full_y, lanes = counts[0] * planes[0], counts[1] * planes[1], counts[1] * 128
    dma = pltpu.SemaphoreType.DMA
    scratch = {
        name: VMEM(value.shape[1:] if name == "gain" else value.shape, value.dtype)
        for name, value in operands.items()
    }
    scratch.update(
        mine=VMEM((8, atoms), F32),
        ext=VMEM((9, 8, atoms), F32),
        placed=VMEM((9, 8, atoms), F32),
        found=VMEM((4, atoms // 128 * slots, 128), F32),
        weight=VMEM((8, 72, 256), F32),
        basis=VMEM((8, 64, 256), F32),
        kinds=VMEM((8, 8, 256), F32),
        moments=VMEM((9, atoms, 8 * hidden), BF16),
        win_wide=VMEM((8 * hidden, 64), BF16),
        pair=VMEM((3, 8 * hidden, channels), BF16),
        shuffle=VMEM((atoms, atoms), BF16),
        own_state=VMEM((atoms, channels), F32),
        sten_x=VMEM((16, atoms), F32),
        sten_y=VMEM((6, 128, atoms), BF16),
        waves=VMEM((72, atoms), F32),
        product=VMEM((PLANES * 16, atoms), F32),
        patch32=VMEM((PLANES * 16, 128), F32),
        ones_patch=VMEM((PLANES * 16, 128), BF16),
        patch=VMEM((PLANES * 16, 128), BF16),
        ones=VMEM((full_x, lanes), BF16),
        received=VMEM((full_x, lanes), BF16),
        grid=VMEM((counts[1], full_x, 128), F32),
        coefficient=VMEM((counts[1], counts[0], 128), F32),
        lines=VMEM((full_y // 128, full_x, 128), F32),
        x_parts=VMEM((2, full_x, full_x), BF16),
        xt_parts=VMEM((2, full_x, full_x), BF16),
        y_parts=VMEM((2, 3, lanes, full_y), BF16),
        answer=VMEM((full_x, lanes), BF16),
        back=VMEM((PLANES * 16, 128), BF16),
        sent=VMEM(((devices - 1) * 16, 128), BF16),
        fetch_sem=dma((len(operands),)),
        ext_send=dma((8,)),
        ext_recv=dma((8,)),
        ones_send=dma,
        ones_recv=dma,
        patch_send=dma,
        patch_recv=dma,
        back_send=dma,
        back_recv=dma,
    )
    names = [name + "_in" for name in operands] + ["out"] + list(scratch)
    vmem = pl.BlockSpec(memory_space=VMEM)
    both = pl.pallas_call(
        functools.partial(program_kernel, counts, planes, names),
        out_shape=jax.ShapeDtypeStruct((2, atoms), F32),
        in_specs=[pl.BlockSpec(memory_space=pl.ANY)] * len(operands),
        out_specs=vmem,
        scratch_shapes=list(scratch.values()),
        compiler_params=pltpu.CompilerParams(
            collective_id=0, has_side_effects=True, vmem_limit_bytes=58 << 20
        ),
        name="potential",
    )(*operands.values())
    return tuple(
        pl.pallas_call(
            part_kernel,
            out_shape=[jax.ShapeDtypeStruct((1, 1, atoms), F32)] * 2,
            in_specs=[vmem],
            out_specs=[vmem] * 2,
            name="outputs",
        )(both)
    )


def solution(mesh):
    counts = (mesh.shape["domain"], mesh.shape["inner"])
    in_specs = (
        P("domain", "inner", None, None),
        P("domain", "inner", None, None),
        P("domain", "inner", None),
        P("domain", "inner", None, None),
        P("domain", "inner", None),
        P(),
        P(),
        P(),
        P(),
        P(),
        P(),
        P(),
    )
    out_specs = (P("domain", "inner", None), P("domain", "inner", None))
    return jax.shard_map(
        functools.partial(local, counts),
        mesh=mesh,
        in_specs=in_specs,
        out_specs=out_specs,
        check_vma=False,
    )
```

```python
import functools
import math

import jax
import jax.numpy as jnp
import numpy as np
from jax import lax
from jax.experimental import pallas as pl
from jax.experimental.pallas import tpu as pltpu
from jax.sharding import PartitionSpec as P

MESH = pl.DeviceIdType.MESH
VMEM = pltpu.VMEM
F32 = jnp.float32
BF16 = jnp.bfloat16

spacing = 0.55
cutoff = 5.0
smearing = 0.2
coulomb = 14.399645
neighbour_scale = 0.25

Z_LOW = 111
Z_SPAN = 33
PLANES = 2 * Z_SPAN
ROW_LOW = 504 // 128
ROW_HIGH = 4103 // 128

DEGREE = (0, 1, 1, 1, 2, 2, 2, 2, 2)


def dot(a, b):
    return lax.dot_general(a, b, (((1,), (0,)), ((), ())), preferred_element_type=F32)


def dot_nt(a, b):
    return lax.dot_general(a, b, (((1,), (1,)), ((), ())), preferred_element_type=F32)


def split(x):
    high = x.astype(BF16)
    return high, (x - high.astype(F32)).astype(BF16)


def dot_left(a, b, form):
    rounded = a.astype(BF16)
    return form(rounded, b[0]) + form(rounded, b[1])


def dot_split(a, b, form):
    return form(a[0], b[0]) + (form(a[0], b[1]) + form(a[1], b[0]))


def three_parts(x):
    first = x.astype(BF16).astype(F32)
    second = (x - first).astype(BF16).astype(F32)
    third = (x - first - second).astype(BF16).astype(F32)
    return first, second, third


def basis_rows(length, positions):
    half = length // 2
    k = np.arange(half)
    angle = 2.0 * np.pi * ((k[:, None] * positions[None, :]) % length) / length
    cosine = np.cos(angle)
    sine = np.sin(angle)
    sine[0] = np.cos(np.pi * positions)
    return np.concatenate([cosine, sine], axis=0)


@functools.lru_cache(maxsize=None)
def host_tables(domain_count, inner_count, planes_x, planes_y, depth):
    full_x = planes_x * domain_count
    full_y = planes_y * inner_count
    table_x = basis_rows(full_x, np.arange(full_x))
    table_y = np.zeros((inner_count, 128, 3, full_y))
    for i in range(inner_count):
        all_y = basis_rows(full_y, (planes_y * i - 1 + np.arange(planes_y + 1)) % full_y).T
        table_y[i, : planes_y + 1, 0] = all_y
        table_y[i, 65:98, 1] = all_y[:33]
        table_y[i, 65:97, 2] = all_y[33:]
    table_y = table_y.transpose(2, 0, 1, 3).reshape(3, inner_count * 128, full_y)

    def squared_freq(length, count):
        return (np.arange(count) / (length * spacing)) ** 2

    def modulus(length, count):
        return (2.0 + np.cos(2.0 * np.pi * np.arange(count) / length)) ** 2 / 9.0

    def twice(length, count):
        k = np.arange(count)
        return np.where((k == 0) | (k == length // 2), 1.0, 2.0)

    cx, cy, cz = full_x // 2 + 1, full_y // 2 + 1, depth // 2 + 1
    squared = (
        squared_freq(full_x, cx)[:, None, None]
        + squared_freq(full_y, cy)[None, :, None]
        + squared_freq(depth, cz)[None, None, :]
    )
    safe = np.where(squared > 0.0, squared, 1.0)
    moduli = (
        modulus(full_x, cx)[:, None, None]
        * modulus(full_y, cy)[None, :, None]
        * modulus(depth, cz)[None, None, :]
    )
    volume = full_x * full_y * depth * spacing**3
    kernel = (
        coulomb
        * np.exp(-2.0 * np.pi**2 * smearing**2 * squared)
        / (np.pi * volume * safe * moduli)
    )
    kernel = np.where(squared > 0.0, kernel, 0.0)
    kernel = kernel * twice(full_x, cx)[:, None, None] * twice(full_y, cy)[None, :, None]
    step = np.arange(Z_SPAN)
    along = np.cos(2.0 * np.pi * np.arange(cz)[:, None] * step[None, :] / depth)
    along = along * twice(depth, cz)[:, None]
    wave = np.cos(np.pi * (2 * np.arange(Z_SPAN)[None, :] + 1) * step[:, None] / (2 * Z_SPAN))
    wave = wave * np.where(step == 0, 1.0, 2.0)[:, None] / Z_SPAN
    gain = np.moveaxis(kernel @ (along @ wave), 2, 0)
    order_y = np.concatenate([np.arange(full_y // 2), [full_y // 2], np.arange(1, full_y // 2)])
    gain = gain[:, :, order_y]
    half = full_x // 2
    padded = np.zeros((Z_SPAN, half + 8, full_y), np.float32)
    padded[:, :half] = gain[:, :half]
    padded[:, half] = gain[:, half]
    plane = np.arange(PLANES)
    angle = (
        np.pi * (2 * (plane // 2)[:, None] + 1) * np.arange(40)[None, :] / (2 * Z_SPAN)
    )
    zeta = np.where(plane[:, None] % 2 == 0, np.cos(angle), np.sin(angle))
    zeta[:, Z_SPAN:] = 0.0
    zeta_full = np.zeros((72, 40), np.float32)
    zeta_full[:PLANES] = zeta
    return dict(
        x=table_x.astype(np.float32),
        xt=np.ascontiguousarray(table_x.T).astype(np.float32),
        y=table_y.astype(np.float32),
        gain=padded,
        zeta=zeta_full,
    )


def half_tanh_silu(x):
    half = 0.5 * x
    return half + half * jnp.tanh(half)


def shuffle_matrix(atoms):
    row = lax.broadcasted_iota(jnp.int32, (atoms, atoms), 0)
    column = lax.broadcasted_iota(jnp.int32, (atoms, atoms), 1)
    return (column == row // 8 + (row % 8) * (atoms // 8)).astype(F32).astype(BF16)


def message_weights(species, embed_ref, win_ref, wout_ref, win_wide, pair, shuffle, own_state):
    kinds, channels = embed_ref.shape
    inputs, hidden = win_ref.shape
    atoms = species.shape[1]
    spread_in = (
        lax.broadcasted_iota(jnp.int32, (8, 64), 1) // 8
        == lax.broadcasted_iota(jnp.int32, (8, 64), 0)
    ).astype(F32).astype(BF16)
    wide = dot(win_ref[...].astype(F32).T.astype(BF16), spread_in)
    full = jnp.concatenate([wide] * 8, axis=0)
    row = lax.broadcasted_iota(jnp.int32, full.shape, 0) // hidden
    column = lax.broadcasted_iota(jnp.int32, full.shape, 1) % 8
    win_wide[...] = jnp.where(row == column, full, 0.0).astype(BF16)
    embed = embed_ref[...].astype(F32)
    out = wout_ref[...].astype(F32)
    for degree in range(3):
        part = out[:, degree * channels : (degree + 1) * channels]
        for s in range(kinds):
            pair[degree, s * hidden : (s + 1) * hidden, :] = (part * embed[s : s + 1]).astype(BF16)
    shuffle[...] = shuffle_matrix(atoms)
    kind = lax.broadcasted_iota(jnp.int32, (128, atoms), 0)
    marks = (kind == species).astype(F32).T.astype(BF16)
    padded = jnp.concatenate([embed, jnp.zeros((128 - kinds, channels), F32)], axis=0)
    own_state[...] = dot(shuffle[...], dot(marks, padded.astype(BF16)).astype(BF16))


def message_rows(
    planes,
    ext_ref,
    nbr_ref,
    count_ref,
    mix_ref,
    prod_ref,
    read_ref,
    charge_ref,
    win_wide,
    pair,
    shuffle,
    own_state,
    placed,
    found,
    weight,
    basis,
    kinds,
    moments,
):
    atoms = ext_ref.shape[-1]
    slots = nbr_ref.shape[0]
    tiles = atoms // 128
    channels = mix_ref.shape[-1]
    hidden_size = pair.shape[1] // 8
    for b in range(9):
        row = lax.broadcasted_iota(jnp.int32, (8, atoms), 0)
        shift = jnp.where(
            row == 0, planes[0] * (b // 3 - 1.0), jnp.where(row == 1, planes[1] * (b % 3 - 1.0), 0.0)
        )
        block = ext_ref[b] + shift
        placed[b] = jnp.where(row == 0, block + 64.0 * ext_ref[b, 3:4, :], block)

    def gather(t, carry):
        rows = pl.ds(pl.multiple_of((t // tiles) * 8, 8), 8)
        lanes = pl.ds(pl.multiple_of((t % tiles) * 128, 128), 128)
        index = nbr_ref[rows, lanes]
        low = index & 127
        high = index >> 7
        values = [jnp.zeros((8, 128), F32) for _ in range(3)]
        for r in range(ROW_LOW, ROW_HIGH + 1):
            here = high == r
            piece = slice((r % tiles) * 128, (r % tiles) * 128 + 128)
            for c in range(3):
                line = jnp.broadcast_to(placed[r // tiles, c : c + 1, piece], (8, 128))
                picked = jnp.take_along_axis(line, low, axis=1)
                values[c] = jnp.where(here, picked, values[c])
        into = pl.ds(pl.multiple_of((t % tiles) * slots + (t // tiles) * 8, 8), 8)
        kind = jnp.floor((values[0] + 32.0) * (1.0 / 64.0))
        found[0, into, :] = values[0] - 64.0 * kind
        found[1, into, :] = values[1]
        found[2, into, :] = values[2]
        found[3, into, :] = kind
        return carry

    lax.fori_loop(0, (slots // 8) * tiles, gather, 0, unroll=2)

    own = ext_ref[4]
    slot = lax.broadcasted_iota(jnp.int32, (slots, 128), 0)
    parts = []
    for c in range(4):
        pieces = []
        for j in range(tiles):
            lanes = slice(j * 128, j * 128 + 128)
            value = found[c, slots * j : slots * j + slots, :]
            if c < 3:
                value = (value - own[c : c + 1, lanes]) * spacing
            else:
                value = jnp.where(slot < count_ref[0:1, lanes], value, 8.0)
            pieces.append(value)
        parts.append(jnp.concatenate(pieces, axis=0).T)
    dx, dy, dz, species = parts
    distance = jnp.sqrt(dx * dx + dy * dy + dz * dz)
    inverse = 1.0 / distance
    ux, uy, uz = dx * inverse, dy * inverse, dz * inverse
    scaled = distance * (1.0 / cutoff)
    scaled_sq = scaled * scaled
    six = scaled_sq * scaled_sq * scaled_sq
    envelope = 1.0 - 28.0 * six + 48.0 * six * scaled - 21.0 * six * scaled_sq
    envelope = jnp.where(scaled < 1.0, envelope * neighbour_scale, 0.0)
    r3, r5, r15 = math.sqrt(3.0), math.sqrt(5.0), math.sqrt(15.0)
    factors = (
        None,
        r3 * ux,
        r3 * uy,
        r3 * uz,
        r15 * ux * uy,
        r15 * uy * uz,
        0.5 * r5 * (3.0 * uz * uz - 1.0),
        r15 * ux * uz,
        0.5 * r15 * (ux * ux - uy * uy),
    )
    octets = 8

    def put(target, first, value):
        for o in range(octets):
            target[o, first : first + 8, 0:128] = value[8 * o : 8 * o + 8]
            target[o, first : first + 8, 128:256] = value[64 + 8 * o : 64 + 8 * o + 8]

    for m, factor in enumerate(factors):
        put(weight, 8 * m, envelope if factor is None else envelope * factor)
    put(kinds, 0, species)
    theta = (math.pi / cutoff) * distance
    sine = jnp.sin(theta)
    cosine = 2.0 * jnp.cos(theta)
    scale = math.sqrt(2.0 / cutoff) * inverse
    before = jnp.zeros_like(sine)
    for n in range(8):
        put(basis, 8 * n, scale * sine)
        sine, before = cosine * sine - before, sine

    lane = lax.broadcasted_iota(jnp.int32, (8, 256), 1)
    element = lax.broadcasted_iota(jnp.int32, (8, 256), 0)
    mine = ((lane % 128) // slots) * 2 + lane // 128 == element

    def octet(o, carry):
        hidden = dot(win_wide[...], basis[o].astype(BF16))
        hidden = half_tanh_silu(hidden).astype(BF16)
        for first in range(0, 8, 2):
            sums = []
            for i in (first, first + 1):
                near = hidden[i * hidden_size : (i + 1) * hidden_size]
                kind = kinds[o, i : i + 1, :]
                by_kind = []
                for s in range(8):
                    mark = jnp.broadcast_to((kind == float(s)).astype(F32), (16, 256)).astype(BF16)
                    by_kind.append(near * jnp.concatenate([mark] * (hidden_size // 16), axis=0))
                left = [
                    jnp.where(mine, jnp.broadcast_to(weight[o, 8 * m + i : 8 * m + i + 1, :], (8, 256)), 0.0)
                    for m in range(9)
                ]
                left = jnp.concatenate(left, axis=0).astype(BF16)
                sums.append(dot_nt(left, jnp.concatenate(by_kind, axis=0)))
            into = pl.ds(pl.multiple_of(64 * o + 8 * first, 16), 16)
            for m in range(9):
                both = jnp.concatenate([part[8 * m : 8 * m + 8] for part in sums], axis=0)
                moments[m, into, :] = both.astype(BF16)
        return carry

    lax.fori_loop(0, octets, octet, 0, unroll=2)

    invariants = []
    for degree, (first, last) in enumerate(((0, 1), (1, 4), (4, 9))):
        rows = moments[first:last].reshape((last - first) * atoms, moments.shape[2])
        aggregate = dot(rows, pair[degree]).astype(BF16)
        mixed = dot(aggregate, mix_ref[degree])
        if degree > 0:
            mixed = mixed * mixed
            mixed = sum(mixed[n * atoms : (n + 1) * atoms] for n in range(last - first))
        invariants.append(mixed)
    stacked = jnp.concatenate(invariants, axis=1).astype(BF16)
    update = dot(stacked, prod_ref[...])
    update = update / (1.0 + jnp.exp(-update))
    new_state = (own_state[...] + update).astype(BF16)
    readout = jnp.concatenate(
        [read_ref[...], charge_ref[...], jnp.zeros((14, channels), BF16)], axis=0
    )
    shuffled = dot_nt(readout, new_state)[0:2]
    stack = jnp.concatenate(three_parts(shuffled) + (jnp.zeros((10, atoms), F32),), axis=0)
    ordered = dot(stack.astype(BF16), shuffle[...])
    return ordered[0:2] + ordered[2:4] + ordered[4:6]


def spline_rows(fraction):
    rest = 1.0 - fraction
    square = fraction * fraction
    cube = square * fraction
    return (
        rest * rest * rest * (1.0 / 6.0),
        (3.0 * cube - 6.0 * square + 4.0) * (1.0 / 6.0),
        (-3.0 * cube + 3.0 * square + 3.0 * fraction + 1.0) * (1.0 / 6.0),
        cube * (1.0 / 6.0),
    )


def stencil_rows(rows, first, weights):
    at = lax.broadcasted_iota(jnp.int32, (rows, first.shape[1]), 0) - first
    out = jnp.where(at == 0, weights[0], 0.0)
    for j in range(1, 4):
        out = jnp.where(at == j, weights[j], out)
    return out


def at_marks(position, parts):
    out = jnp.where(position == 125, parts[0], 0.0)
    out = jnp.where(position == 126, parts[1], out)
    return jnp.where(position == 127, parts[2], out)


def several(first, last, unroll, step):
    def turn(n, carry):
        for k in range(unroll):
            step(first + n * unroll + k)
        return carry

    turns = (last - first) // unroll
    lax.fori_loop(0, turns, turn, 0)
    for k in range(first + turns * unroll, last):
        step(k)


WEIGHTS = ("embed", "win", "wout", "mix", "prod", "read", "charge")


def program_kernel(counts, planes, names, *refs):
    ref = dict(zip(names, refs))
    domain_count, inner_count = counts
    devices = domain_count * inner_count
    per_core = devices // 2
    d, i = lax.axis_index("domain"), lax.axis_index("inner")
    me = d * inner_count + i
    at = (d, i)
    slots, atoms = ref["nbr_in"].shape

    def device(t):
        return (t // inner_count, lax.rem(t, inner_count))

    def owner(r):
        rest = lax.rem(r, per_core)
        return (rest // 2, lax.rem(rest, 2) * 2 + r // per_core)

    my_plane = d * 2 + i // 2 + per_core * lax.rem(i, 2)
    owns = my_plane < PLANES

    def rows16(t):
        return pl.ds(pl.multiple_of(t * 16, 16), 16)

    def lanes128(t):
        return pl.ds(pl.multiple_of(t * 128, 128), 128)

    barrier = pltpu.get_barrier_semaphore()

    def greet(k):
        pl.semaphore_signal(
            barrier, inc=1, device_id=device(lax.rem(me + k, devices)), device_id_type=MESH
        )

    several(1, devices, 7, greet)

    def fetch(n, name):
        source = ref[name + "_in"]
        if name == "gain":
            source = source.at[jnp.minimum(my_plane, PLANES - 1) // 2]
        return pltpu.make_async_copy(source, ref[name], ref["fetch_sem"].at[n])

    fetched = ("cells", "frac", "species", "nbr", "count") + WEIGHTS
    fetched = fetched + ("zeta", "y", "x", "xt", "gain")
    fetches = {name: fetch(n, name) for n, name in enumerate(fetched)}
    for name in fetched:
        fetches[name].start()

    moves = [(dx, dy) for dx in (-1, 0, 1) for dy in (-1, 0, 1) if (dx, dy) != (0, 0)]
    mine, ext = ref["mine"], ref["ext"]
    for name in ("cells", "frac", "species"):
        fetches[name].wait()
    cell = [ref["cells"][c] for c in range(3)]
    fraction = [ref["frac"][c] for c in range(3)]
    mine[...] = jnp.zeros_like(mine)
    for c in range(3):
        mine[c : c + 1, :] = cell[c].astype(F32) + fraction[c]
    mine[3:4, :] = ref["species"][0].astype(F32)
    ext[4] = mine[...]

    weights = [spline_rows(f) for f in fraction]
    sten_x = stencil_rows(16, cell[0] - 1, weights[0])
    rim_x = jnp.where(cell[0] == 0, weights[0][0], 0.0)
    sten_z = stencil_rows(40, cell[2] - 1 - Z_LOW, weights[2])
    lane = lax.broadcasted_iota(jnp.int32, (128, atoms), 0)
    y_main = split(stencil_rows(128, cell[1], weights[1]))
    y_low = split(jnp.where(lane <= 97, stencil_rows(128, cell[1] + 65, weights[1]), 0.0))
    y_high = split(jnp.where(lane >= 65, stencil_rows(128, cell[1] + 32, weights[1]), 0.0))
    for n, part in enumerate(y_main + y_low + y_high):
        ref["sten_y"][n] = part
    fetches["zeta"].wait()
    waves = ref["waves"]
    waves[...] = jnp.dot(ref["zeta"][...], sten_z, precision=lax.Precision.HIGHEST)
    sten = ref["sten_x"]
    sten[...] = sten_x
    product, patch32 = ref["product"], ref["patch32"]

    def y_parts(n):
        return ref["sten_y"][2 * n], ref["sten_y"][2 * n + 1]

    def spread(charged):
        for r in range(PLANES):
            product[16 * r : 16 * r + 16, :] = sten[...] * charged[r : r + 1]
        patch32[...] = dot_left(product[...], y_parts(0), dot_nt)
        rim = charged * rim_x
        low = dot_left(rim, y_parts(1), dot_nt)
        high = dot_left(rim, y_parts(2), dot_nt)
        patch32[pl.ds(0, PLANES, 16), :] = patch32[pl.ds(0, PLANES, 16), :] + low[:PLANES]
        patch32[pl.ds(1, PLANES, 16), :] = patch32[pl.ds(1, PLANES, 16), :] + high[:PLANES]

    def to_owners(patch, received, send_sem, recv_sem):
        def start(k):
            r = lax.rem(my_plane + k, PLANES)
            pltpu.make_async_remote_copy(
                src_ref=patch.at[rows16(r), :],
                dst_ref=received.at[rows16(d), lanes128(i)],
                send_sem=send_sem,
                recv_sem=recv_sem,
                device_id=owner(r),
                device_id_type=MESH,
            ).start()

        several(1, PLANES, 5, start)

        @pl.when(jnp.logical_not(owns))
        def _():
            start(PLANES)

        @pl.when(owns)
        def _():
            pltpu.make_async_copy(
                patch.at[rows16(my_plane), :], received.at[rows16(d), lanes128(i)], recv_sem
            ).start()

    def wait_bytes(buffer, sem):
        pltpu.make_async_copy(buffer, buffer, sem).wait()

    spread(waves[...])
    ref["ones_patch"][...] = patch32[...].astype(BF16)
    for name, source in (("x", "x"), ("xt", "xt"), ("y", "y")):
        fetches[source].wait()
        for n, part in enumerate(split(ref[source][...])):
            ref[name + "_parts"][n] = part

    for name in ("nbr", "count") + WEIGHTS:
        fetches[name].wait()
    message_weights(
        ref["species"][0],
        *[ref[name] for name in ("embed", "win", "wout", "win_wide", "pair", "shuffle", "own_state")],
    )

    pl.semaphore_wait(barrier, devices - 1)
    copies = []
    for n, (dx, dy) in enumerate(moves):
        copy = pltpu.make_async_remote_copy(
            src_ref=mine,
            dst_ref=ext.at[(1 - dx) * 3 + (1 - dy)],
            send_sem=ref["ext_send"].at[n],
            recv_sem=ref["ext_recv"].at[n],
            device_id=tuple(
                lax.rem(at[a] + counts[a] + (dx, dy)[a], counts[a]) for a in range(2)
            ),
            device_id_type=MESH,
        )
        copy.start()
        copies.append(copy)
    to_owners(ref["ones_patch"], ref["ones"], ref["ones_send"], ref["ones_recv"])

    for copy in copies:
        copy.wait()
    rows = message_rows(
        planes,
        ext,
        *[
            ref[name]
            for name in (
                "nbr",
                "count",
                "mix",
                "prod",
                "read",
                "charge",
                "win_wide",
                "pair",
                "shuffle",
                "own_state",
                "placed",
                "found",
                "weight",
                "basis",
                "kinds",
                "moments",
            )
        ],
    )
    energy, latent = rows[0:1], rows[1:2]

    block_mean = jnp.sum(latent, axis=1, keepdims=True) / atoms
    spread(waves[...] * (latent - block_mean))
    position = lax.broadcasted_iota(jnp.int32, (1, 128), 1)
    marks = at_marks(position, three_parts(block_mean))
    patch32[pl.ds(2, PLANES, 16), :] = patch32[pl.ds(2, PLANES, 16), :] + marks
    ref["patch"][...] = patch32[...].astype(BF16)
    to_owners(ref["patch"], ref["received"], ref["patch_send"], ref["patch_recv"])

    fetches["gain"].wait()
    answer, back = ref["answer"], ref["back"]

    @pl.when(owns)
    def _():
        grid, coefficient = ref["grid"], ref["coefficient"]
        x_table = ref["x_parts"][0], ref["x_parts"][1]
        xt_table = ref["xt_parts"][0], ref["xt_parts"][1]

        def y_table(part):
            return ref["y_parts"][0, part], ref["y_parts"][1, part]

        def whole_rows(rows):
            return jnp.concatenate([grid[t, rows, :] for t in range(inner_count)], axis=1)

        def every16(first):
            return pl.ds(first, domain_count, 16)

        wait_bytes(ref["ones"], ref["ones_recv"])
        wait_bytes(ref["received"], ref["patch_recv"])
        tiles = [slice(t * 128, t * 128 + 128) for t in range(inner_count)]
        means = []
        for t in range(inner_count):
            grid[t] = ref["received"][:, tiles[t]].astype(F32)
            marked = grid[t, pl.ds(2, domain_count, 16), :]
            means.append(
                jnp.sum(jnp.where(position >= 125, marked, 0.0), axis=1, keepdims=True)
            )
        mean = jnp.sum(sum(means), axis=0, keepdims=True) / devices
        for t in range(inner_count):
            coefficient[t] = jnp.broadcast_to(means[t] - mean, (domain_count, 128))
            for b in range(domain_count):
                here = slice(16 * b, 16 * b + 16)
                unit = ref["ones"][here, tiles[t]].astype(F32)
                grid[t, here, :] = grid[t, here, :] + unit * coefficient[t, b : b + 1, :]
        along_y = dot_left(whole_rows(slice(None)), y_table(0), dot)
        rim = dot_left(whole_rows(every16(0)), y_table(1), dot)
        rim = rim + dot_left(whole_rows(every16(1)), y_table(2), dot)
        rim = pltpu.roll(rim, domain_count - 1, 0)
        lines_ref = ref["lines"]
        full_y = along_y.shape[1]
        columns = [slice(t * 128, t * 128 + 128) for t in range(full_y // 128)]
        for t, column in enumerate(columns):
            lines_ref[t] = along_y[:, column]
            lines_ref[t, every16(15), :] = lines_ref[t, every16(15), :] + rim[:, column]
        lines = jnp.concatenate([lines_ref[t] for t in range(len(columns))], axis=1)
        spectrum = dot_split(x_table, split(lines), dot)
        half = lines.shape[0] // 2
        top = ref["gain"][0:half, :]
        first_row = lax.broadcasted_iota(jnp.int32, (half, full_y), 0) == 0
        bottom = jnp.where(first_row, ref["gain"][half : half + 1, :], top)
        filtered = jnp.concatenate([spectrum[0:half] * top, spectrum[half:] * bottom], axis=0)
        lines = dot_split(xt_table, split(filtered), dot)
        for t, column in enumerate(columns):
            lines_ref[t] = lines[:, column]
        rim = jnp.concatenate(
            [lines_ref[t, every16(15), :] for t in range(len(columns))], axis=1
        )
        rim = pltpu.roll(rim, 1, 0)
        values = dot_left(lines, y_table(0), dot_nt)
        low_rim = dot_left(rim, y_table(1), dot_nt)
        high_rim = dot_left(rim, y_table(2), dot_nt)
        marks = at_marks(position, three_parts(mean))
        for t in range(inner_count):
            grid[t] = values[:, tiles[t]]
            grid[t, every16(0), :] = grid[t, every16(0), :] + low_rim[:, tiles[t]]
            grid[t, every16(1), :] = grid[t, every16(1), :] + high_rim[:, tiles[t]]
            grid[t, every16(2), :] = grid[t, every16(2), :] + marks
            answer[:, tiles[t]] = grid[t].astype(BF16)

        def back_start(k):
            t = lax.rem(me + k, devices)
            pltpu.make_async_remote_copy(
                src_ref=answer.at[rows16(t // inner_count), lanes128(lax.rem(t, inner_count))],
                dst_ref=back.at[rows16(my_plane), :],
                send_sem=ref["back_send"],
                recv_sem=ref["back_recv"],
                device_id=device(t),
                device_id_type=MESH,
            ).start()

        several(1, devices, 7, back_start)
        pltpu.make_async_copy(
            answer.at[rows16(d), lanes128(i)], back.at[rows16(my_plane), :], ref["back_recv"]
        ).start()

    wait_bytes(back, ref["back_recv"])
    given = back[...]
    main, low, high = y_parts(0), y_parts(1), y_parts(2)
    product[...] = dot(given, main[0]) + dot(given, main[1])
    back32 = patch32
    back32[...] = given.astype(F32)
    mean = jnp.sum(jnp.where(position >= 125, back32[2:3, :], 0.0), axis=1, keepdims=True)
    at_low = back32[pl.ds(0, PLANES, 16), :].astype(BF16)
    at_high = back32[pl.ds(1, PLANES, 16), :].astype(BF16)
    at_rim = dot(at_low, low[0]) + dot(at_low, low[1])
    at_rim = at_rim + dot(at_high, high[0]) + dot(at_high, high[1])
    gathered = jnp.zeros((8, atoms), F32)
    for r in range(PLANES):
        piece = (
            product[16 * r : 16 * r + 8, :] * sten[0:8]
            + product[16 * r + 8 : 16 * r + 16, :] * sten[8:16]
        )
        gathered = gathered + piece * waves[r : r + 1]
    value = jnp.sum(gathered, axis=0, keepdims=True) + rim_x * jnp.sum(
        at_rim * waves[:PLANES], axis=0, keepdims=True
    )
    ref["out"][0:1] = energy + 0.5 * (latent - mean) * value
    ref["out"][1:2] = value

    sent = ref["sent"]
    for sem in (ref["ones_send"], ref["patch_send"]):

        @pl.when(owns)
        def _():
            wait_bytes(sent.at[0 : (PLANES - 1) * 16], sem)

        @pl.when(jnp.logical_not(owns))
        def _():
            wait_bytes(sent.at[0 : PLANES * 16], sem)

    @pl.when(owns)
    def _():
        wait_bytes(sent.at[0 : (devices - 1) * 16], ref["back_send"])


def part_kernel(both_ref, energy_ref, potential_ref):
    energy_ref[0] = both_ref[0:1, :]
    potential_ref[0] = both_ref[1:2, :]


def local(
    counts,
    atom_cells,
    atom_frac,
    species,
    nbr_index,
    nbr_count,
    embed,
    radial_in,
    radial_out,
    mix_weight,
    product_weight,
    read_weight,
    charge_weight,
):
    planes = (16, 64)
    devices = counts[0] * counts[1]
    tables = host_tables(*counts, *planes, 256)
    operands = dict(
        cells=atom_cells.transpose(2, 0, 1, 3)[:, 0],
        frac=atom_frac.transpose(2, 0, 1, 3)[:, 0],
        species=species,
        nbr=nbr_index[0, 0].T,
        count=nbr_count[0],
        embed=embed,
        win=radial_in[0],
        wout=radial_out[0],
        mix=mix_weight[0],
        prod=product_weight[0],
        read=read_weight,
        charge=charge_weight[None],
        **{name: jnp.asarray(tables[name]) for name in ("zeta", "y", "x", "xt", "gain")},
    )
    slots, atoms = operands["nbr"].shape
    channels = embed.shape[1]
    hidden = radial_in.shape[-1]
    full_x, full_y, lanes = counts[0] * planes[0], counts[1] * planes[1], counts[1] * 128
    dma = pltpu.SemaphoreType.DMA
    scratch = {
        name: VMEM(value.shape[1:] if name == "gain" else value.shape, value.dtype)
        for name, value in operands.items()
    }
    scratch.update(
        mine=VMEM((8, atoms), F32),
        ext=VMEM((9, 8, atoms), F32),
        placed=VMEM((9, 8, atoms), F32),
        found=VMEM((4, atoms // 128 * slots, 128), F32),
        weight=VMEM((8, 72, 256), F32),
        basis=VMEM((8, 64, 256), F32),
        kinds=VMEM((8, 8, 256), F32),
        moments=VMEM((9, atoms, 8 * hidden), BF16),
        win_wide=VMEM((8 * hidden, 64), BF16),
        pair=VMEM((3, 8 * hidden, channels), BF16),
        shuffle=VMEM((atoms, atoms), BF16),
        own_state=VMEM((atoms, channels), F32),
        sten_x=VMEM((16, atoms), F32),
        sten_y=VMEM((6, 128, atoms), BF16),
        waves=VMEM((72, atoms), F32),
        product=VMEM((PLANES * 16, atoms), F32),
        patch32=VMEM((PLANES * 16, 128), F32),
        ones_patch=VMEM((PLANES * 16, 128), BF16),
        patch=VMEM((PLANES * 16, 128), BF16),
        ones=VMEM((full_x, lanes), BF16),
        received=VMEM((full_x, lanes), BF16),
        grid=VMEM((counts[1], full_x, 128), F32),
        coefficient=VMEM((counts[1], counts[0], 128), F32),
        lines=VMEM((full_y // 128, full_x, 128), F32),
        x_parts=VMEM((2, full_x, full_x), BF16),
        xt_parts=VMEM((2, full_x, full_x), BF16),
        y_parts=VMEM((2, 3, lanes, full_y), BF16),
        answer=VMEM((full_x, lanes), BF16),
        back=VMEM((PLANES * 16, 128), BF16),
        sent=VMEM(((devices - 1) * 16, 128), BF16),
        fetch_sem=dma((len(operands),)),
        ext_send=dma((8,)),
        ext_recv=dma((8,)),
        ones_send=dma,
        ones_recv=dma,
        patch_send=dma,
        patch_recv=dma,
        back_send=dma,
        back_recv=dma,
    )
    names = [name + "_in" for name in operands] + ["out"] + list(scratch)
    vmem = pl.BlockSpec(memory_space=VMEM)
    both = pl.pallas_call(
        functools.partial(program_kernel, counts, planes, names),
        out_shape=jax.ShapeDtypeStruct((2, atoms), F32),
        in_specs=[pl.BlockSpec(memory_space=pl.ANY)] * len(operands),
        out_specs=vmem,
        scratch_shapes=list(scratch.values()),
        compiler_params=pltpu.CompilerParams(
            collective_id=0, has_side_effects=True, vmem_limit_bytes=58 << 20
        ),
        name="potential",
    )(*operands.values())
    return tuple(
        pl.pallas_call(
            part_kernel,
            out_shape=[jax.ShapeDtypeStruct((1, 1, atoms), F32)] * 2,
            in_specs=[vmem],
            out_specs=[vmem] * 2,
            name="outputs",
        )(both)
    )


def solution(mesh):
    counts = (mesh.shape["domain"], mesh.shape["inner"])
    in_specs = (
        P("domain", "inner", None, None),
        P("domain", "inner", None, None),
        P("domain", "inner", None),
        P("domain", "inner", None, None),
        P("domain", "inner", None),
        P(),
        P(),
        P(),
        P(),
        P(),
        P(),
        P(),
    )
    out_specs = (P("domain", "inner", None), P("domain", "inner", None))
    return jax.shard_map(
        functools.partial(local, counts),
        mesh=mesh,
        in_specs=in_specs,
        out_specs=out_specs,
        check_vma=False,
    )
```

```python
import functools
import math

import jax
import jax.numpy as jnp
import numpy as np
from jax import lax
from jax.experimental import pallas as pl
from jax.experimental.pallas import tpu as pltpu
from jax.sharding import PartitionSpec as P

MESH = pl.DeviceIdType.MESH
VMEM = pltpu.VMEM
F32 = jnp.float32
BF16 = jnp.bfloat16

spacing = 0.55
cutoff = 5.0
smearing = 0.2
coulomb = 14.399645
neighbour_scale = 0.25

Z_LOW = 111
Z_SPAN = 33
PLANES = 2 * Z_SPAN
ROW_LOW = 504 // 128
ROW_HIGH = 4103 // 128

DEGREE = (0, 1, 1, 1, 2, 2, 2, 2, 2)


def dot(a, b):
    return lax.dot_general(a, b, (((1,), (0,)), ((), ())), preferred_element_type=F32)


def dot_nt(a, b):
    return lax.dot_general(a, b, (((1,), (1,)), ((), ())), preferred_element_type=F32)


def split(x):
    high = x.astype(BF16)
    return high, (x - high.astype(F32)).astype(BF16)


def dot_left(a, b, form):
    rounded = a.astype(BF16)
    return form(rounded, b[0]) + form(rounded, b[1])


def dot_split(a, b, form):
    return form(a[0], b[0]) + (form(a[0], b[1]) + form(a[1], b[0]))


def three_parts(x):
    first = x.astype(BF16).astype(F32)
    second = (x - first).astype(BF16).astype(F32)
    third = (x - first - second).astype(BF16).astype(F32)
    return first, second, third


def basis_rows(length, positions):
    half = length // 2
    k = np.arange(half)
    angle = 2.0 * np.pi * ((k[:, None] * positions[None, :]) % length) / length
    cosine = np.cos(angle)
    sine = np.sin(angle)
    sine[0] = np.cos(np.pi * positions)
    return np.concatenate([cosine, sine], axis=0)


@functools.lru_cache(maxsize=None)
def host_tables(domain_count, inner_count, planes_x, planes_y, depth):
    full_x = planes_x * domain_count
    full_y = planes_y * inner_count
    table_x = basis_rows(full_x, np.arange(full_x))
    table_y = np.zeros((inner_count, 128, 3, full_y))
    for i in range(inner_count):
        all_y = basis_rows(full_y, (planes_y * i - 1 + np.arange(planes_y + 1)) % full_y).T
        table_y[i, : planes_y + 1, 0] = all_y
        table_y[i, 65:98, 1] = all_y[:33]
        table_y[i, 65:97, 2] = all_y[33:]
    table_y = table_y.transpose(2, 0, 1, 3).reshape(3, inner_count * 128, full_y)

    def squared_freq(length, count):
        return (np.arange(count) / (length * spacing)) ** 2

    def modulus(length, count):
        return (2.0 + np.cos(2.0 * np.pi * np.arange(count) / length)) ** 2 / 9.0

    def twice(length, count):
        k = np.arange(count)
        return np.where((k == 0) | (k == length // 2), 1.0, 2.0)

    cx, cy, cz = full_x // 2 + 1, full_y // 2 + 1, depth // 2 + 1
    squared = (
        squared_freq(full_x, cx)[:, None, None]
        + squared_freq(full_y, cy)[None, :, None]
        + squared_freq(depth, cz)[None, None, :]
    )
    safe = np.where(squared > 0.0, squared, 1.0)
    moduli = (
        modulus(full_x, cx)[:, None, None]
        * modulus(full_y, cy)[None, :, None]
        * modulus(depth, cz)[None, None, :]
    )
    volume = full_x * full_y * depth * spacing**3
    kernel = (
        coulomb
        * np.exp(-2.0 * np.pi**2 * smearing**2 * squared)
        / (np.pi * volume * safe * moduli)
    )
    kernel = np.where(squared > 0.0, kernel, 0.0)
    kernel = kernel * twice(full_x, cx)[:, None, None] * twice(full_y, cy)[None, :, None]
    step = np.arange(Z_SPAN)
    along = np.cos(2.0 * np.pi * np.arange(cz)[:, None] * step[None, :] / depth)
    along = along * twice(depth, cz)[:, None]
    wave = np.cos(np.pi * (2 * np.arange(Z_SPAN)[None, :] + 1) * step[:, None] / (2 * Z_SPAN))
    wave = wave * np.where(step == 0, 1.0, 2.0)[:, None] / Z_SPAN
    gain = np.moveaxis(kernel @ (along @ wave), 2, 0)
    order_y = np.concatenate([np.arange(full_y // 2), [full_y // 2], np.arange(1, full_y // 2)])
    gain = gain[:, :, order_y]
    half = full_x // 2
    padded = np.zeros((Z_SPAN, half + 8, full_y), np.float32)
    padded[:, :half] = gain[:, :half]
    padded[:, half] = gain[:, half]
    plane = np.arange(PLANES)
    angle = (
        np.pi * (2 * (plane // 2)[:, None] + 1) * np.arange(40)[None, :] / (2 * Z_SPAN)
    )
    zeta = np.where(plane[:, None] % 2 == 0, np.cos(angle), np.sin(angle))
    zeta[:, Z_SPAN:] = 0.0
    zeta_full = np.zeros((72, 40), np.float32)
    zeta_full[:PLANES] = zeta
    return dict(
        x=table_x.astype(np.float32),
        xt=np.ascontiguousarray(table_x.T).astype(np.float32),
        y=table_y.astype(np.float32),
        gain=padded,
        zeta=zeta_full,
    )


def half_tanh_silu(x):
    half = 0.5 * x
    return half + half * jnp.tanh(half)


def shuffle_matrix(atoms):
    row = lax.broadcasted_iota(jnp.int32, (atoms, atoms), 0)
    column = lax.broadcasted_iota(jnp.int32, (atoms, atoms), 1)
    return (column == row // 8 + (row % 8) * (atoms // 8)).astype(F32).astype(BF16)


def message_weights(species, embed_ref, win_ref, wout_ref, win_wide, pair, shuffle, own_state):
    kinds, channels = embed_ref.shape
    inputs, hidden = win_ref.shape
    atoms = species.shape[1]
    spread_in = (
        lax.broadcasted_iota(jnp.int32, (8, 64), 1) // 8
        == lax.broadcasted_iota(jnp.int32, (8, 64), 0)
    ).astype(F32).astype(BF16)
    wide = dot(win_ref[...].astype(F32).T.astype(BF16), spread_in)
    full = jnp.concatenate([wide] * 8, axis=0)
    row = lax.broadcasted_iota(jnp.int32, full.shape, 0) // hidden
    column = lax.broadcasted_iota(jnp.int32, full.shape, 1) % 8
    win_wide[...] = jnp.where(row == column, full, 0.0).astype(BF16)
    embed = embed_ref[...].astype(F32)
    out = wout_ref[...].astype(F32)
    for degree in range(3):
        part = out[:, degree * channels : (degree + 1) * channels]
        for s in range(kinds):
            pair[degree, s * hidden : (s + 1) * hidden, :] = (part * embed[s : s + 1]).astype(BF16)
    shuffle[...] = shuffle_matrix(atoms)
    kind = lax.broadcasted_iota(jnp.int32, (128, atoms), 0)
    marks = (kind == species).astype(F32).T.astype(BF16)
    padded = jnp.concatenate([embed, jnp.zeros((128 - kinds, channels), F32)], axis=0)
    own_state[...] = dot(shuffle[...], dot(marks, padded.astype(BF16)).astype(BF16))


def message_rows(
    planes,
    ext_ref,
    nbr_ref,
    count_ref,
    mix_ref,
    prod_ref,
    read_ref,
    charge_ref,
    win_wide,
    pair,
    shuffle,
    own_state,
    placed,
    found,
    weight,
    basis,
    kinds,
    moments,
):
    atoms = ext_ref.shape[-1]
    slots = nbr_ref.shape[0]
    tiles = atoms // 128
    channels = mix_ref.shape[-1]
    hidden_size = pair.shape[1] // 8
    for b in range(9):
        row = lax.broadcasted_iota(jnp.int32, (8, atoms), 0)
        shift = jnp.where(
            row == 0, planes[0] * (b // 3 - 1.0), jnp.where(row == 1, planes[1] * (b % 3 - 1.0), 0.0)
        )
        block = ext_ref[b] + shift
        placed[b] = jnp.where(row == 0, block + 64.0 * ext_ref[b, 3:4, :], block)

    def gather(t, carry):
        rows = pl.ds(pl.multiple_of((t // tiles) * 8, 8), 8)
        lanes = pl.ds(pl.multiple_of((t % tiles) * 128, 128), 128)
        index = nbr_ref[rows, lanes]
        low = index & 127
        high = index >> 7
        values = [jnp.zeros((8, 128), F32) for _ in range(3)]
        for r in range(ROW_LOW, ROW_HIGH + 1):
            here = high == r
            piece = slice((r % tiles) * 128, (r % tiles) * 128 + 128)
            for c in range(3):
                line = jnp.broadcast_to(placed[r // tiles, c : c + 1, piece], (8, 128))
                picked = jnp.take_along_axis(line, low, axis=1)
                values[c] = jnp.where(here, picked, values[c])
        into = pl.ds(pl.multiple_of((t % tiles) * slots + (t // tiles) * 8, 8), 8)
        kind = jnp.floor((values[0] + 32.0) * (1.0 / 64.0))
        found[0, into, :] = values[0] - 64.0 * kind
        found[1, into, :] = values[1]
        found[2, into, :] = values[2]
        found[3, into, :] = kind
        return carry

    lax.fori_loop(0, (slots // 8) * tiles, gather, 0, unroll=4)

    own = ext_ref[4]
    slot = lax.broadcasted_iota(jnp.int32, (slots, 128), 0)
    parts = []
    for c in range(4):
        pieces = []
        for j in range(tiles):
            lanes = slice(j * 128, j * 128 + 128)
            value = found[c, slots * j : slots * j + slots, :]
            if c < 3:
                value = (value - own[c : c + 1, lanes]) * spacing
            else:
                value = jnp.where(slot < count_ref[0:1, lanes], value, 8.0)
            pieces.append(value)
        parts.append(jnp.concatenate(pieces, axis=0).T)
    dx, dy, dz, species = parts
    distance = jnp.sqrt(dx * dx + dy * dy + dz * dz)
    inverse = 1.0 / distance
    ux, uy, uz = dx * inverse, dy * inverse, dz * inverse
    scaled = distance * (1.0 / cutoff)
    scaled_sq = scaled * scaled
    six = scaled_sq * scaled_sq * scaled_sq
    envelope = 1.0 - 28.0 * six + 48.0 * six * scaled - 21.0 * six * scaled_sq
    envelope = jnp.where(scaled < 1.0, envelope * neighbour_scale, 0.0)
    r3, r5, r15 = math.sqrt(3.0), math.sqrt(5.0), math.sqrt(15.0)
    factors = (
        None,
        r3 * ux,
        r3 * uy,
        r3 * uz,
        r15 * ux * uy,
        r15 * uy * uz,
        0.5 * r5 * (3.0 * uz * uz - 1.0),
        r15 * ux * uz,
        0.5 * r15 * (ux * ux - uy * uy),
    )
    octets = 8

    def put(target, first, value):
        for o in range(octets):
            target[o, first : first + 8, 0:128] = value[8 * o : 8 * o + 8]
            target[o, first : first + 8, 128:256] = value[64 + 8 * o : 64 + 8 * o + 8]

    for m, factor in enumerate(factors):
        put(weight, 8 * m, envelope if factor is None else envelope * factor)
    put(kinds, 0, species)
    theta = (math.pi / cutoff) * distance
    sine = jnp.sin(theta)
    cosine = 2.0 * jnp.cos(theta)
    scale = math.sqrt(2.0 / cutoff) * inverse
    before = jnp.zeros_like(sine)
    for n in range(8):
        put(basis, 8 * n, scale * sine)
        sine, before = cosine * sine - before, sine

    lane = lax.broadcasted_iota(jnp.int32, (8, 256), 1)
    element = lax.broadcasted_iota(jnp.int32, (8, 256), 0)
    mine = ((lane % 128) // slots) * 2 + lane // 128 == element

    def octet(o, carry):
        hidden = dot(win_wide[...], basis[o].astype(BF16))
        hidden = half_tanh_silu(hidden).astype(BF16)
        for first in range(0, 8, 2):
            sums = []
            for i in (first, first + 1):
                near = hidden[i * hidden_size : (i + 1) * hidden_size]
                kind = kinds[o, i : i + 1, :]
                by_kind = []
                for s in range(8):
                    mark = jnp.broadcast_to((kind == float(s)).astype(F32), (16, 256)).astype(BF16)
                    by_kind.append(near * jnp.concatenate([mark] * (hidden_size // 16), axis=0))
                left = [
                    jnp.where(mine, jnp.broadcast_to(weight[o, 8 * m + i : 8 * m + i + 1, :], (8, 256)), 0.0)
                    for m in range(9)
                ]
                left = jnp.concatenate(left, axis=0).astype(BF16)
                sums.append(dot_nt(left, jnp.concatenate(by_kind, axis=0)))
            into = pl.ds(pl.multiple_of(64 * o + 8 * first, 16), 16)
            for m in range(9):
                both = jnp.concatenate([part[8 * m : 8 * m + 8] for part in sums], axis=0)
                moments[m, into, :] = both.astype(BF16)
        return carry

    lax.fori_loop(0, octets, octet, 0, unroll=4)

    invariants = []
    for degree, (first, last) in enumerate(((0, 1), (1, 4), (4, 9))):
        rows = moments[first:last].reshape((last - first) * atoms, moments.shape[2])
        aggregate = dot(rows, pair[degree]).astype(BF16)
        mixed = dot(aggregate, mix_ref[degree])
        if degree > 0:
            mixed = mixed * mixed
            mixed = sum(mixed[n * atoms : (n + 1) * atoms] for n in range(last - first))
        invariants.append(mixed)
    stacked = jnp.concatenate(invariants, axis=1).astype(BF16)
    update = dot(stacked, prod_ref[...])
    update = update / (1.0 + jnp.exp(-update))
    new_state = (own_state[...] + update).astype(BF16)
    readout = jnp.concatenate(
        [read_ref[...], charge_ref[...], jnp.zeros((14, channels), BF16)], axis=0
    )
    shuffled = dot_nt(readout, new_state)[0:2]
    stack = jnp.concatenate(three_parts(shuffled) + (jnp.zeros((10, atoms), F32),), axis=0)
    ordered = dot(stack.astype(BF16), shuffle[...])
    return ordered[0:2] + ordered[2:4] + ordered[4:6]


def spline_rows(fraction):
    rest = 1.0 - fraction
    square = fraction * fraction
    cube = square * fraction
    return (
        rest * rest * rest * (1.0 / 6.0),
        (3.0 * cube - 6.0 * square + 4.0) * (1.0 / 6.0),
        (-3.0 * cube + 3.0 * square + 3.0 * fraction + 1.0) * (1.0 / 6.0),
        cube * (1.0 / 6.0),
    )


def stencil_rows(rows, first, weights):
    at = lax.broadcasted_iota(jnp.int32, (rows, first.shape[1]), 0) - first
    out = jnp.where(at == 0, weights[0], 0.0)
    for j in range(1, 4):
        out = jnp.where(at == j, weights[j], out)
    return out


def at_marks(position, parts):
    out = jnp.where(position == 125, parts[0], 0.0)
    out = jnp.where(position == 126, parts[1], out)
    return jnp.where(position == 127, parts[2], out)


def several(first, last, unroll, step):
    def turn(n, carry):
        for k in range(unroll):
            step(first + n * unroll + k)
        return carry

    turns = (last - first) // unroll
    lax.fori_loop(0, turns, turn, 0)
    for k in range(first + turns * unroll, last):
        step(k)


WEIGHTS = ("embed", "win", "wout", "mix", "prod", "read", "charge")


def program_kernel(counts, planes, names, *refs):
    ref = dict(zip(names, refs))
    domain_count, inner_count = counts
    devices = domain_count * inner_count
    per_core = devices // 2
    d, i = lax.axis_index("domain"), lax.axis_index("inner")
    me = d * inner_count + i
    at = (d, i)
    slots, atoms = ref["nbr_in"].shape

    def device(t):
        return (t // inner_count, lax.rem(t, inner_count))

    def owner(r):
        rest = lax.rem(r, per_core)
        return (rest // 2, lax.rem(rest, 2) * 2 + r // per_core)

    my_plane = d * 2 + i // 2 + per_core * lax.rem(i, 2)
    owns = my_plane < PLANES

    def rows16(t):
        return pl.ds(pl.multiple_of(t * 16, 16), 16)

    def lanes128(t):
        return pl.ds(pl.multiple_of(t * 128, 128), 128)

    barrier = pltpu.get_barrier_semaphore()

    def greet(k):
        pl.semaphore_signal(
            barrier, inc=1, device_id=device(lax.rem(me + k, devices)), device_id_type=MESH
        )

    several(1, devices, 7, greet)

    def fetch(n, name):
        source = ref[name + "_in"]
        if name == "gain":
            source = source.at[jnp.minimum(my_plane, PLANES - 1) // 2]
        return pltpu.make_async_copy(source, ref[name], ref["fetch_sem"].at[n])

    fetched = ("cells", "frac", "species", "nbr", "count") + WEIGHTS
    fetched = fetched + ("zeta", "y", "x", "xt", "gain")
    fetches = {name: fetch(n, name) for n, name in enumerate(fetched)}
    for name in fetched:
        fetches[name].start()

    moves = [(dx, dy) for dx in (-1, 0, 1) for dy in (-1, 0, 1) if (dx, dy) != (0, 0)]
    mine, ext = ref["mine"], ref["ext"]
    for name in ("cells", "frac", "species"):
        fetches[name].wait()
    cell = [ref["cells"][c] for c in range(3)]
    fraction = [ref["frac"][c] for c in range(3)]
    mine[...] = jnp.zeros_like(mine)
    for c in range(3):
        mine[c : c + 1, :] = cell[c].astype(F32) + fraction[c]
    mine[3:4, :] = ref["species"][0].astype(F32)
    ext[4] = mine[...]

    weights = [spline_rows(f) for f in fraction]
    sten_x = stencil_rows(16, cell[0] - 1, weights[0])
    rim_x = jnp.where(cell[0] == 0, weights[0][0], 0.0)
    sten_z = stencil_rows(40, cell[2] - 1 - Z_LOW, weights[2])
    lane = lax.broadcasted_iota(jnp.int32, (128, atoms), 0)
    y_main = split(stencil_rows(128, cell[1], weights[1]))
    y_low = split(jnp.where(lane <= 97, stencil_rows(128, cell[1] + 65, weights[1]), 0.0))
    y_high = split(jnp.where(lane >= 65, stencil_rows(128, cell[1] + 32, weights[1]), 0.0))
    for n, part in enumerate(y_main + y_low + y_high):
        ref["sten_y"][n] = part
    fetches["zeta"].wait()
    waves = ref["waves"]
    waves[...] = jnp.dot(ref["zeta"][...], sten_z, precision=lax.Precision.HIGHEST)
    sten = ref["sten_x"]
    sten[...] = sten_x
    product, patch32 = ref["product"], ref["patch32"]

    def y_parts(n):
        return ref["sten_y"][2 * n], ref["sten_y"][2 * n + 1]

    def spread(charged):
        for r in range(PLANES):
            product[16 * r : 16 * r + 16, :] = sten[...] * charged[r : r + 1]
        patch32[...] = dot_left(product[...], y_parts(0), dot_nt)
        rim = charged * rim_x
        low = dot_left(rim, y_parts(1), dot_nt)
        high = dot_left(rim, y_parts(2), dot_nt)
        patch32[pl.ds(0, PLANES, 16), :] = patch32[pl.ds(0, PLANES, 16), :] + low[:PLANES]
        patch32[pl.ds(1, PLANES, 16), :] = patch32[pl.ds(1, PLANES, 16), :] + high[:PLANES]

    def to_owners(patch, received, send_sem, recv_sem):
        def start(k):
            r = lax.rem(my_plane + k, PLANES)
            pltpu.make_async_remote_copy(
                src_ref=patch.at[rows16(r), :],
                dst_ref=received.at[rows16(d), lanes128(i)],
                send_sem=send_sem,
                recv_sem=recv_sem,
                device_id=owner(r),
                device_id_type=MESH,
            ).start()

        several(1, PLANES, 5, start)

        @pl.when(jnp.logical_not(owns))
        def _():
            start(PLANES)

        @pl.when(owns)
        def _():
            pltpu.make_async_copy(
                patch.at[rows16(my_plane), :], received.at[rows16(d), lanes128(i)], recv_sem
            ).start()

    def wait_bytes(buffer, sem):
        pltpu.make_async_copy(buffer, buffer, sem).wait()

    spread(waves[...])
    ref["ones_patch"][...] = patch32[...].astype(BF16)
    for name, source in (("x", "x"), ("xt", "xt"), ("y", "y")):
        fetches[source].wait()
        for n, part in enumerate(split(ref[source][...])):
            ref[name + "_parts"][n] = part

    for name in ("nbr", "count") + WEIGHTS:
        fetches[name].wait()
    message_weights(
        ref["species"][0],
        *[ref[name] for name in ("embed", "win", "wout", "win_wide", "pair", "shuffle", "own_state")],
    )

    pl.semaphore_wait(barrier, devices - 1)
    copies = []
    for n, (dx, dy) in enumerate(moves):
        copy = pltpu.make_async_remote_copy(
            src_ref=mine,
            dst_ref=ext.at[(1 - dx) * 3 + (1 - dy)],
            send_sem=ref["ext_send"].at[n],
            recv_sem=ref["ext_recv"].at[n],
            device_id=tuple(
                lax.rem(at[a] + counts[a] + (dx, dy)[a], counts[a]) for a in range(2)
            ),
            device_id_type=MESH,
        )
        copy.start()
        copies.append(copy)
    to_owners(ref["ones_patch"], ref["ones"], ref["ones_send"], ref["ones_recv"])

    for copy in copies:
        copy.wait()
    rows = message_rows(
        planes,
        ext,
        *[
            ref[name]
            for name in (
                "nbr",
                "count",
                "mix",
                "prod",
                "read",
                "charge",
                "win_wide",
                "pair",
                "shuffle",
                "own_state",
                "placed",
                "found",
                "weight",
                "basis",
                "kinds",
                "moments",
            )
        ],
    )
    energy, latent = rows[0:1], rows[1:2]

    block_mean = jnp.sum(latent, axis=1, keepdims=True) / atoms
    spread(waves[...] * (latent - block_mean))
    position = lax.broadcasted_iota(jnp.int32, (1, 128), 1)
    marks = at_marks(position, three_parts(block_mean))
    patch32[pl.ds(2, PLANES, 16), :] = patch32[pl.ds(2, PLANES, 16), :] + marks
    ref["patch"][...] = patch32[...].astype(BF16)
    to_owners(ref["patch"], ref["received"], ref["patch_send"], ref["patch_recv"])

    fetches["gain"].wait()
    answer, back = ref["answer"], ref["back"]

    @pl.when(owns)
    def _():
        grid, coefficient = ref["grid"], ref["coefficient"]
        x_table = ref["x_parts"][0], ref["x_parts"][1]
        xt_table = ref["xt_parts"][0], ref["xt_parts"][1]

        def y_table(part):
            return ref["y_parts"][0, part], ref["y_parts"][1, part]

        def whole_rows(rows):
            return jnp.concatenate([grid[t, rows, :] for t in range(inner_count)], axis=1)

        def every16(first):
            return pl.ds(first, domain_count, 16)

        wait_bytes(ref["ones"], ref["ones_recv"])
        wait_bytes(ref["received"], ref["patch_recv"])
        tiles = [slice(t * 128, t * 128 + 128) for t in range(inner_count)]
        means = []
        for t in range(inner_count):
            grid[t] = ref["received"][:, tiles[t]].astype(F32)
            marked = grid[t, pl.ds(2, domain_count, 16), :]
            means.append(
                jnp.sum(jnp.where(position >= 125, marked, 0.0), axis=1, keepdims=True)
            )
        mean = jnp.sum(sum(means), axis=0, keepdims=True) / devices
        for t in range(inner_count):
            coefficient[t] = jnp.broadcast_to(means[t] - mean, (domain_count, 128))
            for b in range(domain_count):
                here = slice(16 * b, 16 * b + 16)
                unit = ref["ones"][here, tiles[t]].astype(F32)
                grid[t, here, :] = grid[t, here, :] + unit * coefficient[t, b : b + 1, :]
        along_y = dot_left(whole_rows(slice(None)), y_table(0), dot)
        rim = dot_left(whole_rows(every16(0)), y_table(1), dot)
        rim = rim + dot_left(whole_rows(every16(1)), y_table(2), dot)
        rim = pltpu.roll(rim, domain_count - 1, 0)
        lines_ref = ref["lines"]
        full_y = along_y.shape[1]
        columns = [slice(t * 128, t * 128 + 128) for t in range(full_y // 128)]
        for t, column in enumerate(columns):
            lines_ref[t] = along_y[:, column]
            lines_ref[t, every16(15), :] = lines_ref[t, every16(15), :] + rim[:, column]
        lines = jnp.concatenate([lines_ref[t] for t in range(len(columns))], axis=1)
        spectrum = dot_split(x_table, split(lines), dot)
        half = lines.shape[0] // 2
        top = ref["gain"][0:half, :]
        first_row = lax.broadcasted_iota(jnp.int32, (half, full_y), 0) == 0
        bottom = jnp.where(first_row, ref["gain"][half : half + 1, :], top)
        filtered = jnp.concatenate([spectrum[0:half] * top, spectrum[half:] * bottom], axis=0)
        lines = dot_split(xt_table, split(filtered), dot)
        for t, column in enumerate(columns):
            lines_ref[t] = lines[:, column]
        rim = jnp.concatenate(
            [lines_ref[t, every16(15), :] for t in range(len(columns))], axis=1
        )
        rim = pltpu.roll(rim, 1, 0)
        values = dot_left(lines, y_table(0), dot_nt)
        low_rim = dot_left(rim, y_table(1), dot_nt)
        high_rim = dot_left(rim, y_table(2), dot_nt)
        marks = at_marks(position, three_parts(mean))
        for t in range(inner_count):
            grid[t] = values[:, tiles[t]]
            grid[t, every16(0), :] = grid[t, every16(0), :] + low_rim[:, tiles[t]]
            grid[t, every16(1), :] = grid[t, every16(1), :] + high_rim[:, tiles[t]]
            grid[t, every16(2), :] = grid[t, every16(2), :] + marks
            answer[:, tiles[t]] = grid[t].astype(BF16)

        def back_start(k):
            t = lax.rem(me + k, devices)
            pltpu.make_async_remote_copy(
                src_ref=answer.at[rows16(t // inner_count), lanes128(lax.rem(t, inner_count))],
                dst_ref=back.at[rows16(my_plane), :],
                send_sem=ref["back_send"],
                recv_sem=ref["back_recv"],
                device_id=device(t),
                device_id_type=MESH,
            ).start()

        several(1, devices, 7, back_start)
        pltpu.make_async_copy(
            answer.at[rows16(d), lanes128(i)], back.at[rows16(my_plane), :], ref["back_recv"]
        ).start()

    wait_bytes(back, ref["back_recv"])
    given = back[...]
    main, low, high = y_parts(0), y_parts(1), y_parts(2)
    product[...] = dot(given, main[0]) + dot(given, main[1])
    back32 = patch32
    back32[...] = given.astype(F32)
    mean = jnp.sum(jnp.where(position >= 125, back32[2:3, :], 0.0), axis=1, keepdims=True)
    at_low = back32[pl.ds(0, PLANES, 16), :].astype(BF16)
    at_high = back32[pl.ds(1, PLANES, 16), :].astype(BF16)
    at_rim = dot(at_low, low[0]) + dot(at_low, low[1])
    at_rim = at_rim + dot(at_high, high[0]) + dot(at_high, high[1])
    gathered = jnp.zeros((8, atoms), F32)
    for r in range(PLANES):
        piece = (
            product[16 * r : 16 * r + 8, :] * sten[0:8]
            + product[16 * r + 8 : 16 * r + 16, :] * sten[8:16]
        )
        gathered = gathered + piece * waves[r : r + 1]
    value = jnp.sum(gathered, axis=0, keepdims=True) + rim_x * jnp.sum(
        at_rim * waves[:PLANES], axis=0, keepdims=True
    )
    ref["out"][0:1] = energy + 0.5 * (latent - mean) * value
    ref["out"][1:2] = value

    sent = ref["sent"]
    for sem in (ref["ones_send"], ref["patch_send"]):

        @pl.when(owns)
        def _():
            wait_bytes(sent.at[0 : (PLANES - 1) * 16], sem)

        @pl.when(jnp.logical_not(owns))
        def _():
            wait_bytes(sent.at[0 : PLANES * 16], sem)

    @pl.when(owns)
    def _():
        wait_bytes(sent.at[0 : (devices - 1) * 16], ref["back_send"])


def part_kernel(both_ref, energy_ref, potential_ref):
    energy_ref[0] = both_ref[0:1, :]
    potential_ref[0] = both_ref[1:2, :]


def local(
    counts,
    atom_cells,
    atom_frac,
    species,
    nbr_index,
    nbr_count,
    embed,
    radial_in,
    radial_out,
    mix_weight,
    product_weight,
    read_weight,
    charge_weight,
):
    planes = (16, 64)
    devices = counts[0] * counts[1]
    tables = host_tables(*counts, *planes, 256)
    operands = dict(
        cells=atom_cells.transpose(2, 0, 1, 3)[:, 0],
        frac=atom_frac.transpose(2, 0, 1, 3)[:, 0],
        species=species,
        nbr=nbr_index[0, 0].T,
        count=nbr_count[0],
        embed=embed,
        win=radial_in[0],
        wout=radial_out[0],
        mix=mix_weight[0],
        prod=product_weight[0],
        read=read_weight,
        charge=charge_weight[None],
        **{name: jnp.asarray(tables[name]) for name in ("zeta", "y", "x", "xt", "gain")},
    )
    slots, atoms = operands["nbr"].shape
    channels = embed.shape[1]
    hidden = radial_in.shape[-1]
    full_x, full_y, lanes = counts[0] * planes[0], counts[1] * planes[1], counts[1] * 128
    dma = pltpu.SemaphoreType.DMA
    scratch = {
        name: VMEM(value.shape[1:] if name == "gain" else value.shape, value.dtype)
        for name, value in operands.items()
    }
    scratch.update(
        mine=VMEM((8, atoms), F32),
        ext=VMEM((9, 8, atoms), F32),
        placed=VMEM((9, 8, atoms), F32),
        found=VMEM((4, atoms // 128 * slots, 128), F32),
        weight=VMEM((8, 72, 256), F32),
        basis=VMEM((8, 64, 256), F32),
        kinds=VMEM((8, 8, 256), F32),
        moments=VMEM((9, atoms, 8 * hidden), BF16),
        win_wide=VMEM((8 * hidden, 64), BF16),
        pair=VMEM((3, 8 * hidden, channels), BF16),
        shuffle=VMEM((atoms, atoms), BF16),
        own_state=VMEM((atoms, channels), F32),
        sten_x=VMEM((16, atoms), F32),
        sten_y=VMEM((6, 128, atoms), BF16),
        waves=VMEM((72, atoms), F32),
        product=VMEM((PLANES * 16, atoms), F32),
        patch32=VMEM((PLANES * 16, 128), F32),
        ones_patch=VMEM((PLANES * 16, 128), BF16),
        patch=VMEM((PLANES * 16, 128), BF16),
        ones=VMEM((full_x, lanes), BF16),
        received=VMEM((full_x, lanes), BF16),
        grid=VMEM((counts[1], full_x, 128), F32),
        coefficient=VMEM((counts[1], counts[0], 128), F32),
        lines=VMEM((full_y // 128, full_x, 128), F32),
        x_parts=VMEM((2, full_x, full_x), BF16),
        xt_parts=VMEM((2, full_x, full_x), BF16),
        y_parts=VMEM((2, 3, lanes, full_y), BF16),
        answer=VMEM((full_x, lanes), BF16),
        back=VMEM((PLANES * 16, 128), BF16),
        sent=VMEM(((devices - 1) * 16, 128), BF16),
        fetch_sem=dma((len(operands),)),
        ext_send=dma((8,)),
        ext_recv=dma((8,)),
        ones_send=dma,
        ones_recv=dma,
        patch_send=dma,
        patch_recv=dma,
        back_send=dma,
        back_recv=dma,
    )
    names = [name + "_in" for name in operands] + ["out"] + list(scratch)
    vmem = pl.BlockSpec(memory_space=VMEM)
    both = pl.pallas_call(
        functools.partial(program_kernel, counts, planes, names),
        out_shape=jax.ShapeDtypeStruct((2, atoms), F32),
        in_specs=[pl.BlockSpec(memory_space=pl.ANY)] * len(operands),
        out_specs=vmem,
        scratch_shapes=list(scratch.values()),
        compiler_params=pltpu.CompilerParams(
            collective_id=0, has_side_effects=True, vmem_limit_bytes=58 << 20
        ),
        name="potential",
    )(*operands.values())
    return tuple(
        pl.pallas_call(
            part_kernel,
            out_shape=[jax.ShapeDtypeStruct((1, 1, atoms), F32)] * 2,
            in_specs=[vmem],
            out_specs=[vmem] * 2,
            name="outputs",
        )(both)
    )


def solution(mesh):
    counts = (mesh.shape["domain"], mesh.shape["inner"])
    in_specs = (
        P("domain", "inner", None, None),
        P("domain", "inner", None, None),
        P("domain", "inner", None),
        P("domain", "inner", None, None),
        P("domain", "inner", None),
        P(),
        P(),
        P(),
        P(),
        P(),
        P(),
        P(),
    )
    out_specs = (P("domain", "inner", None), P("domain", "inner", None))
    return jax.shard_map(
        functools.partial(local, counts),
        mesh=mesh,
        in_specs=in_specs,
        out_specs=out_specs,
        check_vma=False,
    )
```
